256 devices in a mesh: dp: 16 (over y_lo, z), proto: 16 (over x, y_hi, core).
Axes of the slice: x: 4, y: 4 (y_hi: 2, y_lo: 2; y = y_hi * 2 + y_lo), z: 8, core: 2. Of those that a mesh axis runs over, the one named last changes fastest.
Arguments:
- student_feats: bfloat16 [16384, 256], P('dp'), may hold values from -0.5 to 0.5
- teacher_feats: bfloat16 [16384, 256], P('dp'), may hold values from -6 to 6
- student_protos: bfloat16 [256, 65536], P(None, 'proto'), may hold values from -0.375 to 0.375
- teacher_protos: bfloat16 [256, 65536], P(None, 'proto'), may hold values from -0.1875 to 0.1875
Outputs:
- proto_grad: float32 [256, 65536], P(None, 'proto')
- feature_grad: float32 [16384, 256], P('dp')
The draws below stay inside these ranges and needn't reach their ends.
All inputs are finite; a program needn't handle non-finite values.
Results may differ from the reference program's by a relative error of at most 0.0009.
The reference program's roundings to bfloat16 on the way (of `grads`) count: a program that leaves them out, or rounds other values in their place, can miss the bound.
Values sent between devices are 32-bit elements; how exact they have to be, the bound alone decides.
A program may use at most 128 MiB of HBM per device.

```python
import math
import jax
import jax.numpy as jnp
from jax import lax

D_BOT = 256
PROTOS = 65536
ROUNDS = 3
BATCH = 16384


def shared_centers(key):
    return jax.random.truncated_normal(key, -3.0, 3.0, (4, D_BOT), jnp.float32)


def cluster_of(key, count, flip):
    draws = jax.random.randint(key, (count,), 0, 10)
    member = (draws >= 4).astype(jnp.int32) + (draws >= 7).astype(jnp.int32) + (draws >= 9).astype(jnp.int32)
    return jnp.abs(flip - member)


def draw_teacher_feats(key, part):
    centers = shared_centers(key)
    key = jax.random.fold_in(key, 11)
    member_key, noise_key = jax.random.split(key)
    member = cluster_of(member_key, BATCH, 0)
    noise = jax.random.normal(noise_key, (BATCH, D_BOT), jnp.float32)
    strength = 3.0
    values = strength * centers[member] + noise
    return jnp.clip(values, -6.0, 6.0).astype(jnp.bfloat16)


def draw_teacher_protos(key, part):
    centers = shared_centers(key)
    key = jax.random.fold_in(key, 13)
    member_key, noise_key = jax.random.split(key)
    member = cluster_of(member_key, PROTOS, 3)
    noise = jax.random.normal(noise_key, (D_BOT, PROTOS), jnp.float32)
    strength = 0.35
    values = (strength * centers[member].T + noise) * 0.0625
    return jnp.clip(values, -0.1875, 0.1875).astype(jnp.bfloat16)


def block_levels(rng, shape, shards, least, top_value):
    def one(dim, blocks):
        steps = jax.random.uniform(jax.random.fold_in(jax.random.fold_in(rng, 6), dim), (blocks,), jnp.float32, least / len(shards), top_value / len(shards))
        return jnp.repeat(jnp.exp(steps), shape[dim] // blocks).reshape((-1,) + (1,) * (len(shape) - dim - 1))

    level = one(*shards[0])
    for cut in shards[1:]:
        level = level * one(*cut)
    return level


def scatter_about(rng, dims, scale, limit, shards=(), dtype=jnp.bfloat16):
    loudness = block_levels(rng, dims, shards, -0.22, 0.18) if shards else 1.0
    entries = jax.random.normal(rng, dims, jnp.float32) * scale * loudness
    return jnp.minimum(jnp.maximum(entries, -limit), limit).astype(dtype)


def setup_inputs(seed: int = 0) -> dict:
    key_list = jax.random.split(jax.random.key(seed), 5)
    student_feats = scatter_about(key_list[0], (BATCH, D_BOT), 0.0625, 0.5, ((0, 16),))
    teacher_feats = draw_teacher_feats(jax.random.fold_in(key_list[4], 71), 0)
    student_protos = scatter_about(key_list[2], (D_BOT, PROTOS), D_BOT ** -0.5, 0.375, ((1, 16),))
    teacher_protos = draw_teacher_protos(jax.random.fold_in(key_list[4], 71), 0)
    return dict(student_feats=student_feats, teacher_feats=teacher_feats, student_protos=student_protos, teacher_protos=teacher_protos)


EPS = 1e-06
TEACHER_TEMP = 0.07
STUDENT_TEMP = 0.1

def unit_rows(values):
    wide = values.astype(jnp.float32)
    norms = jnp.sqrt(lax.optimization_barrier(jnp.sum(wide * wide, axis=1, keepdims=True)) + EPS)
    return (wide / norms, norms)

def unit_cols(values):
    wide = values.astype(jnp.float32)
    norms = jnp.sqrt(lax.optimization_barrier(jnp.sum(wide * wide, axis=0, keepdims=True)) + EPS)
    return (wide / norms, norms)

def reference(student_feats, teacher_feats, student_protos, teacher_protos):
    s_unit, s_norm = unit_rows(student_feats)
    s_hat = s_unit.astype(jnp.bfloat16)
    t_hat = unit_rows(teacher_feats)[0].astype(jnp.bfloat16)
    w_unit, w_norm = unit_cols(student_protos)
    ws = w_unit.astype(jnp.bfloat16)
    wt = unit_cols(teacher_protos)[0].astype(jnp.bfloat16)
    block = min(512, BATCH)
    nblocks = BATCH // block
    t_blocks = t_hat.reshape(nblocks, block, D_BOT)

    def teacher_exp(tb):
        return jnp.exp(jnp.dot(tb, wt, preferred_element_type=jnp.float32) / TEACHER_TEMP)

    def first_cols(acc, tb):
        return (acc + lax.optimization_barrier(jnp.sum(teacher_exp(tb), axis=0)), None)
    cols, _ = lax.scan(first_cols, jnp.zeros((PROTOS,), jnp.float32), t_blocks)
    col_scale = 1.0 / cols

    def next_cols(scale_now, acc, tb):
        weights = teacher_exp(tb) * scale_now
        weights = weights / lax.optimization_barrier(jnp.sum(weights, axis=1, keepdims=True))
        return (acc + lax.optimization_barrier(jnp.sum(weights, axis=0)), None)
    for turn in range(ROUNDS - 1):
        nxt, _ = lax.scan(lambda acc, tb: next_cols(col_scale, acc, tb), jnp.zeros((PROTOS,), jnp.float32), t_blocks)
        col_scale = col_scale / nxt
    factor = PROTOS / math.sqrt(BATCH) / STUDENT_TEMP
    s_blocks = s_hat.reshape(nblocks, block, D_BOT)
    u_blocks = s_unit.reshape(nblocks, block, D_BOT)
    n_blocks = s_norm.reshape(nblocks, block, 1)

    def final(acc, pieces):
        tb, sb, ub, nb = pieces
        target = teacher_exp(tb) * col_scale
        target = target / lax.optimization_barrier(jnp.sum(target, axis=1, keepdims=True))
        expo = jnp.exp(jnp.dot(sb, ws, preferred_element_type=jnp.float32) / STUDENT_TEMP)
        probs = expo / lax.optimization_barrier(jnp.sum(expo, axis=1, keepdims=True))
        grads = ((probs - target) * factor).astype(jnp.bfloat16)
        acc = acc + lax.dot_general(sb, grads, (((0,), (0,)), ((), ())), preferred_element_type=jnp.float32)
        hat_grad = lax.dot_general(grads, ws, (((1,), (1,)), ((), ())), preferred_element_type=jnp.float32)
        feat = (hat_grad - ub * lax.optimization_barrier(jnp.sum(ub * hat_grad, axis=1, keepdims=True))) / nb
        return (acc, feat)
    unit_grad, feats = lax.scan(final, jnp.zeros((D_BOT, PROTOS), jnp.float32), (t_blocks, s_blocks, u_blocks, n_blocks))
    proto_grad = (unit_grad - w_unit * lax.optimization_barrier(jnp.sum(w_unit * unit_grad, axis=0, keepdims=True))) / w_norm
    return (proto_grad, feats.reshape(BATCH, D_BOT))
```

```python
import functools
import math

import jax
import jax.numpy as jnp
from jax import lax
from jax.experimental import pallas as pl
from jax.experimental.pallas import tpu as pltpu
from jax.sharding import PartitionSpec as P

PROTOS = 65536
ROUNDS = 3
EPS = 1e-06
TEACHER_TEMP = 0.07
STUDENT_TEMP = 0.1
LOG2E = 1.4426950408889634
MESH = pl.DeviceIdType.MESH
F32 = jnp.float32
BF16 = jnp.bfloat16


def unit_rows(values):
    wide = values.astype(F32)
    norms = jnp.sqrt(jnp.sum(wide * wide, axis=1, keepdims=True) + EPS)
    return (wide / norms, norms)


def unit_cols(values):
    wide = values.astype(F32)
    norms = jnp.sqrt(jnp.sum(wide * wide, axis=0, keepdims=True) + EPS)
    return (wide / norms, norms)


def wait_bytes(ref, sem):
    pltpu.make_async_copy(ref, ref, sem).wait()


def kernel(
    n_dp, n_pr,
    sf_ref, tf_ref, sp_ref, tp_ref,
    u_out, v_out, t_out,
    expo, th, sh, part, vb, ub,
    csend, crecv, vbuf, rsend, rrecv,
    csend_sem, crecv_sem, vsend_sem, vrecv_sem, rsend_sem, rrecv_sem,
):
    rows, dim = sf_ref.shape
    cols = tp_ref.shape[1]
    me = lax.axis_index("dp")
    mp = lax.axis_index("proto")
    width = cols // n_dp
    blocks = rows // 128

    barrier = pltpu.get_barrier_semaphore()

    def greet_dp(j, _):
        pl.semaphore_signal(barrier, inc=1, device_id={"dp": lax.rem(me + j, n_dp)}, device_id_type=MESH)
        return 0

    def greet_pr(j, _):
        pl.semaphore_signal(barrier, inc=1, device_id={"proto": lax.rem(mp + j, n_pr)}, device_id_type=MESH)
        return 0

    lax.fori_loop(1, n_dp, greet_dp, 0)
    lax.fori_loop(1, n_pr, greet_pr, 0)

    def norm_rows(b, _):
        r = pl.ds(pl.multiple_of(b * 128, 128), 128)
        th[r, :] = unit_rows(tf_ref[r, :])[0].astype(BF16)
        sh[r, :] = unit_rows(sf_ref[r, :])[0].astype(BF16)
        return 0

    lax.fori_loop(0, blocks, norm_rows, 0)
    pl.semaphore_wait(barrier, n_dp + n_pr - 2)

    def send_cols(rnd, owner, slot):
        pltpu.make_async_remote_copy(
            src_ref=csend.at[rnd, owner], dst_ref=crecv.at[rnd, slot],
            send_sem=csend_sem.at[rnd], recv_sem=crecv_sem.at[rnd],
            device_id={"dp": owner}, device_id_type=MESH,
        ).start()

    def first_cols(i, _):
        owner = lax.rem(me + 1 + i, n_dp)
        c = pl.ds(pl.multiple_of(owner * width, width), width)
        wt = unit_cols(tp_ref[:, c])[0].astype(BF16)
        acc = jnp.zeros((8, width), F32)
        for m in range(rows // 256):
            r = pl.ds(m * 256, 256)
            logits = jnp.dot(th[r, :], wt, preferred_element_type=F32)
            e = jnp.exp2(logits * (LOG2E / TEACHER_TEMP))
            expo[r, c] = e
            acc = acc + jnp.sum(e.reshape(32, 8, width), axis=0)
        csend[0, owner] = jnp.sum(acc, axis=0, keepdims=True)

        @pl.when(i < n_dp - 1)
        def _():
            send_cols(0, owner, i)

        return 0

    lax.fori_loop(0, n_dp, first_cols, 0)

    part[...] = jnp.zeros_like(part)

    def student(lo, hi):
        def body(k, _):
            c = pl.ds(pl.multiple_of(k * width, width), width)
            ws = unit_cols(sp_ref[:, c])[0].astype(BF16)
            for m in range(rows // 256):
                r = pl.ds(m * 256, 256)
                logits = jnp.dot(sh[r, :], ws, preferred_element_type=F32)
                e = jnp.exp2(logits * (LOG2E / STUDENT_TEMP))
                s = e[:, 0:128]
                for t in range(1, width // 128):
                    s = s + e[:, t * 128:(t + 1) * 128]
                part[r, :] += s
            return 0

        lax.fori_loop(lo, hi, body, 0)

    def finish_cols(rnd):
        wait_bytes(crecv.at[rnd], crecv_sem.at[rnd])
        total = csend[rnd, me] + jnp.sum(crecv[rnd], axis=0)
        vbuf[rnd, me] = 1.0 / total

        def share(j, _):
            pltpu.make_async_remote_copy(
                src_ref=vbuf.at[rnd, me], dst_ref=vbuf.at[rnd, me],
                send_sem=vsend_sem.at[rnd], recv_sem=vrecv_sem.at[rnd],
                device_id={"dp": lax.rem(me + j, n_dp)}, device_id_type=MESH,
            ).start()
            return 0

        lax.fori_loop(1, n_dp, share, 0)

    def receive_v(rnd):
        wait_bytes(vbuf.at[rnd, pl.ds(0, n_dp - 1)], vrecv_sem.at[rnd])
        for k in range(n_dp):
            vb[:, k * width:(k + 1) * width] = jnp.broadcast_to(vbuf[rnd, k], (8, width))

    def lane_sums(slot, k, acc):
        rsend[slot, pl.ds(k, 1), :] = jnp.sum(acc.T, axis=0, keepdims=True)

    def send_rows(slot):
        def share(j, _):
            pltpu.make_async_remote_copy(
                src_ref=rsend.at[slot], dst_ref=rrecv.at[slot, j - 1],
                send_sem=rsend_sem.at[slot], recv_sem=rrecv_sem.at[slot],
                device_id={"proto": lax.rem(mp + j, n_pr)}, device_id_type=MESH,
            ).start()
            return 0

        lax.fori_loop(1, n_pr, share, 0)

    def receive_rows(slot):
        wait_bytes(rrecv.at[slot], rrecv_sem.at[slot])
        return 1.0 / (rsend[slot] + jnp.sum(rrecv[slot], axis=0))

    def widen(u, out):
        for k in range(blocks):
            out[k * 128:(k + 1) * 128, :] = jnp.broadcast_to(u[k:k + 1, :], (128, 128)).T

    def row_pass(rnd):
        def body(k, _):
            r = pl.ds(pl.multiple_of(k * 128, 128), 128)
            acc = jnp.zeros((16, 8, 128), F32)
            for t in range(cols // 128):
                e = expo[r, t * 128:(t + 1) * 128].reshape(16, 8, 128)
                acc = acc + e * vb[:, t * 128:(t + 1) * 128][None]
            lane_sums(rnd, k, acc.reshape(128, 128))
            return 0

        lax.fori_loop(0, blocks, body, 0)

    def col_pass(rnd):
        def body(i, _):
            owner = lax.rem(me + 1 + i, n_dp)
            c = pl.ds(pl.multiple_of(owner * width, width), width)

            def inner(b, acc):
                r = pl.ds(pl.multiple_of(b * 128, 128), 128)
                u = ub[r, :].reshape(16, 8, 128)
                e = expo[r, c].reshape(16, 8, width)
                new = [e[:, :, t * 128:(t + 1) * 128] * u for t in range(width // 128)]
                return tuple(a + jnp.sum(x, axis=0) for a, x in zip(acc, new))

            acc = lax.fori_loop(0, blocks, inner, (jnp.zeros((8, 128), F32),) * (width // 128))
            csend[rnd, owner] = jnp.sum(jnp.concatenate(acc, axis=1), axis=0, keepdims=True)

            @pl.when(i < n_dp - 1)
            def _():
                send_cols(rnd, owner, i)

            return 0

        lax.fori_loop(0, n_dp, body, 0)

    half = n_dp // 4
    student(0, half)
    finish_cols(0)
    student(half, 2 * half)
    receive_v(0)
    for rnd in range(ROUNDS):
        row_pass(rnd)
        send_rows(rnd)
        if rnd == 0:
            student(2 * half, 3 * half)
        if rnd == 1:
            student(3 * half, 4 * half)

            def student_rows(k, _):
                lane_sums(ROUNDS, k, part[pl.ds(pl.multiple_of(k * 128, 128), 128), :])
                return 0

            lax.fori_loop(0, blocks, student_rows, 0)
            send_rows(ROUNDS)
        u = receive_rows(rnd)
        if rnd < ROUNDS - 1:
            widen(u, ub)
            col_pass(rnd + 1)
            finish_cols(rnd + 1)
            receive_v(rnd + 1)
        else:
            u_out[...] = u
    t_out[...] = receive_rows(ROUNDS)
    v_out[...] = vb[...]
    for rnd in range(ROUNDS):
        wait_bytes(crecv.at[rnd], csend_sem.at[rnd])
        wait_bytes(crecv.at[rnd], vsend_sem.at[rnd])
    for slot in range(ROUNDS + 1):
        wait_bytes(rrecv.at[slot], rsend_sem.at[slot])


def sinkhorn(n_dp, n_pr, sf, tf, sp, tp):
    rows, dim = sf.shape
    cols = tp.shape[1]
    width = cols // n_dp
    blocks = rows // 128
    vmem = pl.BlockSpec(memory_space=pltpu.VMEM)
    dma = pltpu.SemaphoreType.DMA
    return pl.pallas_call(
        functools.partial(kernel, n_dp, n_pr),
        out_shape=(
            jax.ShapeDtypeStruct((blocks, 128), F32),
            jax.ShapeDtypeStruct((8, cols), F32),
            jax.ShapeDtypeStruct((blocks, 128), F32),
        ),
        in_specs=[vmem] * 4,
        out_specs=[vmem] * 3,
        scratch_shapes=[
            pltpu.VMEM((rows, cols), F32),
            pltpu.VMEM((rows, dim), BF16),
            pltpu.VMEM((rows, dim), BF16),
            pltpu.VMEM((rows, 128), F32),
            pltpu.VMEM((8, cols), F32),
            pltpu.VMEM((rows, 128), F32),
            pltpu.VMEM((ROUNDS, n_dp, 1, width), F32),
            pltpu.VMEM((ROUNDS, n_dp - 1, 1, width), F32),
            pltpu.VMEM((ROUNDS, n_dp, 1, width), F32),
            pltpu.VMEM((ROUNDS + 1, blocks, 128), F32),
            pltpu.VMEM((ROUNDS + 1, n_pr - 1, blocks, 128), F32),
            dma((ROUNDS,)), dma((ROUNDS,)), dma((ROUNDS,)), dma((ROUNDS,)),
            dma((ROUNDS + 1,)), dma((ROUNDS + 1,)),
        ],
        compiler_params=pltpu.CompilerParams(
            collective_id=0, has_side_effects=True, vmem_limit_bytes=56 * 1024 * 1024
        ),
    )(sf, tf, sp, tp)


def project(grad_part, unit_part, norm_part):
    return (
        grad_part - unit_part * jnp.sum(unit_part * grad_part, axis=0, keepdims=True)
    ) / norm_part


def local(n_dp, n_pr, student_feats, teacher_feats, student_protos, teacher_protos):
    u, v, t = sinkhorn(n_dp, n_pr, student_feats, teacher_feats, student_protos, teacher_protos)
    rows = student_feats.shape[0]
    s_unit, s_norm = unit_rows(student_feats)
    s_hat = s_unit.astype(BF16)
    t_hat = unit_rows(teacher_feats)[0].astype(BF16)
    w_unit, w_norm = unit_cols(student_protos)
    ws = w_unit.astype(BF16)
    wt = unit_cols(teacher_protos)[0].astype(BF16)
    weights = jnp.exp(jnp.dot(t_hat, wt, preferred_element_type=F32) / TEACHER_TEMP)
    expo = jnp.exp(jnp.dot(s_hat, ws, preferred_element_type=F32) / STUDENT_TEMP)
    weights = weights * u.reshape(rows, 1) * v[0:1, :]
    batch_all = rows * n_dp
    factor = PROTOS / math.sqrt(batch_all) / STUDENT_TEMP
    probs = expo * t.reshape(rows, 1)
    grads = ((probs - weights) * factor).astype(BF16)
    partial_grad = lax.dot_general(s_hat, grads, (((0,), (0,)), ((), ())), preferred_element_type=F32)
    local_hat = lax.dot_general(grads, ws, (((1,), (1,)), ((), ())), preferred_element_type=F32)
    hat_grad = lax.psum(local_hat, "proto")
    feature_grad = (hat_grad - s_unit * jnp.sum(s_unit * hat_grad, axis=1, keepdims=True)) / s_norm
    summed = lax.psum(partial_grad, "dp")
    proto_grad = project(summed, w_unit, w_norm)
    return (proto_grad, feature_grad)


def solution(mesh):
    in_specs = (P("dp", None), P("dp", None), P(None, "proto"), P(None, "proto"))
    out_specs = (P(None, "proto"), P("dp", None))
    return jax.shard_map(
        functools.partial(local, mesh.shape["dp"], mesh.shape["proto"]),
        mesh=mesh, in_specs=in_specs, out_specs=out_specs, check_vma=False,
    )
```

```python
import functools
import math

import jax
import jax.numpy as jnp
from jax import lax
from jax.experimental import pallas as pl
from jax.experimental.pallas import tpu as pltpu
from jax.sharding import PartitionSpec as P

PROTOS = 65536
ROUNDS = 3
EPS = 1e-06
TEACHER_TEMP = 0.07
STUDENT_TEMP = 0.1
LOG2E = 1.4426950408889634
MESH = pl.DeviceIdType.MESH
F32 = jnp.float32
BF16 = jnp.bfloat16


def unit_rows(values):
    wide = values.astype(F32)
    norms = jnp.sqrt(jnp.sum(wide * wide, axis=1, keepdims=True) + EPS)
    return (wide / norms, norms)


def unit_cols(values):
    wide = values.astype(F32)
    norms = jnp.sqrt(jnp.sum(wide * wide, axis=0, keepdims=True) + EPS)
    return (wide / norms, norms)


def wait_bytes(ref, sem):
    pltpu.make_async_copy(ref, ref, sem).wait()


def kernel(
    n_dp, n_pr,
    sf_ref, tf_ref, sp_ref, tp_ref,
    pg_ref, fg_ref,
    expo, th, sh, part, vb, ub,
    csend, crecv, vbuf, rsend, rrecv,
    st, wsn, pb, gbuf, hat, ubuf, yrecv, zrecv, brecv, gat, h1, h2, h3, fgb,
    csend_sem, crecv_sem, vsend_sem, vrecv_sem, rsend_sem, rrecv_sem,
    ysend_sem, yrecv_sem, zsend_sem, zrecv_sem, bsend_sem, brecv_sem,
    gzsend_sem, gzrecv_sem, gysend_sem, gyrecv_sem, hsend_sem, hrecv_sem, out_sem,
):
    rows, dim = sf_ref.shape
    cols = tp_ref.shape[1]
    me = lax.axis_index("dp")
    mp = lax.axis_index("proto")
    width = cols // n_dp
    blocks = rows // 128
    nz = n_dp // 2
    y, z = me // nz, lax.rem(me, nz)
    other = {"dp": (1 - y) * nz + z}
    sides = ({"dp": y * nz + lax.rem(z + 1, nz)}, {"dp": y * nz + lax.rem(z + nz - 1, nz)})
    part_rows = dim // 4
    core, h, x = lax.rem(mp, 2), lax.rem(mp // 2, 2), mp // 4
    nx = n_pr // 4
    factor = PROTOS / math.sqrt(rows * n_dp) / STUDENT_TEMP

    barrier = pltpu.get_barrier_semaphore()

    def greet_dp(j, _):
        pl.semaphore_signal(barrier, inc=1, device_id={"dp": lax.rem(me + j, n_dp)}, device_id_type=MESH)
        return 0

    def greet_pr(j, _):
        pl.semaphore_signal(barrier, inc=1, device_id={"proto": lax.rem(mp + j, n_pr)}, device_id_type=MESH)
        return 0

    lax.fori_loop(1, n_dp, greet_dp, 0)
    lax.fori_loop(1, n_pr, greet_pr, 0)

    def norm_rows(b, _):
        r = pl.ds(pl.multiple_of(b * 128, 128), 128)
        th[r, :] = unit_rows(tf_ref[r, :])[0].astype(BF16)
        unit = unit_rows(sf_ref[r, :])[0]
        sh[r, :] = unit.astype(BF16)
        turned = unit.T.astype(BF16)
        st[pl.ds(pl.multiple_of((1 - y) * part_rows, part_rows), part_rows), r] = turned[:part_rows]
        st[pl.ds(pl.multiple_of(y * part_rows, part_rows), part_rows), r] = turned[part_rows:2 * part_rows]
        st[2 * part_rows:, r] = turned[2 * part_rows:]
        return 0

    lax.fori_loop(0, blocks, norm_rows, 0)
    pl.semaphore_wait(barrier, n_dp + n_pr - 2)

    def send_cols(rnd, owner, slot):
        pltpu.make_async_remote_copy(
            src_ref=csend.at[rnd, owner], dst_ref=crecv.at[rnd, slot],
            send_sem=csend_sem.at[rnd], recv_sem=crecv_sem.at[rnd],
            device_id={"dp": owner}, device_id_type=MESH,
        ).start()

    def first_cols(i, _):
        owner = lax.rem(me + 1 + i, n_dp)
        c = pl.ds(pl.multiple_of(owner * width, width), width)
        wt = unit_cols(tp_ref[:, c])[0].astype(BF16)
        acc = jnp.zeros((8, width), F32)
        for m in range(rows // 256):
            r = pl.ds(m * 256, 256)
            logits = jnp.dot(th[r, :], wt, preferred_element_type=F32)
            e = jnp.exp2(logits * (LOG2E / TEACHER_TEMP))
            expo[r, c] = e
            acc = acc + jnp.sum(e.reshape(32, 8, width), axis=0)
        csend[0, owner] = jnp.sum(acc, axis=0, keepdims=True)

        @pl.when(i < n_dp - 1)
        def _():
            send_cols(0, owner, i)

        return 0

    lax.fori_loop(0, n_dp, first_cols, 0)

    part[...] = jnp.zeros_like(part)

    def student(lo, hi):
        def body(k, _):
            c = pl.ds(pl.multiple_of(k * width, width), width)
            ws = unit_cols(sp_ref[:, c])[0].astype(BF16)
            wsn[:, c] = ws
            for m in range(rows // 256):
                r = pl.ds(m * 256, 256)
                logits = jnp.dot(sh[r, :], ws, preferred_element_type=F32)
                e = jnp.exp2(logits * (LOG2E / STUDENT_TEMP))
                s = e[:, 0:128]
                for t in range(1, width // 128):
                    s = s + e[:, t * 128:(t + 1) * 128]
                part[r, :] += s
            return 0

        lax.fori_loop(lo, hi, body, 0)

    def finish_cols(rnd):
        wait_bytes(crecv.at[rnd], crecv_sem.at[rnd])
        total = csend[rnd, me] + jnp.sum(crecv[rnd], axis=0)
        vbuf[rnd, me] = 1.0 / total

        def share(j, _):
            pltpu.make_async_remote_copy(
                src_ref=vbuf.at[rnd, me], dst_ref=vbuf.at[rnd, me],
                send_sem=vsend_sem.at[rnd], recv_sem=vrecv_sem.at[rnd],
                device_id={"dp": lax.rem(me + j, n_dp)}, device_id_type=MESH,
            ).start()
            return 0

        lax.fori_loop(1, n_dp, share, 0)

    def receive_v(rnd):
        wait_bytes(vbuf.at[rnd, pl.ds(0, n_dp - 1)], vrecv_sem.at[rnd])
        for k in range(n_dp):
            vb[:, k * width:(k + 1) * width] = jnp.broadcast_to(vbuf[rnd, k], (8, width))

    def lane_sums(slot, k, acc):
        rsend[slot, pl.ds(k, 1), :] = jnp.sum(acc.T, axis=0, keepdims=True)

    def send_rows(slot):
        def share(j, _):
            pltpu.make_async_remote_copy(
                src_ref=rsend.at[slot], dst_ref=rrecv.at[slot, j - 1],
                send_sem=rsend_sem.at[slot], recv_sem=rrecv_sem.at[slot],
                device_id={"proto": lax.rem(mp + j, n_pr)}, device_id_type=MESH,
            ).start()
            return 0

        lax.fori_loop(1, n_pr, share, 0)

    def receive_rows(slot):
        wait_bytes(rrecv.at[slot], rrecv_sem.at[slot])
        return 1.0 / (rsend[slot] + jnp.sum(rrecv[slot], axis=0))

    def widen(u, out):
        for k in range(blocks):
            out[k * 128:(k + 1) * 128, :] = jnp.broadcast_to(u[k:k + 1, :], (128, 128)).T

    def row_pass(rnd):
        def body(k, _):
            r = pl.ds(pl.multiple_of(k * 128, 128), 128)
            acc = jnp.zeros((16, 8, 128), F32)
            for t in range(cols // 128):
                e = expo[r, t * 128:(t + 1) * 128].reshape(16, 8, 128)
                acc = acc + e * vb[:, t * 128:(t + 1) * 128][None]
            lane_sums(rnd, k, acc.reshape(128, 128))
            return 0

        lax.fori_loop(0, blocks, body, 0)

    def col_pass(rnd):
        def body(i, _):
            owner = lax.rem(me + 1 + i, n_dp)
            c = pl.ds(pl.multiple_of(owner * width, width), width)

            def inner(b, acc):
                r = pl.ds(pl.multiple_of(b * 128, 128), 128)
                u = ub[r, :].reshape(16, 8, 128)
                e = expo[r, c].reshape(16, 8, width)
                new = [e[:, :, t * 128:(t + 1) * 128] * u for t in range(width // 128)]
                return tuple(a + jnp.sum(x, axis=0) for a, x in zip(acc, new))

            acc = lax.fori_loop(0, blocks, inner, (jnp.zeros((8, 128), F32),) * (width // 128))
            csend[rnd, owner] = jnp.sum(jnp.concatenate(acc, axis=1), axis=0, keepdims=True)

            @pl.when(i < n_dp - 1)
            def _():
                send_cols(rnd, owner, i)

            return 0

        lax.fori_loop(0, n_dp, body, 0)

    half = n_dp // 4
    student(0, half)
    finish_cols(0)
    student(half, 2 * half)
    receive_v(0)
    for rnd in range(ROUNDS):
        row_pass(rnd)
        send_rows(rnd)
        if rnd == 0:
            student(2 * half, 3 * half)
        if rnd == 1:
            student(3 * half, 4 * half)

            def student_rows(k, _):
                lane_sums(ROUNDS, k, part[pl.ds(pl.multiple_of(k * 128, 128), 128), :])
                return 0

            lax.fori_loop(0, blocks, student_rows, 0)
            send_rows(ROUNDS)
        u = receive_rows(rnd)
        if rnd < ROUNDS - 1:
            widen(u, ub)
            col_pass(rnd + 1)
            finish_cols(rnd + 1)
            receive_v(rnd + 1)
        else:
            widen(u * factor, ub)
    widen(receive_rows(ROUNDS) * factor, pb)

    hat[...] = jnp.zeros_like(hat)

    def span(turn, k):
        chunk = lax.rem(jnp.where(turn == 0, z + nz - k, z + k), nz)
        return pl.ds(pl.multiple_of(chunk * 2 * width + turn * width, width), width)

    def copy(src, dst, send, recv, to):
        return pltpu.make_async_remote_copy(
            src_ref=src, dst_ref=dst, send_sem=send, recv_sem=recv, device_id=to, device_id_type=MESH)

    def grad_block(b, _):
        step = b // 2
        turn = lax.rem(b, 2)
        c = span(turn, lax.rem(step + 1, nz))
        ws = wsn[:, c]
        v = vb[:, c]
        for m in range(rows // 256):
            r = pl.ds(m * 256, 256)
            logits = jnp.dot(sh[r, :], ws, preferred_element_type=F32)
            e = jnp.exp2(logits * (LOG2E / STUDENT_TEMP)).reshape(32, 8, width)
            q = expo[r, c].reshape(32, 8, width)
            us = ub[r, :].reshape(32, 8, 128)
            ps = pb[r, :].reshape(32, 8, 128)
            g = []
            for t in range(width // 128):
                lanes = slice(t * 128, (t + 1) * 128)
                g.append(e[:, :, lanes] * ps - q[:, :, lanes] * us * v[None, :, lanes])
            g = jnp.concatenate(g, axis=2).reshape(256, width).astype(BF16)
            gbuf[r, :] = g
            hat[r, :] += lax.dot_general(g, ws, (((1,), (1,)), ((), ())), preferred_element_type=F32)
        ubuf[b] = jnp.dot(st[...], gbuf[...], preferred_element_type=F32)
        copy(ubuf.at[b, pl.ds(0, part_rows)], yrecv.at[b], ysend_sem, yrecv_sem.at[b], other).start()
        return 0

    half_rows = rows // 2
    x_rows = half_rows // nx

    def peer(nx_, nh, ncore):
        return {"proto": (nx_ * 2 + nh) * 2 + ncore}

    mine = pl.multiple_of(core * half_rows, half_rows)
    theirs = pl.multiple_of((1 - core) * half_rows, half_rows)

    def x_start(xx):
        return pl.multiple_of(xx * x_rows, x_rows)

    def hat_1():
        copy(hat.at[pl.ds(theirs, half_rows)], h1, hsend_sem.at[0], hrecv_sem.at[0], peer(x, h, 1 - core)).start()

    def hat_2():
        wait_bytes(h1, hrecv_sem.at[0])
        hat[pl.ds(mine, half_rows), :] += h1[...]
        for j in range(1, nx):
            to = lax.rem(x + j, nx)
            copy(hat.at[pl.ds(mine + x_start(to), x_rows)], h2.at[j - 1], hsend_sem.at[1], hrecv_sem.at[1],
                 peer(to, h, core)).start()

    def hat_3():
        wait_bytes(h2, hrecv_sem.at[1])
        h3[0] = hat[pl.ds(mine + x_start(x), x_rows), :] + jnp.sum(h2[...], axis=0)
        copy(h3.at[0], h3.at[1], hsend_sem.at[2], hrecv_sem.at[2], peer(x, 1 - h, core)).start()

    def hat_4():
        wait_bytes(h3.at[1], hrecv_sem.at[2])
        r = pl.ds(mine + x_start(x), x_rows)
        grad = h3[0] + h3[1]
        unit, norm = unit_rows(sf_ref[r, :])
        fgb[r, :] = (grad - unit * jnp.sum(unit * grad, axis=1, keepdims=True)) / norm
        for j in range(1, nx):
            copy(fgb.at[r], fgb.at[r], hsend_sem.at[3], hrecv_sem.at[3], peer(lax.rem(x + j, nx), h, core)).start()

    def hat_5():
        wait_bytes(h2, hrecv_sem.at[3])
        r = pl.ds(mine, half_rows)
        copy(fgb.at[r], fgb.at[r], hsend_sem.at[4], hrecv_sem.at[4], peer(x, h, 1 - core)).start()

    def hat_6():
        wait_bytes(h1, hrecv_sem.at[4])
        pltpu.make_async_copy(fgb, fg_ref, out_sem.at[0]).start()

    def piece_rows(p):
        return pl.ds((p + 1) * part_rows, part_rows)

    lax.fori_loop(0, 4, grad_block, 0)
    extra = {3: hat_1, 4: hat_2, 5: hat_3, 6: hat_4, 7: hat_5}
    for s in range(nz):
        for p in range(3):
            for turn in range(2):
                b = 2 * s + turn
                r = piece_rows(p)
                block = ubuf[b, r]
                if p == 0:
                    wait_bytes(yrecv.at[b], yrecv_sem.at[b])
                    block = block + yrecv[b]
                if s > 0:
                    wait_bytes(zrecv.at[turn, s - 1, p], zrecv_sem.at[turn, s - 1, p])
                    block = block + zrecv[turn, s - 1, p]
                if s < nz - 1:
                    ubuf[b, r] = block
                    copy(ubuf.at[b, r], zrecv.at[turn, s, p], zsend_sem, zrecv_sem.at[turn, s, p], sides[turn]).start()
                elif p == 0:
                    gat[turn, 0, r] = block
                else:
                    ubuf[b, r] = block
                    copy(ubuf.at[b, r], brecv.at[turn, p - 1], bsend_sem, brecv_sem.at[turn, p - 1], other).start()
        if s < nz // 2 - 1:
            lax.fori_loop(4 * s + 4, 4 * s + 8, grad_block, 0)
        if s in extra:
            extra[s]()

    def pass_on(turn, k, p):
        r = piece_rows(p)
        copy(gat.at[turn, k, r], gat.at[turn, k + 1, r], gzsend_sem, gzrecv_sem.at[turn, k, p], sides[turn]).start()

    def hand_over(turn, k):
        copy(gat.at[turn, k, piece_rows(0)], gat.at[turn, k, pl.ds(0, part_rows)],
             gysend_sem, gyrecv_sem.at[turn, k], other).start()

    for turn in range(2):
        pass_on(turn, 0, 0)
        hand_over(turn, 0)
    for p in range(1, 3):
        for turn in range(2):
            wait_bytes(brecv.at[turn, p - 1], brecv_sem.at[turn, p - 1])
            r = piece_rows(p)
            gat[turn, 0, r] = ubuf[2 * nz - 2 + turn, r] + brecv[turn, p - 1]
            pass_on(turn, 0, p)

    wait_bytes(yrecv, ysend_sem)
    wait_bytes(zrecv, zsend_sem)
    wait_bytes(brecv, bsend_sem)
    low = pl.ds(pl.multiple_of(y * part_rows, part_rows), part_rows)
    high = pl.ds(pl.multiple_of((1 - y) * part_rows, part_rows), part_rows)
    rest = pl.ds(2 * part_rows, 2 * part_rows)

    def finish(turn, k):
        c = span(turn, k)
        wait_bytes(gat.at[turn, k, pl.ds(0, part_rows)], gyrecv_sem.at[turn, k])
        places = ((low, pl.ds(part_rows, part_rows)), (high, pl.ds(0, part_rows)), (rest, rest))
        wide = [sp_ref[here, c].astype(F32) for here, _ in places]
        square = sum(jnp.sum(w * w, axis=0, keepdims=True) for w in wide)
        norm = jnp.sqrt(square + EPS)
        units = [w / norm for w in wide]
        grads = [gat[turn, k, there] for _, there in places]
        along = sum(jnp.sum(u * g, axis=0, keepdims=True) for u, g in zip(units, grads))
        b = 2 * k + turn
        for (here, _), u, g in zip(places, units, grads):
            ubuf[b, here] = (g - u * along) / norm
        pltpu.make_async_copy(ubuf.at[b], pg_ref.at[:, c], out_sem.at[1]).start()

    def gather_step(s, _):
        for p in range(3):
            for turn in range(2):
                wait_bytes(gat.at[turn, s + 1, piece_rows(p)], gzrecv_sem.at[turn, s, p])

                @pl.when(s < nz - 2)
                def _():
                    pass_on(turn, s + 1, p)

                if p == 0:
                    hand_over(turn, s + 1)
        for turn in range(2):
            finish(turn, s)
        return 0

    hat_6()
    lax.fori_loop(0, nz - 1, gather_step, 0)
    for turn in range(2):
        finish(turn, nz - 1)

    wait_bytes(zrecv, gzsend_sem)
    wait_bytes(yrecv, gysend_sem)
    wait_bytes(h1, hsend_sem.at[0])
    wait_bytes(h2, hsend_sem.at[1])
    wait_bytes(h3.at[1], hsend_sem.at[2])
    wait_bytes(h2, hsend_sem.at[3])
    wait_bytes(h1, hsend_sem.at[4])
    for rnd in range(ROUNDS):
        wait_bytes(crecv.at[rnd], csend_sem.at[rnd])
        wait_bytes(crecv.at[rnd], vsend_sem.at[rnd])
    for slot in range(ROUNDS + 1):
        wait_bytes(rrecv.at[slot], rsend_sem.at[slot])
    pltpu.make_async_copy(fgb, fg_ref, out_sem.at[0]).wait()
    wait_bytes(ubuf, out_sem.at[1])


def fused(n_dp, n_pr, sf, tf, sp, tp):
    rows, dim = sf.shape
    cols = tp.shape[1]
    width = cols // n_dp
    blocks = rows // 128
    nz, nx = n_dp // 2, n_pr // 4
    quarter = dim // 4
    vmem = pl.BlockSpec(memory_space=pltpu.VMEM)
    anywhere = pl.BlockSpec(memory_space=pl.ANY)
    dma = pltpu.SemaphoreType.DMA
    return pl.pallas_call(
        functools.partial(kernel, n_dp, n_pr),
        out_shape=(
            jax.ShapeDtypeStruct((dim, cols), F32),
            jax.ShapeDtypeStruct((rows, dim), F32),
        ),
        in_specs=[vmem] * 4,
        out_specs=[anywhere] * 2,
        scratch_shapes=[
            pltpu.VMEM((rows, cols), F32),
            pltpu.VMEM((rows, dim), BF16),
            pltpu.VMEM((rows, dim), BF16),
            pltpu.VMEM((rows, 128), F32),
            pltpu.VMEM((8, cols), F32),
            pltpu.VMEM((rows, 128), F32),
            pltpu.VMEM((ROUNDS, n_dp, 1, width), F32),
            pltpu.VMEM((ROUNDS, n_dp - 1, 1, width), F32),
            pltpu.VMEM((ROUNDS, n_dp, 1, width), F32),
            pltpu.VMEM((ROUNDS + 1, blocks, 128), F32),
            pltpu.VMEM((ROUNDS + 1, n_pr - 1, blocks, 128), F32),
            pltpu.VMEM((dim, rows), BF16),
            pltpu.VMEM((dim, cols), BF16),
            pltpu.VMEM((rows, 128), F32),
            pltpu.VMEM((rows, width), BF16),
            pltpu.VMEM((rows, dim), F32),
            pltpu.VMEM((n_dp, dim, width), F32),
            pltpu.VMEM((n_dp, quarter, width), F32),
            pltpu.VMEM((2, nz - 1, 3, quarter, width), F32),
            pltpu.VMEM((2, 2, quarter, width), F32),
            pltpu.VMEM((2, nz, dim, width), F32),
            pltpu.VMEM((rows // 2, dim), F32),
            pltpu.VMEM((nx - 1, rows // 2 // nx, dim), F32),
            pltpu.VMEM((2, rows // 2 // nx, dim), F32),
            pltpu.VMEM((rows, dim), F32),
            dma((ROUNDS,)), dma((ROUNDS,)), dma((ROUNDS,)), dma((ROUNDS,)),
            dma((ROUNDS + 1,)), dma((ROUNDS + 1,)),
            dma, dma((n_dp,)), dma, dma((2, nz - 1, 3)), dma, dma((2, 2)),
            dma, dma((2, nz - 1, 3)), dma, dma((2, nz)), dma((5,)), dma((5,)), dma((2,)),
        ],
        compiler_params=pltpu.CompilerParams(
            collective_id=0, has_side_effects=True, vmem_limit_bytes=56 * 1024 * 1024
        ),
    )(sf, tf, sp, tp)


def solution(mesh):
    in_specs = (P("dp", None), P("dp", None), P(None, "proto"), P(None, "proto"))
    out_specs = (P(None, "proto"), P("dp", None))
    return jax.shard_map(
        functools.partial(fused, mesh.shape["dp"], mesh.shape["proto"]),
        mesh=mesh, in_specs=in_specs, out_specs=out_specs, check_vma=False,
    )
```

```python
import functools
import math

import jax
import jax.numpy as jnp
from jax import lax
from jax.experimental import pallas as pl
from jax.experimental.pallas import tpu as pltpu
from jax.sharding import PartitionSpec as P

PROTOS = 65536
ROUNDS = 3
EPS = 1e-06
TEACHER_TEMP = 0.07
STUDENT_TEMP = 0.1
LOG2E = 1.4426950408889634
MESH = pl.DeviceIdType.MESH
F32 = jnp.float32
BF16 = jnp.bfloat16


def unit_rows(values):
    wide = values.astype(F32)
    norms = jnp.sqrt(jnp.sum(wide * wide, axis=1, keepdims=True) + EPS)
    return (wide / norms, norms)


def unit_cols(values):
    wide = values.astype(F32)
    norms = jnp.sqrt(jnp.sum(wide * wide, axis=0, keepdims=True) + EPS)
    return (wide / norms, norms)


def wait_bytes(ref, sem):
    pltpu.make_async_copy(ref, ref, sem).wait()


def kernel(
    n_dp, n_pr,
    sf_ref, tf_ref, sp_ref, tp_ref,
    pg_ref, fg_ref,
    expo, th, sh, part, vb, ub, racc,
    csend, crecv, rsend, rrecv,
    st, wsn, pb, gbuf, hat, ubuf, yrecv, zrecv, brecv, gat, h1, h2, h3, fgb,
    csend_sem, crecv_sem, rsend_sem, rrecv_sem,
    ysend_sem, yrecv_sem, zsend_sem, zrecv_sem, bsend_sem, brecv_sem,
    gzsend_sem, gzrecv_sem, gysend_sem, gyrecv_sem, hsend_sem, hrecv_sem, out_sem,
):
    rows, dim = sf_ref.shape
    cols = tp_ref.shape[1]
    me = lax.axis_index("dp")
    mp = lax.axis_index("proto")
    width = cols // n_dp
    blocks = rows // 128
    nz = n_dp // 2
    y, z = me // nz, lax.rem(me, nz)
    other = {"dp": (1 - y) * nz + z}
    sides = ({"dp": y * nz + lax.rem(z + 1, nz)}, {"dp": y * nz + lax.rem(z + nz - 1, nz)})
    part_rows = dim // 4
    core, h, x = lax.rem(mp, 2), lax.rem(mp // 2, 2), mp // 4
    nx = n_pr // 4
    factor = PROTOS / math.sqrt(rows * n_dp) / STUDENT_TEMP

    barrier = pltpu.get_barrier_semaphore()

    def greet_dp(j, _):
        pl.semaphore_signal(barrier, inc=1, device_id={"dp": lax.rem(me + j, n_dp)}, device_id_type=MESH)
        return 0

    def greet_pr(j, _):
        pl.semaphore_signal(barrier, inc=1, device_id={"proto": lax.rem(mp + j, n_pr)}, device_id_type=MESH)
        return 0

    lax.fori_loop(1, n_dp, greet_dp, 0)
    lax.fori_loop(1, n_pr, greet_pr, 0)

    def norm_rows(b, _):
        r = pl.ds(pl.multiple_of(b * 128, 128), 128)
        th[r, :] = unit_rows(tf_ref[r, :])[0].astype(BF16)
        return 0

    def norm_student(b, _):
        r = pl.ds(pl.multiple_of(b * 128, 128), 128)
        unit = unit_rows(sf_ref[r, :])[0]
        sh[r, :] = unit.astype(BF16)
        turned = unit.T.astype(BF16)
        st[pl.ds(pl.multiple_of((1 - y) * part_rows, part_rows), part_rows), r] = turned[:part_rows]
        st[pl.ds(pl.multiple_of(y * part_rows, part_rows), part_rows), r] = turned[part_rows:2 * part_rows]
        st[2 * part_rows:, r] = turned[2 * part_rows:]
        return 0

    lax.fori_loop(0, blocks, norm_rows, 0)
    tiles = width // 128
    half_tiles = n_dp * tiles // 2

    def send_cols(rnd, hf):
        r = pl.ds(hf * half_tiles, half_tiles)
        for j in range(1, n_dp):
            pltpu.make_async_remote_copy(
                src_ref=csend.at[rnd, r], dst_ref=crecv.at[rnd, hf, j - 1],
                send_sem=csend_sem.at[rnd, hf], recv_sem=crecv_sem.at[rnd, hf],
                device_id={"dp": lax.rem(me + j, n_dp)}, device_id_type=MESH,
            ).start()

    def put_cols(rnd, k, sums):
        for t in range(tiles):
            csend[rnd, pl.ds(k * tiles + t, 1), :] = sums[:, t * 128:(t + 1) * 128]

    def first_cols(k, _):
        c = pl.ds(pl.multiple_of(k * width, width), width)
        wt = unit_cols(tp_ref[:, c])[0].astype(BF16)
        acc = jnp.zeros((8, width), F32)
        for m in range(rows // 256):
            r = pl.ds(m * 256, 256)
            logits = jnp.dot(th[r, :], wt, preferred_element_type=F32)
            e = jnp.exp2(logits * (LOG2E / TEACHER_TEMP))
            expo[r, c] = e
            acc = acc + jnp.sum(e.reshape(32, 8, width), axis=0)
        put_cols(0, k, jnp.sum(acc, axis=0, keepdims=True))
        return 0

    lax.fori_loop(0, n_dp // 2, first_cols, 0)
    pl.semaphore_wait(barrier, n_dp + n_pr - 2)
    send_cols(0, 0)
    lax.fori_loop(n_dp // 2, n_dp, first_cols, 0)
    send_cols(0, 1)
    lax.fori_loop(0, blocks, norm_student, 0)

    part[...] = jnp.zeros_like(part)

    def student(lo, hi):
        def body(k, _):
            c = pl.ds(pl.multiple_of(k * width, width), width)
            ws = unit_cols(sp_ref[:, c])[0].astype(BF16)
            wsn[:, c] = ws
            for m in range(rows // 256):
                r = pl.ds(m * 256, 256)
                logits = jnp.dot(sh[r, :], ws, preferred_element_type=F32)
                e = jnp.exp2(logits * (LOG2E / STUDENT_TEMP))
                s = e[:, 0:128]
                for t in range(1, width // 128):
                    s = s + e[:, t * 128:(t + 1) * 128]
                part[r, :] += s
            return 0

        lax.fori_loop(lo, hi, body, 0)

    def receive_v(rnd, hf):
        wait_bytes(crecv.at[rnd, hf], crecv_sem.at[rnd, hf])
        v = 1.0 / (csend[rnd, pl.ds(hf * half_tiles, half_tiles), :] + jnp.sum(crecv[rnd, hf], axis=0))
        for t in range(half_tiles):
            lanes = slice((hf * half_tiles + t) * 128, (hf * half_tiles + t + 1) * 128)
            vb[:, lanes] = jnp.broadcast_to(v[t:t + 1, :], (8, 128))

    def lane_sums(slot, k, acc):
        rsend[slot, pl.ds(k, 1), :] = jnp.sum(acc.T, axis=0, keepdims=True)

    def send_rows(slot):
        for j in range(1, n_pr):
            pltpu.make_async_remote_copy(
                src_ref=rsend.at[slot], dst_ref=rrecv.at[slot, j - 1],
                send_sem=rsend_sem.at[slot], recv_sem=rrecv_sem.at[slot],
                device_id={"proto": lax.rem(mp + j, n_pr)}, device_id_type=MESH,
            ).start()

    def receive_rows(slot):
        wait_bytes(rrecv.at[slot], rrecv_sem.at[slot])
        return 1.0 / (rsend[slot] + jnp.sum(rrecv[slot], axis=0))

    def widen(u, out):
        for k in range(blocks):
            out[k * 128:(k + 1) * 128, :] = jnp.broadcast_to(u[k:k + 1, :], (128, 128)).T

    def row_pass(rnd, hf):
        def body(k, _):
            r = pl.ds(pl.multiple_of(k * 128, 128), 128)
            acc = racc[r, :].reshape(16, 8, 128) if hf else jnp.zeros((16, 8, 128), F32)
            for t in range(hf * half_tiles, (hf + 1) * half_tiles):
                e = expo[r, t * 128:(t + 1) * 128].reshape(16, 8, 128)
                acc = acc + e * vb[:, t * 128:(t + 1) * 128][None]
            if hf:
                lane_sums(rnd, k, acc.reshape(128, 128))
            else:
                racc[r, :] = acc.reshape(128, 128)
            return 0

        lax.fori_loop(0, blocks, body, 0)

    def col_pass(rnd, hf):
        def body(i, _):
            k = hf * (n_dp // 2) + i
            c = pl.ds(pl.multiple_of(k * width, width), width)

            def inner(b, acc):
                r = pl.ds(pl.multiple_of(b * 128, 128), 128)
                u = ub[r, :].reshape(16, 8, 128)
                e = expo[r, c].reshape(16, 8, width)
                new = [e[:, :, t * 128:(t + 1) * 128] * u for t in range(tiles)]
                return tuple(a + jnp.sum(n, axis=0) for a, n in zip(acc, new))

            acc = lax.fori_loop(0, blocks, inner, (jnp.zeros((8, 128), F32),) * tiles)
            put_cols(rnd, k, jnp.sum(jnp.concatenate(acc, axis=1), axis=0, keepdims=True))
            return 0

        lax.fori_loop(0, n_dp // 2, body, 0)

    share = n_dp // 4
    student(0, share)
    for rnd in range(ROUNDS):
        if rnd == 1:
            student(2 * share, 3 * share)
        receive_v(rnd, 0)
        row_pass(rnd, 0)
        receive_v(rnd, 1)
        row_pass(rnd, 1)
        send_rows(rnd)
        if rnd == 0:
            student(share, 2 * share)
        if rnd == 1:
            student(3 * share, 4 * share)

            def student_rows(k, _):
                lane_sums(ROUNDS, k, part[pl.ds(pl.multiple_of(k * 128, 128), 128), :])
                return 0

            lax.fori_loop(0, blocks, student_rows, 0)
            send_rows(ROUNDS)
        u = receive_rows(rnd)
        if rnd < ROUNDS - 1:
            widen(u, ub)
            col_pass(rnd + 1, 0)
            send_cols(rnd + 1, 0)
            col_pass(rnd + 1, 1)
            send_cols(rnd + 1, 1)
        else:
            widen(u * factor, ub)
    widen(receive_rows(ROUNDS) * factor, pb)

    hat[...] = jnp.zeros_like(hat)

    def span(rel, hc):
        chunk = lax.rem(z + rel, nz)
        return pl.ds(pl.multiple_of((chunk * 2 + hc) * width, width), width)

    def copy(src, dst, send, recv, to):
        return pltpu.make_async_remote_copy(
            src_ref=src, dst_ref=dst, send_sem=send, recv_sem=recv, device_id=to, device_id_type=MESH)

    def grad_block(b, _):
        q = b // 2
        far = nz // 2 - (q + 1) // 2
        c = span(jnp.where(lax.rem(q, 2) == 1, far, nz - far), lax.rem(b, 2))
        ws = wsn[:, c]
        v = vb[:, c]
        for m in range(rows // 256):
            r = pl.ds(m * 256, 256)
            logits = jnp.dot(sh[r, :], ws, preferred_element_type=F32)
            e = jnp.exp2(logits * (LOG2E / STUDENT_TEMP)).reshape(32, 8, width)
            q = expo[r, c].reshape(32, 8, width)
            us = ub[r, :].reshape(32, 8, 128)
            ps = pb[r, :].reshape(32, 8, 128)
            g = []
            for t in range(width // 128):
                lanes = slice(t * 128, (t + 1) * 128)
                g.append(e[:, :, lanes] * ps - q[:, :, lanes] * us * v[None, :, lanes])
            g = jnp.concatenate(g, axis=2).reshape(256, width).astype(BF16)
            gbuf[r, :] = g
            hat[r, :] += lax.dot_general(g, ws, (((1,), (1,)), ((), ())), preferred_element_type=F32)
        ubuf[b] = jnp.dot(st[...], gbuf[...], preferred_element_type=F32)
        copy(ubuf.at[b, pl.ds(0, part_rows)], yrecv.at[b], ysend_sem, yrecv_sem.at[b], other).start()
        return 0

    half_rows = rows // 2
    x_rows = half_rows // nx

    def peer(nx_, nh, ncore):
        return {"proto": (nx_ * 2 + nh) * 2 + ncore}

    mine = pl.multiple_of(core * half_rows, half_rows)
    theirs = pl.multiple_of((1 - core) * half_rows, half_rows)

    def x_start(xx):
        return pl.multiple_of(xx * x_rows, x_rows)

    def hat_1():
        copy(hat.at[pl.ds(theirs, half_rows)], h1, hsend_sem.at[0], hrecv_sem.at[0], peer(x, h, 1 - core)).start()

    def hat_2():
        wait_bytes(h1, hrecv_sem.at[0])
        hat[pl.ds(mine, half_rows), :] += h1[...]
        for j in range(1, nx):
            to = lax.rem(x + j, nx)
            copy(hat.at[pl.ds(mine + x_start(to), x_rows)], h2.at[j - 1], hsend_sem.at[1], hrecv_sem.at[1],
                 peer(to, h, core)).start()

    def hat_3():
        wait_bytes(h2, hrecv_sem.at[1])
        h3[0] = hat[pl.ds(mine + x_start(x), x_rows), :] + jnp.sum(h2[...], axis=0)
        copy(h3.at[0], h3.at[1], hsend_sem.at[2], hrecv_sem.at[2], peer(x, 1 - h, core)).start()

    def hat_4():
        wait_bytes(h3.at[1], hrecv_sem.at[2])
        r = pl.ds(mine + x_start(x), x_rows)
        grad = h3[0] + h3[1]
        unit, norm = unit_rows(sf_ref[r, :])
        fgb[r, :] = (grad - unit * jnp.sum(unit * grad, axis=1, keepdims=True)) / norm
        for j in range(1, nx):
            copy(fgb.at[r], fgb.at[r], hsend_sem.at[3], hrecv_sem.at[3], peer(lax.rem(x + j, nx), h, core)).start()

    def hat_5():
        wait_bytes(h2, hrecv_sem.at[3])
        r = pl.ds(mine, half_rows)
        copy(fgb.at[r], fgb.at[r], hsend_sem.at[4], hrecv_sem.at[4], peer(x, h, 1 - core)).start()

    def hat_6():
        wait_bytes(h1, hrecv_sem.at[4])
        pltpu.make_async_copy(fgb, fg_ref, out_sem.at[0]).start()

    def piece_rows(p):
        return pl.ds((p + 1) * part_rows, part_rows)

    top = nz // 2

    def arrive(q, hc, p):
        b = 2 * q + hc
        block = ubuf[b, piece_rows(p)]
        if p == 0:
            wait_bytes(yrecv.at[b], yrecv_sem.at[b])
            block = block + yrecv[b]
        return block

    def landed(turn, t, hc, p):
        wait_bytes(zrecv.at[turn, t, hc, p], zrecv_sem.at[turn, t, hc, p])
        return zrecv[turn, t, hc, p]

    def ring(t, pieces):
        for p in pieces:
            for hc in range(2):
                for turn in range(2):
                    if t == 0 and hc != turn:
                        continue
                    q = 2 * t - 1 + turn if t else 0
                    b = 2 * q + hc
                    block = arrive(q, hc, p)
                    if t > 1 or (t == 1 and hc == turn):
                        block = block + landed(turn, t - 1, hc, p)
                    ubuf[b, piece_rows(p)] = block
                    copy(ubuf.at[b, piece_rows(p)], zrecv.at[turn, t, hc, p],
                         zsend_sem.at[turn, min(t, 1)], zrecv_sem.at[turn, t, hc, p], sides[turn]).start()

    def pass_on(t, turn, hc, p):
        if t == top - 1 and hc != turn:
            return
        src = 2 * t - 1 + turn if t else 0
        dst = min(2 * t + 1 + turn, nz - 1)
        r = piece_rows(p)
        copy(gat.at[src, hc, r], gat.at[dst, hc, r], gzsend_sem.at[turn, min(top - 1 - t, 1)],
             gzrecv_sem.at[dst, hc, p], sides[turn]).start()

    def hand_over(slot, hc):
        copy(gat.at[slot, hc, piece_rows(0)], gat.at[slot, hc, pl.ds(0, part_rows)],
             gysend_sem, gyrecv_sem.at[slot, hc], other).start()

    lax.fori_loop(0, 2, grad_block, 0)
    ring(0, (1, 2))
    lax.fori_loop(2, 6, grad_block, 0)
    ring(0, (0,))
    for t in range(1, top):
        ring(t, (1, 2, 0))
        if t < top - 1:
            lax.fori_loop(4 * t + 2, 4 * t + (6 if t < top - 2 else 8), grad_block, 0)
    own = 2 * nz - 2
    hat_1()
    for p in range(1, 3):
        for hc in range(2):
            block = arrive(nz - 1, hc, p)
            ubuf[own + hc, piece_rows(p)] = block + landed(0, top - 1, hc, p) + landed(1, top - 1, hc, p)
            copy(ubuf.at[own + hc, piece_rows(p)], brecv.at[hc, p - 1], bsend_sem, brecv_sem.at[hc, p - 1], other).start()
    for hc in range(2):
        gat[0, hc, piece_rows(0)] = arrive(nz - 1, hc, 0) + landed(0, top - 1, hc, 0) + landed(1, top - 1, hc, 0)
        for turn in range(2):
            pass_on(0, turn, hc, 0)
        hand_over(0, hc)
    hat_2()
    for p in range(1, 3):
        for hc in range(2):
            wait_bytes(brecv.at[hc, p - 1], brecv_sem.at[hc, p - 1])
            gat[0, hc, piece_rows(p)] = ubuf[own + hc, piece_rows(p)] + brecv[hc, p - 1]
            for turn in range(2):
                pass_on(0, turn, hc, p)

    wait_bytes(yrecv, ysend_sem)
    for turn in range(2):
        wait_bytes(zrecv.at[turn, 0, turn], zsend_sem.at[turn, 0])
        wait_bytes(zrecv.at[turn, pl.ds(1, top - 1)], zsend_sem.at[turn, 1])
    wait_bytes(brecv, bsend_sem)
    low = pl.ds(pl.multiple_of(y * part_rows, part_rows), part_rows)
    high = pl.ds(pl.multiple_of((1 - y) * part_rows, part_rows), part_rows)
    rest = pl.ds(2 * part_rows, 2 * part_rows)

    def finish(b, _):
        slot = b // 2
        hc = lax.rem(b, 2)
        far = (slot + 1) // 2
        c = span(jnp.where(lax.rem(slot, 2) == 1, nz - far, far), hc)
        wait_bytes(gat.at[slot, hc, pl.ds(0, part_rows)], gyrecv_sem.at[slot, hc])
        places = ((low, pl.ds(part_rows, part_rows)), (high, pl.ds(0, part_rows)), (rest, rest))
        wide = [sp_ref[here, c].astype(F32) for here, _ in places]
        square = sum(jnp.sum(w * w, axis=0, keepdims=True) for w in wide)
        norm = jnp.sqrt(square + EPS)
        units = [w / norm for w in wide]
        grads = [gat[slot, hc, there] for _, there in places]
        along = sum(jnp.sum(u * g, axis=0, keepdims=True) for u, g in zip(units, grads))
        for (here, _), u, g in zip(places, units, grads):
            ubuf[b, here] = (g - u * along) / norm
        pltpu.make_async_copy(ubuf.at[b], pg_ref.at[:, c], out_sem.at[1]).start()
        return 0

    hat_3()
    later = {0: hat_4, 1: hat_5, 2: hat_6}
    for t in range(top):
        for p in range(3):
            for hc in range(2):
                for turn in range(2):
                    if t == top - 1 and hc != turn:
                        continue
                    slot = min(2 * t + 1 + turn, nz - 1)
                    wait_bytes(gat.at[slot, hc, piece_rows(p)], gzrecv_sem.at[slot, hc, p])
                    if t < top - 1:
                        pass_on(t + 1, turn, hc, p)
                    if p == 0:
                        hand_over(slot, hc)
        if t == 0:
            lax.fori_loop(0, 2, finish, 0)
        else:
            lax.fori_loop(4 * t - 2, 4 * t + 2, finish, 0)
        if t in later:
            later[t]()
    lax.fori_loop(2 * nz - 2, 2 * nz, finish, 0)

    for turn in range(2):
        wait_bytes(zrecv.at[turn, 0, turn], gzsend_sem.at[turn, 0])
        wait_bytes(zrecv.at[turn, pl.ds(1, top - 1)], gzsend_sem.at[turn, 1])
    wait_bytes(yrecv, gysend_sem)
    wait_bytes(h1, hsend_sem.at[0])
    wait_bytes(h2, hsend_sem.at[1])
    wait_bytes(h3.at[1], hsend_sem.at[2])
    wait_bytes(h2, hsend_sem.at[3])
    wait_bytes(h1, hsend_sem.at[4])
    for rnd in range(ROUNDS):
        for hf in range(2):
            wait_bytes(crecv.at[rnd, hf], csend_sem.at[rnd, hf])
    for slot in range(ROUNDS + 1):
        wait_bytes(rrecv.at[slot], rsend_sem.at[slot])
    pltpu.make_async_copy(fgb, fg_ref, out_sem.at[0]).wait()
    wait_bytes(ubuf, out_sem.at[1])


def fused(n_dp, n_pr, sf, tf, sp, tp):
    rows, dim = sf.shape
    cols = tp.shape[1]
    width = cols // n_dp
    blocks = rows // 128
    nz, nx = n_dp // 2, n_pr // 4
    quarter = dim // 4
    vmem = pl.BlockSpec(memory_space=pltpu.VMEM)
    anywhere = pl.BlockSpec(memory_space=pl.ANY)
    dma = pltpu.SemaphoreType.DMA
    return pl.pallas_call(
        functools.partial(kernel, n_dp, n_pr),
        out_shape=(
            jax.ShapeDtypeStruct((dim, cols), F32),
            jax.ShapeDtypeStruct((rows, dim), F32),
        ),
        in_specs=[vmem] * 4,
        out_specs=[anywhere] * 2,
        scratch_shapes=[
            pltpu.VMEM((rows, cols), F32),
            pltpu.VMEM((rows, dim), BF16),
            pltpu.VMEM((rows, dim), BF16),
            pltpu.VMEM((rows, 128), F32),
            pltpu.VMEM((8, cols), F32),
            pltpu.VMEM((rows, 128), F32),
            pltpu.VMEM((rows, 128), F32),
            pltpu.VMEM((ROUNDS, cols // 128, 128), F32),
            pltpu.VMEM((ROUNDS, 2, n_dp - 1, cols // 256, 128), F32),
            pltpu.VMEM((ROUNDS + 1, blocks, 128), F32),
            pltpu.VMEM((ROUNDS + 1, n_pr - 1, blocks, 128), F32),
            pltpu.VMEM((dim, rows), BF16),
            pltpu.VMEM((dim, cols), BF16),
            pltpu.VMEM((rows, 128), F32),
            pltpu.VMEM((rows, width), BF16),
            pltpu.VMEM((rows, dim), F32),
            pltpu.VMEM((n_dp, dim, width), F32),
            pltpu.VMEM((n_dp, quarter, width), F32),
            pltpu.VMEM((2, nz // 2, 2, 3, quarter, width), F32),
            pltpu.VMEM((2, 2, quarter, width), F32),
            pltpu.VMEM((nz, 2, dim, width), F32),
            pltpu.VMEM((rows // 2, dim), F32),
            pltpu.VMEM((nx - 1, rows // 2 // nx, dim), F32),
            pltpu.VMEM((2, rows // 2 // nx, dim), F32),
            pltpu.VMEM((rows, dim), F32),
            dma((ROUNDS, 2)), dma((ROUNDS, 2)),
            dma((ROUNDS + 1,)), dma((ROUNDS + 1,)),
            dma, dma((n_dp,)), dma((2, 2)), dma((2, nz // 2, 2, 3)), dma, dma((2, 2)),
            dma((2, 2)), dma((nz, 2, 3)), dma, dma((nz, 2)), dma((5,)), dma((5,)), dma((2,)),
        ],
        compiler_params=pltpu.CompilerParams(
            collective_id=0, has_side_effects=True, vmem_limit_bytes=56 * 1024 * 1024
        ),
    )(sf, tf, sp, tp)


def solution(mesh):
    in_specs = (P("dp", None), P("dp", None), P(None, "proto"), P(None, "proto"))
    out_specs = (P(None, "proto"), P("dp", None))
    return jax.shard_map(
        functools.partial(fused, mesh.shape["dp"], mesh.shape["proto"]),
        mesh=mesh, in_specs=in_specs, out_specs=out_specs, check_vma=False,
    )
```

```python
import functools
import math

import jax
import jax.numpy as jnp
from jax import lax
from jax.experimental import pallas as pl
from jax.experimental.pallas import tpu as pltpu
from jax.sharding import PartitionSpec as P

PROTOS = 65536
ROUNDS = 3
EPS = 1e-06
TEACHER_TEMP = 0.07
STUDENT_TEMP = 0.1
LOG2E = 1.4426950408889634
MESH = pl.DeviceIdType.MESH
F32 = jnp.float32
BF16 = jnp.bfloat16


def unit_rows(values):
    wide = values.astype(F32)
    norms = jnp.sqrt(jnp.sum(wide * wide, axis=1, keepdims=True) + EPS)
    return (wide * (1.0 / norms), norms)


def unit_cols(values):
    wide = values.astype(F32)
    norms = jnp.sqrt(jnp.sum(wide * wide, axis=0, keepdims=True) + EPS)
    return (wide * (1.0 / norms), norms)


def wait_bytes(ref, sem):
    pltpu.make_async_copy(ref, ref, sem).wait()


def kernel(
    n_dp, n_pr,
    sf_in, tf_in, sp_in, tp_in,
    pg_ref, fg_ref,
    sf_ref, tf_ref, sp_ref, tp_ref, wts,
    expo, th, sh, part, vb, ub, racc,
    csend, crecv, rsend, rrecv,
    st, wsn, pb, gbuf, hat, ubuf, yrecv, zrecv, brecv, gat, h1, h2, h3,
    csend_sem, crecv_sem, rsend_sem, rrecv_sem,
    ysend_sem, yrecv_sem, zsend_sem, zrecv_sem, bsend_sem, brecv_sem,
    gzsend_sem, gzrecv_sem, gysend_sem, gyrecv_sem, hsend_sem, hrecv_sem, in_sem,
):
    rows, dim = sf_ref.shape
    cols = tp_ref.shape[1]
    me = lax.axis_index("dp")
    mp = lax.axis_index("proto")
    width = cols // n_dp
    blocks = rows // 128
    nz = n_dp // 2
    y, z = me // nz, lax.rem(me, nz)
    other = {"dp": (1 - y) * nz + z}
    sides = ({"dp": y * nz + lax.rem(z + 1, nz)}, {"dp": y * nz + lax.rem(z + nz - 1, nz)})
    part_rows = dim // 4
    core, h, x = lax.rem(mp, 2), lax.rem(mp // 2, 2), mp // 4
    nx = n_pr // 4
    factor = PROTOS / math.sqrt(rows * n_dp) / STUDENT_TEMP

    loads = [
        pltpu.make_async_copy(src, dst, in_sem.at[k])
        for k, (src, dst) in enumerate(((tf_in, tf_ref), (tp_in, tp_ref), (sf_in, sf_ref), (sp_in, sp_ref)))
    ]
    for load in loads:
        load.start()
    barrier = pltpu.get_barrier_semaphore()

    def greet_dp(j, _):
        pl.semaphore_signal(barrier, inc=1, device_id={"dp": lax.rem(me + j, n_dp)}, device_id_type=MESH)
        return 0

    def greet_pr(j, _):
        pl.semaphore_signal(barrier, inc=1, device_id={"proto": lax.rem(mp + j, n_pr)}, device_id_type=MESH)
        return 0

    lax.fori_loop(1, n_dp, greet_dp, 0)
    lax.fori_loop(1, n_pr, greet_pr, 0)

    def norm_rows(b, _):
        r = pl.ds(pl.multiple_of(b * 128, 128), 128)
        th[r, :] = unit_rows(tf_ref[r, :])[0].astype(BF16)
        return 0

    def norm_student(b, _):
        r = pl.ds(pl.multiple_of(b * 128, 128), 128)
        unit = unit_rows(sf_ref[r, :])[0]
        sh[r, :] = unit.astype(BF16)
        turned = unit.T.astype(BF16)
        st[pl.ds(pl.multiple_of((1 - y) * part_rows, part_rows), part_rows), r] = turned[:part_rows]
        st[pl.ds(pl.multiple_of(y * part_rows, part_rows), part_rows), r] = turned[part_rows:2 * part_rows]
        st[2 * part_rows:, r] = turned[2 * part_rows:]
        return 0

    loads[0].wait()
    lax.fori_loop(0, blocks, norm_rows, 0)
    loads[1].wait()
    tiles = width // 128
    half_tiles = n_dp * tiles // 2

    def send_cols(rnd, hf):
        r = pl.ds(hf * half_tiles, half_tiles)
        for j in range(1, n_dp):
            pltpu.make_async_remote_copy(
                src_ref=csend.at[rnd, r], dst_ref=crecv.at[rnd, hf, j - 1],
                send_sem=csend_sem.at[rnd, hf], recv_sem=crecv_sem.at[rnd, hf],
                device_id={"dp": lax.rem(me + j, n_dp)}, device_id_type=MESH,
            ).start()

    def put_cols(rnd, k, sums):
        for t in range(tiles):
            csend[rnd, pl.ds(k * tiles + t, 1), :] = sums[:, t * 128:(t + 1) * 128]

    def teacher_unit(k):
        c = pl.ds(pl.multiple_of(k * width, width), width)
        return unit_cols(tp_ref[:, c])[0].astype(BF16)

    def first_cols(k, _):
        c = pl.ds(pl.multiple_of(k * width, width), width)
        wt = wts[lax.rem(k, 2)]
        wts[lax.rem(k + 1, 2)] = teacher_unit(jnp.minimum(k + 1, n_dp - 1))
        acc = jnp.zeros((8, width), F32)
        for m in range(rows // 256):
            r = pl.ds(m * 256, 256)
            logits = jnp.dot(th[r, :], wt, preferred_element_type=F32)
            e = jnp.exp2(logits * (LOG2E / TEACHER_TEMP))
            expo[r, c] = e
            acc = acc + jnp.sum(e.reshape(32, 8, width), axis=0)
        put_cols(0, k, jnp.sum(acc, axis=0, keepdims=True))
        return 0

    wts[0] = teacher_unit(0)
    lax.fori_loop(0, n_dp // 2, first_cols, 0, unroll=2)
    pl.semaphore_wait(barrier, n_dp + n_pr - 2)
    send_cols(0, 0)
    lax.fori_loop(n_dp // 2, n_dp, first_cols, 0, unroll=2)
    send_cols(0, 1)
    loads[2].wait()
    lax.fori_loop(0, blocks, norm_student, 0)
    loads[3].wait()

    part[...] = jnp.zeros_like(part)

    def student(lo, hi):
        def body(k, _):
            c = pl.ds(pl.multiple_of(k * width, width), width)
            ws = unit_cols(sp_ref[:, c])[0].astype(BF16)
            wsn[:, c] = ws
            for m in range(rows // 256):
                r = pl.ds(m * 256, 256)
                logits = jnp.dot(sh[r, :], ws, preferred_element_type=F32)
                e = jnp.exp2(logits * (LOG2E / STUDENT_TEMP))
                s = e[:, 0:128]
                for t in range(1, width // 128):
                    s = s + e[:, t * 128:(t + 1) * 128]
                part[r, :] += s
            return 0

        lax.fori_loop(lo, hi, body, 0)

    def receive_v(rnd, hf):
        wait_bytes(crecv.at[rnd, hf], crecv_sem.at[rnd, hf])
        v = 1.0 / (csend[rnd, pl.ds(hf * half_tiles, half_tiles), :] + jnp.sum(crecv[rnd, hf], axis=0))
        for t in range(half_tiles):
            lanes = slice((hf * half_tiles + t) * 128, (hf * half_tiles + t + 1) * 128)
            vb[:, lanes] = jnp.broadcast_to(v[t:t + 1, :], (8, 128))

    def lane_sums(slot, k, acc):
        rsend[slot, pl.ds(k, 1), :] = jnp.sum(acc.T, axis=0, keepdims=True)

    def send_rows(slot):
        for j in range(1, n_pr):
            pltpu.make_async_remote_copy(
                src_ref=rsend.at[slot], dst_ref=rrecv.at[slot, j - 1],
                send_sem=rsend_sem.at[slot], recv_sem=rrecv_sem.at[slot],
                device_id={"proto": lax.rem(mp + j, n_pr)}, device_id_type=MESH,
            ).start()

    def receive_rows(slot):
        wait_bytes(rrecv.at[slot], rrecv_sem.at[slot])
        return 1.0 / (rsend[slot] + jnp.sum(rrecv[slot], axis=0))

    def widen(u, out):
        for k in range(blocks):
            out[k * 128:(k + 1) * 128, :] = jnp.broadcast_to(u[k:k + 1, :], (128, 128)).T

    def row_pass(rnd, hf):
        def body(k, _):
            r = pl.ds(pl.multiple_of(k * 128, 128), 128)
            acc = racc[r, :].reshape(16, 8, 128) if hf else jnp.zeros((16, 8, 128), F32)
            for t in range(hf * half_tiles, (hf + 1) * half_tiles):
                e = expo[r, t * 128:(t + 1) * 128].reshape(16, 8, 128)
                acc = acc + e * vb[:, t * 128:(t + 1) * 128][None]
            if hf:
                lane_sums(rnd, k, acc.reshape(128, 128))
            else:
                racc[r, :] = acc.reshape(128, 128)
            return 0

        lax.fori_loop(0, blocks, body, 0)

    def col_pass(rnd, hf):
        def body(i, _):
            k = hf * (n_dp // 2) + i
            c = pl.ds(pl.multiple_of(k * width, width), width)

            def inner(b, acc):
                r = pl.ds(pl.multiple_of(b * 128, 128), 128)
                u = ub[r, :].reshape(16, 8, 128)
                e = expo[r, c].reshape(16, 8, width)
                new = [e[:, :, t * 128:(t + 1) * 128] * u for t in range(tiles)]
                return tuple(a + jnp.sum(n, axis=0) for a, n in zip(acc, new))

            acc = lax.fori_loop(0, blocks, inner, (jnp.zeros((8, 128), F32),) * tiles)
            put_cols(rnd, k, jnp.sum(jnp.concatenate(acc, axis=1), axis=0, keepdims=True))
            return 0

        lax.fori_loop(0, n_dp // 2, body, 0)

    share = n_dp // 4
    student(0, share)
    for rnd in range(ROUNDS):
        if rnd == 1:
            student(2 * share, 3 * share)
        receive_v(rnd, 0)
        row_pass(rnd, 0)
        receive_v(rnd, 1)
        row_pass(rnd, 1)
        send_rows(rnd)
        if rnd == 0:
            student(share, 2 * share)
        if rnd == 1:
            student(3 * share, 4 * share)

            def student_rows(k, _):
                lane_sums(ROUNDS, k, part[pl.ds(pl.multiple_of(k * 128, 128), 128), :])
                return 0

            lax.fori_loop(0, blocks, student_rows, 0)
            send_rows(ROUNDS)
        u = receive_rows(rnd)
        if rnd < ROUNDS - 1:
            widen(u, ub)
            col_pass(rnd + 1, 0)
            send_cols(rnd + 1, 0)
            col_pass(rnd + 1, 1)
            send_cols(rnd + 1, 1)
        else:
            widen(u * factor, ub)
    widen(receive_rows(ROUNDS) * factor, pb)

    hat[...] = jnp.zeros_like(hat)

    def span(rel, hc):
        chunk = lax.rem(z + rel, nz)
        return pl.ds(pl.multiple_of((chunk * 2 + hc) * width, width), width)

    def copy(src, dst, send, recv, to):
        return pltpu.make_async_remote_copy(
            src_ref=src, dst_ref=dst, send_sem=send, recv_sem=recv, device_id=to, device_id_type=MESH)

    def grad_block(b, _):
        q = b // 2
        far = nz // 2 - (q + 1) // 2
        c = span(jnp.where(lax.rem(q, 2) == 1, far, nz - far), lax.rem(b, 2))
        ws = wsn[:, c]
        v = vb[:, c]
        for m in range(rows // 256):
            r = pl.ds(m * 256, 256)
            logits = jnp.dot(sh[r, :], ws, preferred_element_type=F32)
            e = jnp.exp2(logits * (LOG2E / STUDENT_TEMP)).reshape(32, 8, width)
            q = expo[r, c].reshape(32, 8, width)
            us = ub[r, :].reshape(32, 8, 128)
            ps = pb[r, :].reshape(32, 8, 128)
            g = []
            for t in range(width // 128):
                lanes = slice(t * 128, (t + 1) * 128)
                g.append(e[:, :, lanes] * ps - q[:, :, lanes] * us * v[None, :, lanes])
            g = jnp.concatenate(g, axis=2).reshape(256, width).astype(BF16)
            gbuf[r, :] = g
            hat[r, :] += lax.dot_general(g, ws, (((1,), (1,)), ((), ())), preferred_element_type=F32)
        ubuf[b] = jnp.dot(st[...], gbuf[...], preferred_element_type=F32)
        copy(ubuf.at[b, pl.ds(0, part_rows)], yrecv.at[b], ysend_sem, yrecv_sem.at[b], other).start()
        return 0

    half_rows = rows // 2
    x_rows = half_rows // nx

    def peer(nx_, nh, ncore):
        return {"proto": (nx_ * 2 + nh) * 2 + ncore}

    mine = pl.multiple_of(core * half_rows, half_rows)
    theirs = pl.multiple_of((1 - core) * half_rows, half_rows)

    def x_start(xx):
        return pl.multiple_of(xx * x_rows, x_rows)

    def hat_1():
        copy(hat.at[pl.ds(theirs, half_rows)], h1, hsend_sem.at[0], hrecv_sem.at[0], peer(x, h, 1 - core)).start()

    def hat_2():
        wait_bytes(h1, hrecv_sem.at[0])
        hat[pl.ds(mine, half_rows), :] += h1[...]
        for j in range(1, nx):
            to = lax.rem(x + j, nx)
            copy(hat.at[pl.ds(mine + x_start(to), x_rows)], h2.at[j - 1], hsend_sem.at[1], hrecv_sem.at[1],
                 peer(to, h, core)).start()

    def hat_3():
        wait_bytes(h2, hrecv_sem.at[1])
        h3[0] = hat[pl.ds(mine + x_start(x), x_rows), :] + jnp.sum(h2[...], axis=0)
        copy(h3.at[0], h3.at[1], hsend_sem.at[2], hrecv_sem.at[2], peer(x, 1 - h, core)).start()

    def hat_4():
        wait_bytes(h3.at[1], hrecv_sem.at[2])
        r = pl.ds(mine + x_start(x), x_rows)
        grad = h3[0] + h3[1]
        unit, norm = unit_rows(sf_ref[r, :])
        fg_ref[r, :] = (grad - unit * jnp.sum(unit * grad, axis=1, keepdims=True)) / norm
        for j in range(1, nx):
            copy(fg_ref.at[r], fg_ref.at[r], hsend_sem.at[3], hrecv_sem.at[3], peer(lax.rem(x + j, nx), h, core)).start()

    def hat_5():
        wait_bytes(h2, hrecv_sem.at[3])
        r = pl.ds(mine, half_rows)
        copy(fg_ref.at[r], fg_ref.at[r], hsend_sem.at[4], hrecv_sem.at[4], peer(x, h, 1 - core)).start()

    def hat_6():
        wait_bytes(h1, hrecv_sem.at[4])

    def piece_rows(p):
        return pl.ds((p + 1) * part_rows, part_rows)

    top = nz // 2

    def arrive(q, hc, p):
        b = 2 * q + hc
        block = ubuf[b, piece_rows(p)]
        if p == 0:
            wait_bytes(yrecv.at[b], yrecv_sem.at[b])
            block = block + yrecv[b]
        return block

    def landed(turn, t, hc, p):
        wait_bytes(zrecv.at[turn, t, hc, p], zrecv_sem.at[turn, t, hc, p])
        return zrecv[turn, t, hc, p]

    def ring(t, pieces):
        for p in pieces:
            for hc in range(2):
                for turn in range(2):
                    if t == 0 and hc != turn:
                        continue
                    q = 2 * t - 1 + turn if t else 0
                    b = 2 * q + hc
                    block = arrive(q, hc, p)
                    if t > 1 or (t == 1 and hc == turn):
                        block = block + landed(turn, t - 1, hc, p)
                    ubuf[b, piece_rows(p)] = block
                    copy(ubuf.at[b, piece_rows(p)], zrecv.at[turn, t, hc, p],
                         zsend_sem.at[turn, min(t, 1)], zrecv_sem.at[turn, t, hc, p], sides[turn]).start()

    def pass_on(t, turn, hc, p):
        if t == top - 1 and hc != turn:
            return
        src = 2 * t - 1 + turn if t else 0
        dst = min(2 * t + 1 + turn, nz - 1)
        r = piece_rows(p)
        copy(gat.at[src, hc, r], gat.at[dst, hc, r], gzsend_sem.at[turn, min(top - 1 - t, 1)],
             gzrecv_sem.at[dst, hc, p], sides[turn]).start()

    def hand_over(slot, hc):
        copy(gat.at[slot, hc, piece_rows(0)], gat.at[slot, hc, pl.ds(0, part_rows)],
             gysend_sem, gyrecv_sem.at[slot, hc], other).start()

    lax.fori_loop(0, 2, grad_block, 0)
    ring(0, (1, 2))
    lax.fori_loop(2, 6, grad_block, 0)
    ring(0, (0,))
    for t in range(1, top):
        ring(t, (1, 2, 0))
        if t < top - 1:
            lax.fori_loop(4 * t + 2, 4 * t + (6 if t < top - 2 else 8), grad_block, 0)
    own = 2 * nz - 2
    hat_1()
    for p in range(1, 3):
        for hc in range(2):
            block = arrive(nz - 1, hc, p)
            ubuf[own + hc, piece_rows(p)] = block + landed(0, top - 1, hc, p) + landed(1, top - 1, hc, p)
            copy(ubuf.at[own + hc, piece_rows(p)], brecv.at[hc, p - 1], bsend_sem, brecv_sem.at[hc, p - 1], other).start()
    for hc in range(2):
        gat[0, hc, piece_rows(0)] = arrive(nz - 1, hc, 0) + landed(0, top - 1, hc, 0) + landed(1, top - 1, hc, 0)
        for turn in range(2):
            pass_on(0, turn, hc, 0)
        hand_over(0, hc)
    hat_2()
    for p in range(1, 3):
        for hc in range(2):
            wait_bytes(brecv.at[hc, p - 1], brecv_sem.at[hc, p - 1])
            gat[0, hc, piece_rows(p)] = ubuf[own + hc, piece_rows(p)] + brecv[hc, p - 1]
            for turn in range(2):
                pass_on(0, turn, hc, p)

    wait_bytes(yrecv, ysend_sem)
    for turn in range(2):
        wait_bytes(zrecv.at[turn, 0, turn], zsend_sem.at[turn, 0])
        wait_bytes(zrecv.at[turn, pl.ds(1, top - 1)], zsend_sem.at[turn, 1])
    wait_bytes(brecv, bsend_sem)
    low = pl.ds(pl.multiple_of(y * part_rows, part_rows), part_rows)
    high = pl.ds(pl.multiple_of((1 - y) * part_rows, part_rows), part_rows)
    rest = pl.ds(2 * part_rows, 2 * part_rows)

    def finish(b, _):
        slot = b // 2
        hc = lax.rem(b, 2)
        far = (slot + 1) // 2
        c = span(jnp.where(lax.rem(slot, 2) == 1, nz - far, far), hc)
        wait_bytes(gat.at[slot, hc, pl.ds(0, part_rows)], gyrecv_sem.at[slot, hc])
        places = ((low, pl.ds(part_rows, part_rows)), (high, pl.ds(0, part_rows)), (rest, rest))
        wide = [sp_ref[here, c].astype(F32) for here, _ in places]
        square = sum(jnp.sum(w * w, axis=0, keepdims=True) for w in wide)
        inverse = 1.0 / jnp.sqrt(square + EPS)
        units = [w * inverse for w in wide]
        grads = [gat[slot, hc, there] for _, there in places]
        along = sum(jnp.sum(u * g, axis=0, keepdims=True) for u, g in zip(units, grads))
        for (here, _), u, g in zip(places, units, grads):
            pg_ref[here, c] = (g - u * along) * inverse
        return 0

    hat_3()
    later = {0: hat_4, 1: hat_5, 2: hat_6}
    for t in range(top):
        for p in range(3):
            for hc in range(2):
                for turn in range(2):
                    if t == top - 1 and hc != turn:
                        continue
                    slot = min(2 * t + 1 + turn, nz - 1)
                    wait_bytes(gat.at[slot, hc, piece_rows(p)], gzrecv_sem.at[slot, hc, p])
                    if t < top - 1:
                        pass_on(t + 1, turn, hc, p)
                    if p == 0:
                        hand_over(slot, hc)
        if t == 0:
            lax.fori_loop(0, 2, finish, 0)
        else:
            lax.fori_loop(4 * t - 2, 4 * t + 2, finish, 0)
        if t in later:
            later[t]()
    lax.fori_loop(2 * nz - 2, 2 * nz, finish, 0)

    for turn in range(2):
        wait_bytes(zrecv.at[turn, 0, turn], gzsend_sem.at[turn, 0])
        wait_bytes(zrecv.at[turn, pl.ds(1, top - 1)], gzsend_sem.at[turn, 1])
    wait_bytes(yrecv, gysend_sem)
    wait_bytes(h1, hsend_sem.at[0])
    wait_bytes(h2, hsend_sem.at[1])
    wait_bytes(h3.at[1], hsend_sem.at[2])
    wait_bytes(h2, hsend_sem.at[3])
    wait_bytes(h1, hsend_sem.at[4])
    for rnd in range(ROUNDS):
        for hf in range(2):
            wait_bytes(crecv.at[rnd, hf], csend_sem.at[rnd, hf])
    for slot in range(ROUNDS + 1):
        wait_bytes(rrecv.at[slot], rsend_sem.at[slot])


def fused(n_dp, n_pr, sf, tf, sp, tp):
    rows, dim = sf.shape
    cols = tp.shape[1]
    width = cols // n_dp
    blocks = rows // 128
    nz, nx = n_dp // 2, n_pr // 4
    quarter = dim // 4
    vmem = pl.BlockSpec(memory_space=pltpu.VMEM)
    anywhere = pl.BlockSpec(memory_space=pl.ANY)
    dma = pltpu.SemaphoreType.DMA
    return pl.pallas_call(
        functools.partial(kernel, n_dp, n_pr),
        out_shape=(
            pltpu.VMEM((dim, cols), F32),
            pltpu.VMEM((rows, dim), F32),
        ),
        in_specs=[anywhere] * 4,
        out_specs=[vmem] * 2,
        scratch_shapes=[
            pltpu.VMEM((rows, dim), BF16),
            pltpu.VMEM((rows, dim), BF16),
            pltpu.VMEM((dim, cols), BF16),
            pltpu.VMEM((dim, cols), BF16),
            pltpu.VMEM((2, dim, width), BF16),
            pltpu.VMEM((rows, cols), F32),
            pltpu.VMEM((rows, dim), BF16),
            pltpu.VMEM((rows, dim), BF16),
            pltpu.VMEM((rows, 128), F32),
            pltpu.VMEM((8, cols), F32),
            pltpu.VMEM((rows, 128), F32),
            pltpu.VMEM((rows, 128), F32),
            pltpu.VMEM((ROUNDS, cols // 128, 128), F32),
            pltpu.VMEM((ROUNDS, 2, n_dp - 1, cols // 256, 128), F32),
            pltpu.VMEM((ROUNDS + 1, blocks, 128), F32),
            pltpu.VMEM((ROUNDS + 1, n_pr - 1, blocks, 128), F32),
            pltpu.VMEM((dim, rows), BF16),
            pltpu.VMEM((dim, cols), BF16),
            pltpu.VMEM((rows, 128), F32),
            pltpu.VMEM((rows, width), BF16),
            pltpu.VMEM((rows, dim), F32),
            pltpu.VMEM((n_dp, dim, width), F32),
            pltpu.VMEM((n_dp, quarter, width), F32),
            pltpu.VMEM((2, nz // 2, 2, 3, quarter, width), F32),
            pltpu.VMEM((2, 2, quarter, width), F32),
            pltpu.VMEM((nz, 2, dim, width), F32),
            pltpu.VMEM((rows // 2, dim), F32),
            pltpu.VMEM((nx - 1, rows // 2 // nx, dim), F32),
            pltpu.VMEM((2, rows // 2 // nx, dim), F32),
            dma((ROUNDS, 2)), dma((ROUNDS, 2)),
            dma((ROUNDS + 1,)), dma((ROUNDS + 1,)),
            dma, dma((n_dp,)), dma((2, 2)), dma((2, nz // 2, 2, 3)), dma, dma((2, 2)),
            dma((2, 2)), dma((nz, 2, 3)), dma, dma((nz, 2)), dma((5,)), dma((5,)), dma((4,)),
        ],
        compiler_params=pltpu.CompilerParams(
            collective_id=0, has_side_effects=True, vmem_limit_bytes=56 * 1024 * 1024
        ),
    )(sf, tf, sp, tp)


def solution(mesh):
    in_specs = (P("dp", None), P("dp", None), P(None, "proto"), P(None, "proto"))
    out_specs = (P(None, "proto"), P("dp", None))
    return jax.shard_map(
        functools.partial(fused, mesh.shape["dp"], mesh.shape["proto"]),
        mesh=mesh, in_specs=in_specs, out_specs=out_specs, check_vma=False,
    )
```

```python
import functools
import math

import jax
import jax.numpy as jnp
from jax import lax
from jax.experimental import pallas as pl
from jax.experimental.pallas import tpu as pltpu
from jax.sharding import PartitionSpec as P

PROTOS = 65536
ROUNDS = 3
EPS = 1e-06
TEACHER_TEMP = 0.07
STUDENT_TEMP = 0.1
LOG2E = 1.4426950408889634
MESH = pl.DeviceIdType.MESH
F32 = jnp.float32
BF16 = jnp.bfloat16


def unit_rows(values):
    wide = values.astype(F32)
    norms = jnp.sqrt(jnp.sum(wide * wide, axis=1, keepdims=True) + EPS)
    return (wide * (1.0 / norms), norms)


def unit_cols(values):
    wide = values.astype(F32)
    norms = jnp.sqrt(jnp.sum(wide * wide, axis=0, keepdims=True) + EPS)
    return (wide * (1.0 / norms), norms)


def wait_bytes(ref, sem):
    pltpu.make_async_copy(ref, ref, sem).wait()


def kernel(
    n_dp, n_pr,
    sf_in, tf_in, sp_in, tp_in,
    pg_ref, fg_ref,
    sf_ref, tf_ref, sp_ref, tp_ref, wts,
    expo, th, sh, part, vb, ub, racc, first,
    csend, crecv, rsend, rrecv,
    st, wsn, pb, gbuf, hat, ubuf, yrecv, zrecv, brecv, gat, h1, h2, h3,
    csend_sem, crecv_sem, rsend_sem, rrecv_sem,
    ysend_sem, yrecv_sem, zsend_sem, zrecv_sem, bsend_sem, brecv_sem,
    gzsend_sem, gzrecv_sem, gysend_sem, gyrecv_sem, hsend_sem, hrecv_sem, in_sem,
):
    rows, dim = sf_ref.shape
    cols = tp_ref.shape[1]
    me = lax.axis_index("dp")
    mp = lax.axis_index("proto")
    width = cols // n_dp
    blocks = rows // 128
    nz = n_dp // 2
    y, z = me // nz, lax.rem(me, nz)
    other = {"dp": (1 - y) * nz + z}
    sides = ({"dp": y * nz + lax.rem(z + 1, nz)}, {"dp": y * nz + lax.rem(z + nz - 1, nz)})
    part_rows = dim // 4
    core, h, x = lax.rem(mp, 2), lax.rem(mp // 2, 2), mp // 4
    nx = n_pr // 4
    factor = PROTOS / math.sqrt(rows * n_dp) / STUDENT_TEMP

    def peer(nx_, nh, ncore):
        return {"proto": (nx_ * 2 + nh) * 2 + ncore}

    loads = [
        pltpu.make_async_copy(src, dst, in_sem.at[k])
        for k, (src, dst) in enumerate(((tf_in, tf_ref), (tp_in, tp_ref), (sf_in, sf_ref), (sp_in, sp_ref)))
    ]
    for load in loads:
        load.start()
    barrier = pltpu.get_barrier_semaphore()

    def greet_dp(j, _):
        pl.semaphore_signal(barrier, inc=1, device_id={"dp": lax.rem(me + j, n_dp)}, device_id_type=MESH)
        return 0

    def greet_pr(j, _):
        pl.semaphore_signal(barrier, inc=1, device_id={"proto": lax.rem(mp + j, n_pr)}, device_id_type=MESH)
        return 0

    lax.fori_loop(1, n_dp, greet_dp, 0)
    lax.fori_loop(1, n_pr, greet_pr, 0)

    def norm_rows(b, _):
        r = pl.ds(pl.multiple_of(b * 128, 128), 128)
        th[r, :] = unit_rows(tf_ref[r, :])[0].astype(BF16)
        return 0

    def norm_student(b, _):
        r = pl.ds(pl.multiple_of(b * 128, 128), 128)
        unit = unit_rows(sf_ref[r, :])[0]
        sh[r, :] = unit.astype(BF16)
        turned = unit.T.astype(BF16)
        st[pl.ds(pl.multiple_of((1 - y) * part_rows, part_rows), part_rows), r] = turned[:part_rows]
        st[pl.ds(pl.multiple_of(y * part_rows, part_rows), part_rows), r] = turned[part_rows:2 * part_rows]
        st[2 * part_rows:, r] = turned[2 * part_rows:]
        return 0

    loads[0].wait()
    lax.fori_loop(0, blocks, norm_rows, 0)
    loads[1].wait()
    tiles = width // 128
    half_tiles = n_dp * tiles // 2

    def hops(j, n):
        return min(j, n - j)

    dp_peers = sorted(
        [(a, j) for a in range(2) for j in range(nz) if a or j],
        key=lambda o: -(o[0] + hops(o[1], nz)))
    pr_peers = sorted(
        [(i, b, c) for i in range(nx) for b in range(2) for c in range(2) if i or b or c],
        key=lambda o: -(2 * hops(o[0], nx) + 4 * o[1] + o[2]))

    def send_cols(rnd, hf):
        r = pl.ds(hf * half_tiles, half_tiles)
        for slot, (a, j) in enumerate(dp_peers):
            pltpu.make_async_remote_copy(
                src_ref=csend.at[rnd, r], dst_ref=crecv.at[rnd, hf, slot],
                send_sem=csend_sem.at[rnd, hf], recv_sem=crecv_sem.at[rnd, hf],
                device_id={"dp": lax.rem(y + a, 2) * nz + lax.rem(z + j, nz)}, device_id_type=MESH,
            ).start()

    def put_cols(rnd, k, sums):
        for t in range(tiles):
            csend[rnd, pl.ds(k * tiles + t, 1), :] = sums[:, t * 128:(t + 1) * 128]

    def teacher_unit(k):
        c = pl.ds(pl.multiple_of(k * width, width), width)
        return unit_cols(tp_ref[:, c])[0].astype(BF16)

    def first_cols(k, _):
        c = pl.ds(pl.multiple_of(k * width, width), width)
        wt = wts[lax.rem(k, 2)]
        wts[lax.rem(k + 1, 2)] = teacher_unit(jnp.minimum(k + 1, n_dp - 1))
        acc = jnp.zeros((8, width), F32)
        for m in range(rows // 256):
            r = pl.ds(m * 256, 256)
            logits = jnp.dot(th[r, :], wt, preferred_element_type=F32)
            e = jnp.exp2(logits * (LOG2E / TEACHER_TEMP))
            expo[r, c] = e
            acc = acc + jnp.sum(e.reshape(32, 8, width), axis=0)
        put_cols(0, k, jnp.sum(acc, axis=0, keepdims=True))
        return 0

    wts[0] = teacher_unit(0)
    lax.fori_loop(0, n_dp // 2, first_cols, 0, unroll=2)
    pl.semaphore_wait(barrier, n_dp + n_pr - 2)
    send_cols(0, 0)
    lax.fori_loop(n_dp // 2, n_dp, first_cols, 0, unroll=2)
    send_cols(0, 1)
    loads[2].wait()
    lax.fori_loop(0, blocks, norm_student, 0)
    loads[3].wait()

    part[...] = jnp.zeros_like(part)

    def student(lo, hi):
        def body(k, _):
            c = pl.ds(pl.multiple_of(k * width, width), width)
            ws = unit_cols(sp_ref[:, c])[0].astype(BF16)
            wsn[:, c] = ws
            for m in range(rows // 256):
                r = pl.ds(m * 256, 256)
                logits = jnp.dot(sh[r, :], ws, preferred_element_type=F32)
                e = jnp.exp2(logits * (LOG2E / STUDENT_TEMP))
                s = e[:, 0:128]
                for t in range(1, width // 128):
                    s = s + e[:, t * 128:(t + 1) * 128]
                part[r, :] += s
            return 0

        lax.fori_loop(lo, hi, body, 0)

    def receive_v(rnd, hf):
        wait_bytes(crecv.at[rnd, hf], crecv_sem.at[rnd, hf])
        v = 1.0 / (csend[rnd, pl.ds(hf * half_tiles, half_tiles), :] + jnp.sum(crecv[rnd, hf], axis=0))
        for t in range(half_tiles):
            lanes = slice((hf * half_tiles + t) * 128, (hf * half_tiles + t + 1) * 128)
            vb[:, lanes] = jnp.broadcast_to(v[t:t + 1, :], (8, 128))

    def lane_sums(slot, k, acc):
        rsend[slot, pl.ds(k, 1), :] = jnp.sum(acc.T, axis=0, keepdims=True)

    def send_rows(slot):
        for place, (i, b, c) in enumerate(pr_peers):
            pltpu.make_async_remote_copy(
                src_ref=rsend.at[slot], dst_ref=rrecv.at[slot, place],
                send_sem=rsend_sem.at[slot], recv_sem=rrecv_sem.at[slot],
                device_id=peer(lax.rem(x + i, nx), lax.rem(h + b, 2), lax.rem(core + c, 2)), device_id_type=MESH,
            ).start()

    def receive_rows(slot):
        wait_bytes(rrecv.at[slot], rrecv_sem.at[slot])
        return 1.0 / (rsend[slot] + jnp.sum(rrecv[slot], axis=0))

    def widen(u, out):
        for k in range(blocks):
            out[k * 128:(k + 1) * 128, :] = jnp.broadcast_to(u[k:k + 1, :], (128, 128)).T

    def row_pass(rnd, hf):
        def body(k, _):
            r = pl.ds(pl.multiple_of(k * 128, 128), 128)
            acc = racc[r, :].reshape(16, 8, 128) if hf else jnp.zeros((16, 8, 128), F32)
            for t in range(hf * half_tiles, (hf + 1) * half_tiles):
                e = expo[r, t * 128:(t + 1) * 128].reshape(16, 8, 128)
                acc = acc + e * vb[:, t * 128:(t + 1) * 128][None]
            if hf:
                lane_sums(rnd, k, acc.reshape(128, 128))
            else:
                racc[r, :] = acc.reshape(128, 128)
            return 0

        lax.fori_loop(0, blocks, body, 0)

    def col_pass(rnd, hf):
        def body(i, _):
            k = hf * (n_dp // 2) + i
            c = pl.ds(pl.multiple_of(k * width, width), width)

            def inner(b, acc):
                r = pl.ds(pl.multiple_of(b * 128, 128), 128)
                u = ub[r, :].reshape(16, 8, 128)
                e = expo[r, c].reshape(16, 8, width)
                new = [e[:, :, t * 128:(t + 1) * 128] * u for t in range(tiles)]
                return tuple(a + jnp.sum(n, axis=0) for a, n in zip(acc, new))

            acc = lax.fori_loop(0, blocks, inner, (jnp.zeros((8, 128), F32),) * tiles)
            put_cols(rnd, k, jnp.sum(jnp.concatenate(acc, axis=1), axis=0, keepdims=True))
            return 0

        lax.fori_loop(0, n_dp // 2, body, 0)

    def span(rel, hc):
        chunk = lax.rem(z + rel, nz)
        return pl.ds(pl.multiple_of((chunk * 2 + hc) * width, width), width)

    def place(b):
        q = b // 2
        far = nz // 2 - (q + 1) // 2
        return span(jnp.where(lax.rem(q, 2) == 1, far, nz - far), lax.rem(b, 2))

    def ready(b, _):
        ws = wsn[:, place(b)]
        for m in range(rows // 256):
            r = pl.ds(m * 256, 256)
            logits = jnp.dot(sh[r, :], ws, preferred_element_type=F32)
            e = jnp.exp2(logits * (LOG2E / STUDENT_TEMP)).reshape(32, 8, width)
            ps = pb[r, :].reshape(32, 8, 128)
            first[b, r, :] = jnp.concatenate(
                [e[:, :, t * 128:(t + 1) * 128] * ps for t in range(tiles)], axis=2).reshape(256, width)
        return 0

    share = n_dp // 4
    student(0, share)
    for rnd in range(ROUNDS):
        if rnd == 1:
            student(2 * share, 3 * share)
        receive_v(rnd, 0)
        row_pass(rnd, 0)
        receive_v(rnd, 1)
        row_pass(rnd, 1)
        send_rows(rnd)
        if rnd == 0:
            student(share, 2 * share)
        if rnd == 1:
            student(3 * share, 4 * share)

            def student_rows(k, _):
                lane_sums(ROUNDS, k, part[pl.ds(pl.multiple_of(k * 128, 128), 128), :])
                return 0

            lax.fori_loop(0, blocks, student_rows, 0)
            send_rows(ROUNDS)
        if rnd == ROUNDS - 1:
            widen(receive_rows(ROUNDS) * factor, pb)
            hat[...] = jnp.zeros_like(hat)
            lax.fori_loop(0, 2, ready, 0)
        u = receive_rows(rnd)
        if rnd < ROUNDS - 1:
            widen(u, ub)
            col_pass(rnd + 1, 0)
            send_cols(rnd + 1, 0)
            col_pass(rnd + 1, 1)
            send_cols(rnd + 1, 1)
        else:
            widen(u * factor, ub)
    def copy(src, dst, send, recv, to):
        return pltpu.make_async_remote_copy(
            src_ref=src, dst_ref=dst, send_sem=send, recv_sem=recv, device_id=to, device_id_type=MESH)

    def grad_block(b, _, made=False):
        c = place(b)
        ws = wsn[:, c]
        v = vb[:, c]
        for m in range(rows // 256):
            r = pl.ds(m * 256, 256)
            if made:
                e = first[b, r, :].reshape(32, 8, width)
            else:
                logits = jnp.dot(sh[r, :], ws, preferred_element_type=F32)
                e = jnp.exp2(logits * (LOG2E / STUDENT_TEMP)).reshape(32, 8, width)
            q = expo[r, c].reshape(32, 8, width)
            us = ub[r, :].reshape(32, 8, 128)
            ps = pb[r, :].reshape(32, 8, 128)
            g = []
            for t in range(tiles):
                lanes = slice(t * 128, (t + 1) * 128)
                p = e[:, :, lanes] if made else e[:, :, lanes] * ps
                g.append(p - q[:, :, lanes] * us * v[None, :, lanes])
            g = jnp.concatenate(g, axis=2).reshape(256, width).astype(BF16)
            gbuf[r, :] = g
            hat[r, :] += lax.dot_general(g, ws, (((1,), (1,)), ((), ())), preferred_element_type=F32)
        ubuf[b] = jnp.dot(st[...], gbuf[...], preferred_element_type=F32)
        copy(ubuf.at[b, pl.ds(0, part_rows)], yrecv.at[b], ysend_sem, yrecv_sem.at[b], other).start()
        return 0

    half_rows = rows // 2
    x_rows = half_rows // nx

    mine = pl.multiple_of(core * half_rows, half_rows)
    theirs = pl.multiple_of((1 - core) * half_rows, half_rows)

    def x_start(xx):
        return pl.multiple_of(xx * x_rows, x_rows)

    def hat_1():
        copy(hat.at[pl.ds(theirs, half_rows)], h1, hsend_sem.at[0], hrecv_sem.at[0], peer(x, h, 1 - core)).start()

    def hat_2():
        wait_bytes(h1, hrecv_sem.at[0])
        hat[pl.ds(mine, half_rows), :] += h1[...]
        for j in range(1, nx):
            to = lax.rem(x + j, nx)
            copy(hat.at[pl.ds(mine + x_start(to), x_rows)], h2.at[j - 1], hsend_sem.at[1], hrecv_sem.at[1],
                 peer(to, h, core)).start()

    def hat_3():
        wait_bytes(h2, hrecv_sem.at[1])
        h3[0] = hat[pl.ds(mine + x_start(x), x_rows), :] + jnp.sum(h2[...], axis=0)
        copy(h3.at[0], h3.at[1], hsend_sem.at[2], hrecv_sem.at[2], peer(x, 1 - h, core)).start()

    def hat_4():
        wait_bytes(h3.at[1], hrecv_sem.at[2])
        r = pl.ds(mine + x_start(x), x_rows)
        grad = h3[0] + h3[1]
        unit, norm = unit_rows(sf_ref[r, :])
        fg_ref[r, :] = (grad - unit * jnp.sum(unit * grad, axis=1, keepdims=True)) / norm
        for j in range(1, nx):
            copy(fg_ref.at[r], fg_ref.at[r], hsend_sem.at[3], hrecv_sem.at[3], peer(lax.rem(x + j, nx), h, core)).start()

    def hat_5():
        wait_bytes(h2, hrecv_sem.at[3])
        r = pl.ds(mine, half_rows)
        copy(fg_ref.at[r], fg_ref.at[r], hsend_sem.at[4], hrecv_sem.at[4], peer(x, h, 1 - core)).start()

    def hat_6():
        wait_bytes(h1, hrecv_sem.at[4])

    def piece_rows(p):
        return pl.ds((p + 1) * part_rows, part_rows)

    top = nz // 2

    def arrive(q, hc, p):
        b = 2 * q + hc
        block = ubuf[b, piece_rows(p)]
        if p == 0:
            wait_bytes(yrecv.at[b], yrecv_sem.at[b])
            block = block + yrecv[b]
        return block

    def landed(turn, t, hc, p):
        wait_bytes(zrecv.at[turn, t, hc, p], zrecv_sem.at[turn, t, hc, p])
        return zrecv[turn, t, hc, p]

    def ring(t, pieces, same=(True, False)):
        for p in pieces:
            for hc in range(2):
                for turn in range(2):
                    if (hc == turn) not in same or (t == 0 and hc != turn):
                        continue
                    q = 2 * t - 1 + turn if t else 0
                    b = 2 * q + hc
                    block = arrive(q, hc, p)
                    if t > 1 or (t == 1 and hc == turn):
                        block = block + landed(turn, t - 1, hc, p)
                    ubuf[b, piece_rows(p)] = block
                    copy(ubuf.at[b, piece_rows(p)], zrecv.at[turn, t, hc, p],
                         zsend_sem.at[turn, min(t, 1)], zrecv_sem.at[turn, t, hc, p], sides[turn]).start()

    def pass_on(t, turn, hc, p):
        if t == top - 1 and hc != turn:
            return
        src = 2 * t - 1 + turn if t else 0
        dst = min(2 * t + 1 + turn, nz - 1)
        r = piece_rows(p)
        copy(gat.at[src, hc, r], gat.at[dst, hc, r], gzsend_sem.at[turn, min(top - 1 - t, 1)],
             gzrecv_sem.at[dst, hc, p], sides[turn]).start()

    def hand_over(slot, hc):
        copy(gat.at[slot, hc, piece_rows(0)], gat.at[slot, hc, pl.ds(0, part_rows)],
             gysend_sem, gyrecv_sem.at[slot, hc], other).start()

    lax.fori_loop(0, 2, functools.partial(grad_block, made=True), 0)
    ring(0, (1, 2))
    lax.fori_loop(2, 6, grad_block, 0)
    ring(0, (0,))
    ring(1, (1, 2), (False,))
    for t in range(1, top):
        if t == 1:
            ring(t, (1, 2), (True,))
            ring(t, (0,))
        else:
            ring(t, (1, 2, 0))
        if t < top - 1:
            lax.fori_loop(4 * t + 2, 4 * t + (6 if t < top - 2 else 8), grad_block, 0)
    own = 2 * nz - 2
    hat_1()
    for p in range(1, 3):
        for hc in range(2):
            block = arrive(nz - 1, hc, p)
            ubuf[own + hc, piece_rows(p)] = block + landed(0, top - 1, hc, p) + landed(1, top - 1, hc, p)
            copy(ubuf.at[own + hc, piece_rows(p)], brecv.at[hc, p - 1], bsend_sem, brecv_sem.at[hc, p - 1], other).start()
    for hc in range(2):
        gat[0, hc, piece_rows(0)] = arrive(nz - 1, hc, 0) + landed(0, top - 1, hc, 0) + landed(1, top - 1, hc, 0)
        for turn in range(2):
            pass_on(0, turn, hc, 0)
        hand_over(0, hc)
    hat_2()
    for p in range(1, 3):
        for hc in range(2):
            wait_bytes(brecv.at[hc, p - 1], brecv_sem.at[hc, p - 1])
            gat[0, hc, piece_rows(p)] = ubuf[own + hc, piece_rows(p)] + brecv[hc, p - 1]
            for turn in range(2):
                pass_on(0, turn, hc, p)

    wait_bytes(yrecv, ysend_sem)
    for turn in range(2):
        wait_bytes(zrecv.at[turn, 0, turn], zsend_sem.at[turn, 0])
        wait_bytes(zrecv.at[turn, pl.ds(1, top - 1)], zsend_sem.at[turn, 1])
    wait_bytes(brecv, bsend_sem)
    low = pl.ds(pl.multiple_of(y * part_rows, part_rows), part_rows)
    high = pl.ds(pl.multiple_of((1 - y) * part_rows, part_rows), part_rows)
    rest = pl.ds(2 * part_rows, 2 * part_rows)

    def finish(b, _):
        slot = b // 2
        hc = lax.rem(b, 2)
        far = (slot + 1) // 2
        c = span(jnp.where(lax.rem(slot, 2) == 1, nz - far, far), hc)
        wait_bytes(gat.at[slot, hc, pl.ds(0, part_rows)], gyrecv_sem.at[slot, hc])
        places = ((low, pl.ds(part_rows, part_rows)), (high, pl.ds(0, part_rows)), (rest, rest))
        wide = [sp_ref[here, c].astype(F32) for here, _ in places]
        square = sum(jnp.sum(w * w, axis=0, keepdims=True) for w in wide)
        inverse = 1.0 / jnp.sqrt(square + EPS)
        units = [w * inverse for w in wide]
        grads = [gat[slot, hc, there] for _, there in places]
        along = sum(jnp.sum(u * g, axis=0, keepdims=True) for u, g in zip(units, grads))
        for (here, _), u, g in zip(places, units, grads):
            pg_ref[here, c] = (g - u * along) * inverse
        return 0

    hat_3()
    later = {0: hat_4, 1: hat_5, 2: hat_6}
    for t in range(top):
        for p in range(3):
            for hc in range(2):
                for turn in range(2):
                    if t == top - 1 and hc != turn:
                        continue
                    slot = min(2 * t + 1 + turn, nz - 1)
                    wait_bytes(gat.at[slot, hc, piece_rows(p)], gzrecv_sem.at[slot, hc, p])
                    if t < top - 1:
                        pass_on(t + 1, turn, hc, p)
                    if p == 0:
                        hand_over(slot, hc)
        if t == 0:
            lax.fori_loop(0, 2, finish, 0)
        else:
            lax.fori_loop(4 * t - 2, 4 * t + 2, finish, 0)
        if t in later:
            later[t]()
    lax.fori_loop(2 * nz - 2, 2 * nz, finish, 0)

    for turn in range(2):
        wait_bytes(zrecv.at[turn, 0, turn], gzsend_sem.at[turn, 0])
        wait_bytes(zrecv.at[turn, pl.ds(1, top - 1)], gzsend_sem.at[turn, 1])
    wait_bytes(yrecv, gysend_sem)
    wait_bytes(h1, hsend_sem.at[0])
    wait_bytes(h2, hsend_sem.at[1])
    wait_bytes(h3.at[1], hsend_sem.at[2])
    wait_bytes(h2, hsend_sem.at[3])
    wait_bytes(h1, hsend_sem.at[4])
    for rnd in range(ROUNDS):
        for hf in range(2):
            wait_bytes(crecv.at[rnd, hf], csend_sem.at[rnd, hf])
    for slot in range(ROUNDS + 1):
        wait_bytes(rrecv.at[slot], rsend_sem.at[slot])


def fused(n_dp, n_pr, sf, tf, sp, tp):
    rows, dim = sf.shape
    cols = tp.shape[1]
    width = cols // n_dp
    blocks = rows // 128
    nz, nx = n_dp // 2, n_pr // 4
    quarter = dim // 4
    vmem = pl.BlockSpec(memory_space=pltpu.VMEM)
    anywhere = pl.BlockSpec(memory_space=pl.ANY)
    dma = pltpu.SemaphoreType.DMA
    return pl.pallas_call(
        functools.partial(kernel, n_dp, n_pr),
        out_shape=(
            pltpu.VMEM((dim, cols), F32),
            pltpu.VMEM((rows, dim), F32),
        ),
        in_specs=[anywhere] * 4,
        out_specs=[vmem] * 2,
        scratch_shapes=[
            pltpu.VMEM((rows, dim), BF16),
            pltpu.VMEM((rows, dim), BF16),
            pltpu.VMEM((dim, cols), BF16),
            pltpu.VMEM((dim, cols), BF16),
            pltpu.VMEM((2, dim, width), BF16),
            pltpu.VMEM((rows, cols), F32),
            pltpu.VMEM((rows, dim), BF16),
            pltpu.VMEM((rows, dim), BF16),
            pltpu.VMEM((rows, 128), F32),
            pltpu.VMEM((8, cols), F32),
            pltpu.VMEM((rows, 128), F32),
            pltpu.VMEM((rows, 128), F32),
            pltpu.VMEM((2, rows, width), F32),
            pltpu.VMEM((ROUNDS, cols // 128, 128), F32),
            pltpu.VMEM((ROUNDS, 2, n_dp - 1, cols // 256, 128), F32),
            pltpu.VMEM((ROUNDS + 1, blocks, 128), F32),
            pltpu.VMEM((ROUNDS + 1, n_pr - 1, blocks, 128), F32),
            pltpu.VMEM((dim, rows), BF16),
            pltpu.VMEM((dim, cols), BF16),
            pltpu.VMEM((rows, 128), F32),
            pltpu.VMEM((rows, width), BF16),
            pltpu.VMEM((rows, dim), F32),
            pltpu.VMEM((n_dp, dim, width), F32),
            pltpu.VMEM((n_dp, quarter, width), F32),
            pltpu.VMEM((2, nz // 2, 2, 3, quarter, width), F32),
            pltpu.VMEM((2, 2, quarter, width), F32),
            pltpu.VMEM((nz, 2, dim, width), F32),
            pltpu.VMEM((rows // 2, dim), F32),
            pltpu.VMEM((nx - 1, rows // 2 // nx, dim), F32),
            pltpu.VMEM((2, rows // 2 // nx, dim), F32),
            dma((ROUNDS, 2)), dma((ROUNDS, 2)),
            dma((ROUNDS + 1,)), dma((ROUNDS + 1,)),
            dma, dma((n_dp,)), dma((2, 2)), dma((2, nz // 2, 2, 3)), dma, dma((2, 2)),
            dma((2, 2)), dma((nz, 2, 3)), dma, dma((nz, 2)), dma((5,)), dma((5,)), dma((4,)),
        ],
        compiler_params=pltpu.CompilerParams(
            collective_id=0, has_side_effects=True, vmem_limit_bytes=56 * 1024 * 1024
        ),
    )(sf, tf, sp, tp)


def solution(mesh):
    in_specs = (P("dp", None), P("dp", None), P(None, "proto"), P(None, "proto"))
    out_specs = (P(None, "proto"), P("dp", None))
    return jax.shard_map(
        functools.partial(fused, mesh.shape["dp"], mesh.shape["proto"]),
        mesh=mesh, in_specs=in_specs, out_specs=out_specs, check_vma=False,
    )
```

```python
import functools
import math

import jax
import jax.numpy as jnp
from jax import lax
from jax.experimental import pallas as pl
from jax.experimental.pallas import tpu as pltpu
from jax.sharding import PartitionSpec as P

PROTOS = 65536
ROUNDS = 3
EPS = 1e-06
TEACHER_TEMP = 0.07
STUDENT_TEMP = 0.1
LOG2E = 1.4426950408889634
MESH = pl.DeviceIdType.MESH
F32 = jnp.float32
BF16 = jnp.bfloat16


def unit_rows(values):
    wide = values.astype(F32)
    norms = jnp.sqrt(jnp.sum(wide * wide, axis=1, keepdims=True) + EPS)
    return (wide * (1.0 / norms), norms)


def unit_cols(values):
    wide = values.astype(F32)
    norms = jnp.sqrt(jnp.sum(wide * wide, axis=0, keepdims=True) + EPS)
    return (wide * (1.0 / norms), norms)


def wait_bytes(ref, sem):
    pltpu.make_async_copy(ref, ref, sem).wait()


def kernel(
    n_dp, n_pr,
    sf_in, tf_in, sp_in, tp_in,
    pg_ref, fg_ref,
    sf_ref, tf_ref, sp_ref, tp_ref, wts,
    expo, th, sh, part, vb, ub, racc, first,
    csend, crecv, rsend, rrecv,
    st, wsn, pb, gbuf, hat, ubuf, yrecv, zrecv, brecv, gat, h1, h2, h3,
    csend_sem, crecv_sem, rsend_sem, rrecv_sem,
    ysend_sem, yrecv_sem, zsend_sem, zrecv_sem, bsend_sem, brecv_sem,
    gzsend_sem, gzrecv_sem, gysend_sem, gyrecv_sem, hsend_sem, hrecv_sem, in_sem,
):
    rows, dim = sf_ref.shape
    cols = tp_ref.shape[1]
    me = lax.axis_index("dp")
    mp = lax.axis_index("proto")
    width = cols // n_dp
    blocks = rows // 128
    nz = n_dp // 2
    y, z = me // nz, lax.rem(me, nz)
    other = {"dp": (1 - y) * nz + z}
    sides = ({"dp": y * nz + lax.rem(z + 1, nz)}, {"dp": y * nz + lax.rem(z + nz - 1, nz)})
    part_rows = dim // 4
    core, h, x = lax.rem(mp, 2), lax.rem(mp // 2, 2), mp // 4
    nx = n_pr // 4
    factor = PROTOS / math.sqrt(rows * n_dp) / STUDENT_TEMP

    def peer(nx_, nh, ncore):
        return {"proto": (nx_ * 2 + nh) * 2 + ncore}

    loads = [
        pltpu.make_async_copy(src, dst, in_sem.at[k])
        for k, (src, dst) in enumerate(((tf_in, tf_ref), (tp_in, tp_ref), (sf_in, sf_ref), (sp_in, sp_ref)))
    ]
    for load in loads:
        load.start()
    barrier = pltpu.get_barrier_semaphore()

    def greet_dp(j, _):
        pl.semaphore_signal(barrier, inc=1, device_id={"dp": lax.rem(me + j, n_dp)}, device_id_type=MESH)
        return 0

    def greet_pr(j, _):
        pl.semaphore_signal(barrier, inc=1, device_id={"proto": lax.rem(mp + j, n_pr)}, device_id_type=MESH)
        return 0

    lax.fori_loop(1, n_dp, greet_dp, 0)
    lax.fori_loop(1, n_pr, greet_pr, 0)

    def norm_rows(b, _):
        r = pl.ds(pl.multiple_of(b * 128, 128), 128)
        th[r, :] = unit_rows(tf_ref[r, :])[0].astype(BF16)
        return 0

    def norm_student(b, _):
        r = pl.ds(pl.multiple_of(b * 128, 128), 128)
        unit = unit_rows(sf_ref[r, :])[0]
        sh[r, :] = unit.astype(BF16)
        turned = unit.T.astype(BF16)
        st[pl.ds(pl.multiple_of((1 - y) * part_rows, part_rows), part_rows), r] = turned[:part_rows]
        st[pl.ds(pl.multiple_of(y * part_rows, part_rows), part_rows), r] = turned[part_rows:2 * part_rows]
        st[2 * part_rows:, r] = turned[2 * part_rows:]
        return 0

    loads[0].wait()
    lax.fori_loop(0, blocks, norm_rows, 0)
    loads[1].wait()
    tiles = width // 128
    half_tiles = n_dp * tiles // 2

    def hops(j, n):
        return min(j, n - j)

    dp_peers = sorted(
        [(a, j) for a in range(2) for j in range(nz) if a or j],
        key=lambda o: -(o[0] + hops(o[1], nz)))
    pr_peers = sorted(
        [(i, b, c) for i in range(nx) for b in range(2) for c in range(2) if i or b or c],
        key=lambda o: -(2 * hops(o[0], nx) + 4 * o[1] + o[2]))

    def send_cols(rnd, hf):
        r = pl.ds(hf * half_tiles, half_tiles)
        for slot, (a, j) in enumerate(dp_peers):
            pltpu.make_async_remote_copy(
                src_ref=csend.at[rnd, r], dst_ref=crecv.at[rnd, hf, slot],
                send_sem=csend_sem.at[rnd, hf], recv_sem=crecv_sem.at[rnd, hf],
                device_id={"dp": lax.rem(y + a, 2) * nz + lax.rem(z + j, nz)}, device_id_type=MESH,
            ).start()

    def put_cols(rnd, k, sums):
        for t in range(tiles):
            csend[rnd, pl.ds(k * tiles + t, 1), :] = sums[:, t * 128:(t + 1) * 128]

    def teacher_unit(k):
        c = pl.ds(pl.multiple_of(k * width, width), width)
        return unit_cols(tp_ref[:, c])[0].astype(BF16)

    def first_cols(k, _):
        c = pl.ds(pl.multiple_of(k * width, width), width)
        wt = wts[lax.rem(k, 2)]
        wts[lax.rem(k + 1, 2)] = teacher_unit(jnp.minimum(k + 1, n_dp - 1))
        acc = jnp.zeros((8, width), F32)
        for m in range(rows // 256):
            r = pl.ds(m * 256, 256)
            logits = jnp.dot(th[r, :], wt, preferred_element_type=F32)
            e = jnp.exp2(logits * (LOG2E / TEACHER_TEMP))
            expo[r, c] = e
            acc = acc + jnp.sum(e.reshape(32, 8, width), axis=0)
        put_cols(0, k, jnp.sum(acc, axis=0, keepdims=True))
        return 0

    wts[0] = teacher_unit(0)
    lax.fori_loop(0, n_dp // 2, first_cols, 0, unroll=4)
    pl.semaphore_wait(barrier, n_dp + n_pr - 2)
    send_cols(0, 0)
    lax.fori_loop(n_dp // 2, n_dp, first_cols, 0, unroll=4)
    send_cols(0, 1)
    loads[2].wait()
    lax.fori_loop(0, blocks, norm_student, 0)
    loads[3].wait()

    part[...] = jnp.zeros_like(part)

    def student(lo, hi):
        def body(k, _):
            c = pl.ds(pl.multiple_of(k * width, width), width)
            ws = unit_cols(sp_ref[:, c])[0].astype(BF16)
            wsn[:, c] = ws
            for m in range(rows // 256):
                r = pl.ds(m * 256, 256)
                logits = jnp.dot(sh[r, :], ws, preferred_element_type=F32)
                e = jnp.exp2(logits * (LOG2E / STUDENT_TEMP))
                s = e[:, 0:128]
                for t in range(1, width // 128):
                    s = s + e[:, t * 128:(t + 1) * 128]
                part[r, :] += s
            return 0

        lax.fori_loop(lo, hi, body, 0)

    def receive_v(rnd, hf):
        wait_bytes(crecv.at[rnd, hf], crecv_sem.at[rnd, hf])
        v = 1.0 / (csend[rnd, pl.ds(hf * half_tiles, half_tiles), :] + jnp.sum(crecv[rnd, hf], axis=0))
        for t in range(half_tiles):
            lanes = slice((hf * half_tiles + t) * 128, (hf * half_tiles + t + 1) * 128)
            vb[:, lanes] = jnp.broadcast_to(v[t:t + 1, :], (8, 128))

    def lane_sums(slot, acc):
        for k in range(blocks):
            turned = acc[k * 128:(k + 1) * 128, :].T
            rsend[slot, k:k + 1, :] = jnp.sum(turned, axis=0, keepdims=True)

    def send_rows(slot):
        for place, (i, b, c) in enumerate(pr_peers):
            pltpu.make_async_remote_copy(
                src_ref=rsend.at[slot], dst_ref=rrecv.at[slot, place],
                send_sem=rsend_sem.at[slot], recv_sem=rrecv_sem.at[slot],
                device_id=peer(lax.rem(x + i, nx), lax.rem(h + b, 2), lax.rem(core + c, 2)), device_id_type=MESH,
            ).start()

    def receive_rows(slot):
        wait_bytes(rrecv.at[slot], rrecv_sem.at[slot])
        return 1.0 / (rsend[slot] + jnp.sum(rrecv[slot], axis=0))

    def widen(u, out):
        for k in range(blocks):
            out[k * 128:(k + 1) * 128, :] = jnp.broadcast_to(u[k:k + 1, :], (128, 128)).T

    def row_pass(rnd, hf):
        def body(k, _):
            r = pl.ds(pl.multiple_of(k * 128, 128), 128)
            acc = racc[r, :].reshape(16, 8, 128) if hf else jnp.zeros((16, 8, 128), F32)
            for t in range(hf * half_tiles, (hf + 1) * half_tiles):
                e = expo[r, t * 128:(t + 1) * 128].reshape(16, 8, 128)
                acc = acc + e * vb[:, t * 128:(t + 1) * 128][None]
            racc[r, :] = acc.reshape(128, 128)
            return 0

        lax.fori_loop(0, blocks, body, 0)
        if hf:
            lane_sums(rnd, racc)

    def col_pass(rnd, hf):
        def body(i, _):
            k = hf * (n_dp // 2) + i
            c = pl.ds(pl.multiple_of(k * width, width), width)

            def inner(b, acc):
                r = pl.ds(pl.multiple_of(b * 128, 128), 128)
                u = ub[r, :].reshape(16, 8, 128)
                e = expo[r, c].reshape(16, 8, width)
                new = [e[:, :, t * 128:(t + 1) * 128] * u for t in range(tiles)]
                return tuple(a + jnp.sum(n, axis=0) for a, n in zip(acc, new))

            acc = lax.fori_loop(0, blocks, inner, (jnp.zeros((8, 128), F32),) * tiles)
            put_cols(rnd, k, jnp.sum(jnp.concatenate(acc, axis=1), axis=0, keepdims=True))
            return 0

        lax.fori_loop(0, n_dp // 2, body, 0)

    def span(rel, hc):
        chunk = lax.rem(z + rel, nz)
        return pl.ds(pl.multiple_of((chunk * 2 + hc) * width, width), width)

    def place(b):
        q = b // 2
        far = nz // 2 - (q + 1) // 2
        return span(jnp.where(lax.rem(q, 2) == 1, far, nz - far), lax.rem(b, 2))

    def ready(b, _):
        ws = wsn[:, place(b)]
        for m in range(rows // 256):
            r = pl.ds(m * 256, 256)
            logits = jnp.dot(sh[r, :], ws, preferred_element_type=F32)
            e = jnp.exp2(logits * (LOG2E / STUDENT_TEMP)).reshape(32, 8, width)
            ps = pb[r, :].reshape(32, 8, 128)
            first[b, r, :] = jnp.concatenate(
                [e[:, :, t * 128:(t + 1) * 128] * ps for t in range(tiles)], axis=2).reshape(256, width)
        return 0

    share = n_dp // 4
    student(0, share)
    for rnd in range(ROUNDS):
        if rnd == 1:
            student(2 * share, 3 * share)
        receive_v(rnd, 0)
        row_pass(rnd, 0)
        receive_v(rnd, 1)
        row_pass(rnd, 1)
        send_rows(rnd)
        if rnd == 0:
            student(share, 2 * share)
        if rnd == 1:
            student(3 * share, 4 * share)

            lane_sums(ROUNDS, part)
            send_rows(ROUNDS)
        if rnd == ROUNDS - 1:
            widen(receive_rows(ROUNDS) * factor, pb)
            hat[...] = jnp.zeros_like(hat)
            lax.fori_loop(0, 2, ready, 0)
        u = receive_rows(rnd)
        if rnd < ROUNDS - 1:
            widen(u, ub)
            col_pass(rnd + 1, 0)
            send_cols(rnd + 1, 0)
            col_pass(rnd + 1, 1)
            send_cols(rnd + 1, 1)
        else:
            widen(u * factor, ub)
    def copy(src, dst, send, recv, to):
        return pltpu.make_async_remote_copy(
            src_ref=src, dst_ref=dst, send_sem=send, recv_sem=recv, device_id=to, device_id_type=MESH)

    def grad_block(b, _, made=False):
        c = place(b)
        ws = wsn[:, c]
        v = vb[:, c]
        for m in range(rows // 256):
            r = pl.ds(m * 256, 256)
            if made:
                e = first[b, r, :].reshape(32, 8, width)
            else:
                logits = jnp.dot(sh[r, :], ws, preferred_element_type=F32)
                e = jnp.exp2(logits * (LOG2E / STUDENT_TEMP)).reshape(32, 8, width)
            q = expo[r, c].reshape(32, 8, width)
            us = ub[r, :].reshape(32, 8, 128)
            ps = pb[r, :].reshape(32, 8, 128)
            g = []
            for t in range(tiles):
                lanes = slice(t * 128, (t + 1) * 128)
                p = e[:, :, lanes] if made else e[:, :, lanes] * ps
                g.append(p - q[:, :, lanes] * us * v[None, :, lanes])
            g = jnp.concatenate(g, axis=2).reshape(256, width).astype(BF16)
            gbuf[r, :] = g
            hat[r, :] += lax.dot_general(g, ws, (((1,), (1,)), ((), ())), preferred_element_type=F32)
        ubuf[b] = jnp.dot(st[...], gbuf[...], preferred_element_type=F32)
        copy(ubuf.at[b, pl.ds(0, part_rows)], yrecv.at[b], ysend_sem, yrecv_sem.at[b], other).start()
        return 0

    half_rows = rows // 2
    x_rows = half_rows // nx

    mine = pl.multiple_of(core * half_rows, half_rows)
    theirs = pl.multiple_of((1 - core) * half_rows, half_rows)

    def x_start(xx):
        return pl.multiple_of(xx * x_rows, x_rows)

    def hat_1():
        copy(hat.at[pl.ds(theirs, half_rows)], h1, hsend_sem.at[0], hrecv_sem.at[0], peer(x, h, 1 - core)).start()

    def hat_2():
        wait_bytes(h1, hrecv_sem.at[0])
        hat[pl.ds(mine, half_rows), :] += h1[...]
        for j in range(1, nx):
            to = lax.rem(x + j, nx)
            copy(hat.at[pl.ds(mine + x_start(to), x_rows)], h2.at[j - 1], hsend_sem.at[1], hrecv_sem.at[1],
                 peer(to, h, core)).start()

    def hat_3():
        wait_bytes(h2, hrecv_sem.at[1])
        h3[0] = hat[pl.ds(mine + x_start(x), x_rows), :] + jnp.sum(h2[...], axis=0)
        copy(h3.at[0], h3.at[1], hsend_sem.at[2], hrecv_sem.at[2], peer(x, 1 - h, core)).start()

    def hat_4():
        wait_bytes(h3.at[1], hrecv_sem.at[2])
        r = pl.ds(mine + x_start(x), x_rows)
        grad = h3[0] + h3[1]
        unit, norm = unit_rows(sf_ref[r, :])
        fg_ref[r, :] = (grad - unit * jnp.sum(unit * grad, axis=1, keepdims=True)) / norm
        for j in range(1, nx):
            copy(fg_ref.at[r], fg_ref.at[r], hsend_sem.at[3], hrecv_sem.at[3], peer(lax.rem(x + j, nx), h, core)).start()

    def hat_5():
        wait_bytes(h2, hrecv_sem.at[3])
        r = pl.ds(mine, half_rows)
        copy(fg_ref.at[r], fg_ref.at[r], hsend_sem.at[4], hrecv_sem.at[4], peer(x, h, 1 - core)).start()

    def hat_6():
        wait_bytes(h1, hrecv_sem.at[4])

    def piece_rows(p):
        return pl.ds((p + 1) * part_rows, part_rows)

    top = nz // 2

    def arrive(q, hc, p):
        b = 2 * q + hc
        block = ubuf[b, piece_rows(p)]
        if p == 0:
            wait_bytes(yrecv.at[b], yrecv_sem.at[b])
            block = block + yrecv[b]
        return block

    def landed(turn, t, hc, p):
        wait_bytes(zrecv.at[turn, t, hc, p], zrecv_sem.at[turn, t, hc, p])
        return zrecv[turn, t, hc, p]

    def ring(t, pieces, same=(True, False)):
        for p in pieces:
            for hc in range(2):
                for turn in range(2):
                    if (hc == turn) not in same or (t == 0 and hc != turn):
                        continue
                    q = 2 * t - 1 + turn if t else 0
                    b = 2 * q + hc
                    block = arrive(q, hc, p)
                    if t > 1 or (t == 1 and hc == turn):
                        block = block + landed(turn, t - 1, hc, p)
                    ubuf[b, piece_rows(p)] = block
                    copy(ubuf.at[b, piece_rows(p)], zrecv.at[turn, t, hc, p],
                         zsend_sem.at[turn, min(t, 1)], zrecv_sem.at[turn, t, hc, p], sides[turn]).start()

    def pass_on(t, turn, hc, p):
        if t == top - 1 and hc != turn:
            return
        src = 2 * t - 1 + turn if t else 0
        dst = min(2 * t + 1 + turn, nz - 1)
        r = piece_rows(p)
        copy(gat.at[src, hc, r], gat.at[dst, hc, r], gzsend_sem.at[turn, min(top - 1 - t, 1)],
             gzrecv_sem.at[dst, hc, p], sides[turn]).start()

    def hand_over(slot, hc):
        copy(gat.at[slot, hc, piece_rows(0)], gat.at[slot, hc, pl.ds(0, part_rows)],
             gysend_sem, gyrecv_sem.at[slot, hc], other).start()

    lax.fori_loop(0, 2, functools.partial(grad_block, made=True), 0)
    ring(0, (1, 2))
    lax.fori_loop(2, 6, grad_block, 0)
    ring(0, (0,))
    ring(1, (1, 2), (False,))
    for t in range(1, top):
        if t == 1:
            ring(t, (1, 2), (True,))
            ring(t, (0,))
        else:
            ring(t, (1, 2, 0) if t < top - 1 else (1, 0, 2))
        if t < top - 1:
            lax.fori_loop(4 * t + 2, 4 * t + (6 if t < top - 2 else 8), grad_block, 0)
        if t == top - 2:
            hat_1()
    own = 2 * nz - 2

    def trade(p):
        for hc in range(2):
            block = arrive(nz - 1, hc, p)
            ubuf[own + hc, piece_rows(p)] = block + landed(0, top - 1, hc, p) + landed(1, top - 1, hc, p)
            copy(ubuf.at[own + hc, piece_rows(p)], brecv.at[hc, p - 1], bsend_sem, brecv_sem.at[hc, p - 1], other).start()

    def traded(p):
        for hc in range(2):
            wait_bytes(brecv.at[hc, p - 1], brecv_sem.at[hc, p - 1])
            gat[0, hc, piece_rows(p)] = ubuf[own + hc, piece_rows(p)] + brecv[hc, p - 1]
            for turn in range(2):
                pass_on(0, turn, hc, p)

    trade(1)
    for hc in range(2):
        gat[0, hc, piece_rows(0)] = arrive(nz - 1, hc, 0) + landed(0, top - 1, hc, 0) + landed(1, top - 1, hc, 0)
        for turn in range(2):
            pass_on(0, turn, hc, 0)
        hand_over(0, hc)
    traded(1)
    trade(2)
    hat_2()
    traded(2)

    wait_bytes(yrecv, ysend_sem)
    for turn in range(2):
        wait_bytes(zrecv.at[turn, 0, turn], zsend_sem.at[turn, 0])
        wait_bytes(zrecv.at[turn, pl.ds(1, top - 1)], zsend_sem.at[turn, 1])
    wait_bytes(brecv, bsend_sem)
    low = pl.ds(pl.multiple_of(y * part_rows, part_rows), part_rows)
    high = pl.ds(pl.multiple_of((1 - y) * part_rows, part_rows), part_rows)
    rest = pl.ds(2 * part_rows, 2 * part_rows)

    def finish(b, _):
        slot = b // 2
        hc = lax.rem(b, 2)
        far = (slot + 1) // 2
        c = span(jnp.where(lax.rem(slot, 2) == 1, nz - far, far), hc)
        wait_bytes(gat.at[slot, hc, pl.ds(0, part_rows)], gyrecv_sem.at[slot, hc])
        places = ((low, pl.ds(part_rows, part_rows)), (high, pl.ds(0, part_rows)), (rest, rest))
        wide = [sp_ref[here, c].astype(F32) for here, _ in places]
        square = sum(jnp.sum(w * w, axis=0, keepdims=True) for w in wide)
        inverse = 1.0 / jnp.sqrt(square + EPS)
        units = [w * inverse for w in wide]
        grads = [gat[slot, hc, there] for _, there in places]
        along = sum(jnp.sum(u * g, axis=0, keepdims=True) for u, g in zip(units, grads))
        for (here, _), u, g in zip(places, units, grads):
            pg_ref[here, c] = (g - u * along) * inverse
        return 0

    hat_3()
    later = {0: hat_4, 1: hat_5, 2: hat_6}
    for t in range(top):
        for p in range(3):
            for hc in range(2):
                for turn in range(2):
                    if t == top - 1 and hc != turn:
                        continue
                    slot = min(2 * t + 1 + turn, nz - 1)
                    wait_bytes(gat.at[slot, hc, piece_rows(p)], gzrecv_sem.at[slot, hc, p])
                    if t < top - 1:
                        pass_on(t + 1, turn, hc, p)
                    if p == 0:
                        hand_over(slot, hc)
        if t == 0:
            lax.fori_loop(0, 2, finish, 0)
        else:
            lax.fori_loop(4 * t - 2, 4 * t + 2, finish, 0)
        if t in later:
            later[t]()
    lax.fori_loop(2 * nz - 2, 2 * nz, finish, 0)

    for turn in range(2):
        wait_bytes(zrecv.at[turn, 0, turn], gzsend_sem.at[turn, 0])
        wait_bytes(zrecv.at[turn, pl.ds(1, top - 1)], gzsend_sem.at[turn, 1])
    wait_bytes(yrecv, gysend_sem)
    wait_bytes(h1, hsend_sem.at[0])
    wait_bytes(h2, hsend_sem.at[1])
    wait_bytes(h3.at[1], hsend_sem.at[2])
    wait_bytes(h2, hsend_sem.at[3])
    wait_bytes(h1, hsend_sem.at[4])
    for rnd in range(ROUNDS):
        for hf in range(2):
            wait_bytes(crecv.at[rnd, hf], csend_sem.at[rnd, hf])
    for slot in range(ROUNDS + 1):
        wait_bytes(rrecv.at[slot], rsend_sem.at[slot])


def fused(n_dp, n_pr, sf, tf, sp, tp):
    rows, dim = sf.shape
    cols = tp.shape[1]
    width = cols // n_dp
    blocks = rows // 128
    nz, nx = n_dp // 2, n_pr // 4
    quarter = dim // 4
    vmem = pl.BlockSpec(memory_space=pltpu.VMEM)
    anywhere = pl.BlockSpec(memory_space=pl.ANY)
    dma = pltpu.SemaphoreType.DMA
    return pl.pallas_call(
        functools.partial(kernel, n_dp, n_pr),
        out_shape=(
            pltpu.VMEM((dim, cols), F32),
            pltpu.VMEM((rows, dim), F32),
        ),
        in_specs=[anywhere] * 4,
        out_specs=[vmem] * 2,
        scratch_shapes=[
            pltpu.VMEM((rows, dim), BF16),
            pltpu.VMEM((rows, dim), BF16),
            pltpu.VMEM((dim, cols), BF16),
            pltpu.VMEM((dim, cols), BF16),
            pltpu.VMEM((2, dim, width), BF16),
            pltpu.VMEM((rows, cols), F32),
            pltpu.VMEM((rows, dim), BF16),
            pltpu.VMEM((rows, dim), BF16),
            pltpu.VMEM((rows, 128), F32),
            pltpu.VMEM((8, cols), F32),
            pltpu.VMEM((rows, 128), F32),
            pltpu.VMEM((rows, 128), F32),
            pltpu.VMEM((2, rows, width), F32),
            pltpu.VMEM((ROUNDS, cols // 128, 128), F32),
            pltpu.VMEM((ROUNDS, 2, n_dp - 1, cols // 256, 128), F32),
            pltpu.VMEM((ROUNDS + 1, blocks, 128), F32),
            pltpu.VMEM((ROUNDS + 1, n_pr - 1, blocks, 128), F32),
            pltpu.VMEM((dim, rows), BF16),
            pltpu.VMEM((dim, cols), BF16),
            pltpu.VMEM((rows, 128), F32),
            pltpu.VMEM((rows, width), BF16),
            pltpu.VMEM((rows, dim), F32),
            pltpu.VMEM((n_dp, dim, width), F32),
            pltpu.VMEM((n_dp, quarter, width), F32),
            pltpu.VMEM((2, nz // 2, 2, 3, quarter, width), F32),
            pltpu.VMEM((2, 2, quarter, width), F32),
            pltpu.VMEM((nz, 2, dim, width), F32),
            pltpu.VMEM((rows // 2, dim), F32),
            pltpu.VMEM((nx - 1, rows // 2 // nx, dim), F32),
            pltpu.VMEM((2, rows // 2 // nx, dim), F32),
            dma((ROUNDS, 2)), dma((ROUNDS, 2)),
            dma((ROUNDS + 1,)), dma((ROUNDS + 1,)),
            dma, dma((n_dp,)), dma((2, 2)), dma((2, nz // 2, 2, 3)), dma, dma((2, 2)),
            dma((2, 2)), dma((nz, 2, 3)), dma, dma((nz, 2)), dma((5,)), dma((5,)), dma((4,)),
        ],
        compiler_params=pltpu.CompilerParams(
            collective_id=0, has_side_effects=True, vmem_limit_bytes=56 * 1024 * 1024
        ),
    )(sf, tf, sp, tp)


def solution(mesh):
    in_specs = (P("dp", None), P("dp", None), P(None, "proto"), P(None, "proto"))
    out_specs = (P(None, "proto"), P("dp", None))
    return jax.shard_map(
        functools.partial(fused, mesh.shape["dp"], mesh.shape["proto"]),
        mesh=mesh, in_specs=in_specs, out_specs=out_specs, check_vma=False,
    )
```

```python
import functools
import math

import jax
import jax.numpy as jnp
from jax import lax
from jax.experimental import pallas as pl
from jax.experimental.pallas import tpu as pltpu
from jax.sharding import PartitionSpec as P

PROTOS = 65536
ROUNDS = 3
EPS = 1e-06
TEACHER_TEMP = 0.07
STUDENT_TEMP = 0.1
LOG2E = 1.4426950408889634
MESH = pl.DeviceIdType.MESH
F32 = jnp.float32
BF16 = jnp.bfloat16


def unit_rows(values):
    wide = values.astype(F32)
    norms = jnp.sqrt(jnp.sum(wide * wide, axis=1, keepdims=True) + EPS)
    return (wide * (1.0 / norms), norms)


def unit_cols(values):
    wide = values.astype(F32)
    norms = jnp.sqrt(jnp.sum(wide * wide, axis=0, keepdims=True) + EPS)
    return (wide * (1.0 / norms), norms)


def wait_bytes(ref, sem):
    pltpu.make_async_copy(ref, ref, sem).wait()


def kernel(
    n_dp, n_pr,
    sf_in, tf_in, sp_in, tp_in,
    pg_ref, fg_ref,
    sf_ref, tf_ref, sp_ref, tp_ref, wts,
    expo, th, sh, part, vb, ub, racc, first,
    csend, crecv, rsend, rrecv,
    st, wsn, pb, gbuf, hat, ubuf, yrecv, zrecv, brecv, gat, h1, h2, h3,
    csend_sem, crecv_sem, rsend_sem, rrecv_sem,
    ysend_sem, yrecv_sem, zsend_sem, zrecv_sem, bsend_sem, brecv_sem,
    gzsend_sem, gzrecv_sem, gysend_sem, gyrecv_sem, hsend_sem, hrecv_sem, in_sem,
):
    rows, dim = sf_ref.shape
    cols = tp_ref.shape[1]
    me = lax.axis_index("dp")
    mp = lax.axis_index("proto")
    width = cols // n_dp
    blocks = rows // 128
    nz = n_dp // 2
    y, z = me // nz, lax.rem(me, nz)
    other = {"dp": (1 - y) * nz + z}
    sides = ({"dp": y * nz + lax.rem(z + 1, nz)}, {"dp": y * nz + lax.rem(z + nz - 1, nz)})
    part_rows = dim // 4
    core, h, x = lax.rem(mp, 2), lax.rem(mp // 2, 2), mp // 4
    nx = n_pr // 4
    factor = PROTOS / math.sqrt(rows * n_dp) / STUDENT_TEMP

    def peer(nx_, nh, ncore):
        return {"proto": (nx_ * 2 + nh) * 2 + ncore}

    loads = [
        pltpu.make_async_copy(src, dst, in_sem.at[k])
        for k, (src, dst) in enumerate((
            (tf_in, tf_ref),
            (tp_in.at[:, pl.ds(0, cols // 2)], tp_ref.at[:, pl.ds(0, cols // 2)]),
            (tp_in.at[:, pl.ds(cols // 2, cols // 2)], tp_ref.at[:, pl.ds(cols // 2, cols // 2)]),
            (sf_in, sf_ref),
            (sp_in, sp_ref),
        ))
    ]
    for load in loads[:3]:
        load.start()
    barrier = pltpu.get_barrier_semaphore()

    def greet_dp(j, _):
        pl.semaphore_signal(barrier, inc=1, device_id={"dp": lax.rem(me + j, n_dp)}, device_id_type=MESH)
        return 0

    def greet_pr(j, _):
        pl.semaphore_signal(barrier, inc=1, device_id={"proto": lax.rem(mp + j, n_pr)}, device_id_type=MESH)
        return 0

    lax.fori_loop(1, n_dp, greet_dp, 0)
    lax.fori_loop(1, n_pr, greet_pr, 0)

    def norm_rows(b, _):
        r = pl.ds(pl.multiple_of(b * 128, 128), 128)
        th[r, :] = unit_rows(tf_ref[r, :])[0].astype(BF16)
        return 0

    def norm_student(b, _):
        r = pl.ds(pl.multiple_of(b * 128, 128), 128)
        unit = unit_rows(sf_ref[r, :])[0]
        sh[r, :] = unit.astype(BF16)
        turned = unit.T.astype(BF16)
        st[pl.ds(pl.multiple_of((1 - y) * part_rows, part_rows), part_rows), r] = turned[:part_rows]
        st[pl.ds(pl.multiple_of(y * part_rows, part_rows), part_rows), r] = turned[part_rows:2 * part_rows]
        st[2 * part_rows:, r] = turned[2 * part_rows:]
        return 0

    loads[0].wait()
    lax.fori_loop(0, blocks, norm_rows, 0)
    loads[1].wait()
    loads[2].wait()
    for load in loads[3:]:
        load.start()
    tiles = width // 128
    half_tiles = n_dp * tiles // 2

    def hops(j, n):
        return min(j, n - j)

    dp_peers = sorted(
        [(a, j) for a in range(2) for j in range(nz) if a or j],
        key=lambda o: -(o[0] + hops(o[1], nz)))
    pr_peers = sorted(
        [(i, b, c) for i in range(nx) for b in range(2) for c in range(2) if i or b or c],
        key=lambda o: -(2 * hops(o[0], nx) + 4 * o[1] + o[2]))

    def send_cols(rnd, hf):
        r = pl.ds(hf * half_tiles, half_tiles)
        for slot, (a, j) in enumerate(dp_peers):
            pltpu.make_async_remote_copy(
                src_ref=csend.at[rnd, r], dst_ref=crecv.at[rnd, hf, slot],
                send_sem=csend_sem.at[rnd, hf], recv_sem=crecv_sem.at[rnd, hf],
                device_id={"dp": lax.rem(y + a, 2) * nz + lax.rem(z + j, nz)}, device_id_type=MESH,
            ).start()

    def put_cols(rnd, k, sums):
        for t in range(tiles):
            csend[rnd, pl.ds(k * tiles + t, 1), :] = sums[:, t * 128:(t + 1) * 128]

    def teacher_unit(k):
        c = pl.ds(pl.multiple_of(k * width, width), width)
        return unit_cols(tp_ref[:, c])[0].astype(BF16)

    def first_cols(k, _):
        c = pl.ds(pl.multiple_of(k * width, width), width)
        wt = wts[lax.rem(k, 2)]
        wts[lax.rem(k + 1, 2)] = teacher_unit(jnp.minimum(k + 1, n_dp - 1))
        acc = jnp.zeros((8, width), F32)
        for m in range(rows // 256):
            r = pl.ds(m * 256, 256)
            logits = jnp.dot(th[r, :], wt, preferred_element_type=F32)
            e = jnp.exp2(logits * (LOG2E / TEACHER_TEMP))
            expo[r, c] = e
            acc = acc + jnp.sum(e.reshape(32, 8, width), axis=0)
        put_cols(0, k, jnp.sum(acc, axis=0, keepdims=True))
        return 0

    wts[0] = teacher_unit(0)
    lax.fori_loop(0, n_dp // 2, first_cols, 0, unroll=8)
    pl.semaphore_wait(barrier, n_dp + n_pr - 2)
    send_cols(0, 0)
    lax.fori_loop(n_dp // 2, n_dp, first_cols, 0, unroll=8)
    send_cols(0, 1)
    loads[3].wait()
    lax.fori_loop(0, blocks, norm_student, 0)
    loads[4].wait()

    part[...] = jnp.zeros_like(part)

    def student(lo, hi):
        def body(k, _):
            c = pl.ds(pl.multiple_of(k * width, width), width)
            ws = unit_cols(sp_ref[:, c])[0].astype(BF16)
            wsn[:, c] = ws
            for m in range(rows // 256):
                r = pl.ds(m * 256, 256)
                logits = jnp.dot(sh[r, :], ws, preferred_element_type=F32)
                e = jnp.exp2(logits * (LOG2E / STUDENT_TEMP))
                s = e[:, 0:128]
                for t in range(1, width // 128):
                    s = s + e[:, t * 128:(t + 1) * 128]
                part[r, :] += s
            return 0

        lax.fori_loop(lo, hi, body, 0)

    def receive_v(rnd, hf):
        wait_bytes(crecv.at[rnd, hf], crecv_sem.at[rnd, hf])
        v = 1.0 / (csend[rnd, pl.ds(hf * half_tiles, half_tiles), :] + jnp.sum(crecv[rnd, hf], axis=0))
        for t in range(half_tiles):
            lanes = slice((hf * half_tiles + t) * 128, (hf * half_tiles + t + 1) * 128)
            vb[:, lanes] = jnp.broadcast_to(v[t:t + 1, :], (8, 128))

    def lane_sums(slot, acc):
        for k in range(blocks):
            turned = acc[k * 128:(k + 1) * 128, :].T
            rsend[slot, k:k + 1, :] = jnp.sum(turned, axis=0, keepdims=True)

    def send_rows(slot):
        for place, (i, b, c) in enumerate(pr_peers):
            pltpu.make_async_remote_copy(
                src_ref=rsend.at[slot], dst_ref=rrecv.at[slot, place],
                send_sem=rsend_sem.at[slot], recv_sem=rrecv_sem.at[slot],
                device_id=peer(lax.rem(x + i, nx), lax.rem(h + b, 2), lax.rem(core + c, 2)), device_id_type=MESH,
            ).start()

    def receive_rows(slot):
        wait_bytes(rrecv.at[slot], rrecv_sem.at[slot])
        return 1.0 / (rsend[slot] + jnp.sum(rrecv[slot], axis=0))

    def widen(u, out):
        for k in range(blocks):
            out[k * 128:(k + 1) * 128, :] = jnp.broadcast_to(u[k:k + 1, :], (128, 128)).T

    def row_pass(rnd, hf):
        def body(k, _):
            r = pl.ds(pl.multiple_of(k * 128, 128), 128)
            acc = racc[r, :].reshape(16, 8, 128) if hf else jnp.zeros((16, 8, 128), F32)
            for t in range(hf * half_tiles, (hf + 1) * half_tiles):
                e = expo[r, t * 128:(t + 1) * 128].reshape(16, 8, 128)
                acc = acc + e * vb[:, t * 128:(t + 1) * 128][None]
            racc[r, :] = acc.reshape(128, 128)
            return 0

        lax.fori_loop(0, blocks, body, 0)
        if hf:
            lane_sums(rnd, racc)

    def col_pass(rnd, hf):
        def body(i, _):
            k = hf * (n_dp // 2) + i
            c = pl.ds(pl.multiple_of(k * width, width), width)

            def inner(b, acc):
                r = pl.ds(pl.multiple_of(b * 128, 128), 128)
                u = ub[r, :].reshape(16, 8, 128)
                e = expo[r, c].reshape(16, 8, width)
                new = [e[:, :, t * 128:(t + 1) * 128] * u for t in range(tiles)]
                return tuple(a + jnp.sum(n, axis=0) for a, n in zip(acc, new))

            acc = lax.fori_loop(0, blocks, inner, (jnp.zeros((8, 128), F32),) * tiles)
            put_cols(rnd, k, jnp.sum(jnp.concatenate(acc, axis=1), axis=0, keepdims=True))
            return 0

        lax.fori_loop(0, n_dp // 2, body, 0)

    def span(rel, hc):
        chunk = lax.rem(z + rel, nz)
        return pl.ds(pl.multiple_of((chunk * 2 + hc) * width, width), width)

    def place(b):
        q = b // 2
        far = nz // 2 - (q + 1) // 2
        return span(jnp.where(lax.rem(q, 2) == 1, far, nz - far), lax.rem(b, 2))

    def ready(b, _):
        ws = wsn[:, place(b)]
        for m in range(rows // 256):
            r = pl.ds(m * 256, 256)
            logits = jnp.dot(sh[r, :], ws, preferred_element_type=F32)
            e = jnp.exp2(logits * (LOG2E / STUDENT_TEMP)).reshape(32, 8, width)
            ps = pb[r, :].reshape(32, 8, 128)
            first[b, r, :] = jnp.concatenate(
                [e[:, :, t * 128:(t + 1) * 128] * ps for t in range(tiles)], axis=2).reshape(256, width)
        return 0

    share = n_dp // 4
    student(0, share)
    for rnd in range(ROUNDS):
        if rnd == 1:
            student(2 * share, 3 * share)
        receive_v(rnd, 0)
        row_pass(rnd, 0)
        receive_v(rnd, 1)
        row_pass(rnd, 1)
        send_rows(rnd)
        if rnd == 0:
            student(share, 2 * share)
        if rnd == 1:
            student(3 * share, 4 * share)

            lane_sums(ROUNDS, part)
            send_rows(ROUNDS)
        if rnd == ROUNDS - 1:
            widen(receive_rows(ROUNDS) * factor, pb)
            hat[...] = jnp.zeros_like(hat)
            lax.fori_loop(0, 2, ready, 0)
        u = receive_rows(rnd)
        if rnd < ROUNDS - 1:
            widen(u, ub)
            col_pass(rnd + 1, 0)
            send_cols(rnd + 1, 0)
            col_pass(rnd + 1, 1)
            send_cols(rnd + 1, 1)
        else:
            widen(u * factor, ub)
    def copy(src, dst, send, recv, to):
        return pltpu.make_async_remote_copy(
            src_ref=src, dst_ref=dst, send_sem=send, recv_sem=recv, device_id=to, device_id_type=MESH)

    def grad_block(b, _, made=False):
        c = place(b)
        ws = wsn[:, c]
        v = vb[:, c]
        for m in range(rows // 256):
            r = pl.ds(m * 256, 256)
            if made:
                e = first[b, r, :].reshape(32, 8, width)
            else:
                logits = jnp.dot(sh[r, :], ws, preferred_element_type=F32)
                e = jnp.exp2(logits * (LOG2E / STUDENT_TEMP)).reshape(32, 8, width)
            q = expo[r, c].reshape(32, 8, width)
            us = ub[r, :].reshape(32, 8, 128)
            ps = pb[r, :].reshape(32, 8, 128)
            g = []
            for t in range(tiles):
                lanes = slice(t * 128, (t + 1) * 128)
                p = e[:, :, lanes] if made else e[:, :, lanes] * ps
                g.append(p - q[:, :, lanes] * us * v[None, :, lanes])
            g = jnp.concatenate(g, axis=2).reshape(256, width).astype(BF16)
            gbuf[r, :] = g
            hat[r, :] += lax.dot_general(g, ws, (((1,), (1,)), ((), ())), preferred_element_type=F32)
        ubuf[b] = jnp.dot(st[...], gbuf[...], preferred_element_type=F32)
        copy(ubuf.at[b, pl.ds(0, part_rows)], yrecv.at[b], ysend_sem, yrecv_sem.at[b], other).start()
        return 0

    half_rows = rows // 2
    x_rows = half_rows // nx

    mine = pl.multiple_of(core * half_rows, half_rows)
    theirs = pl.multiple_of((1 - core) * half_rows, half_rows)

    def x_start(xx):
        return pl.multiple_of(xx * x_rows, x_rows)

    def hat_1():
        copy(hat.at[pl.ds(theirs, half_rows)], h1, hsend_sem.at[0], hrecv_sem.at[0], peer(x, h, 1 - core)).start()

    def hat_2():
        wait_bytes(h1, hrecv_sem.at[0])
        hat[pl.ds(mine, half_rows), :] += h1[...]
        for j in range(1, nx):
            to = lax.rem(x + j, nx)
            copy(hat.at[pl.ds(mine + x_start(to), x_rows)], h2.at[j - 1], hsend_sem.at[1], hrecv_sem.at[1],
                 peer(to, h, core)).start()

    def hat_3():
        wait_bytes(h2, hrecv_sem.at[1])
        h3[0] = hat[pl.ds(mine + x_start(x), x_rows), :] + jnp.sum(h2[...], axis=0)
        copy(h3.at[0], h3.at[1], hsend_sem.at[2], hrecv_sem.at[2], peer(x, 1 - h, core)).start()

    def hat_4():
        wait_bytes(h3.at[1], hrecv_sem.at[2])
        r = pl.ds(mine + x_start(x), x_rows)
        grad = h3[0] + h3[1]
        unit, norm = unit_rows(sf_ref[r, :])
        fg_ref[r, :] = (grad - unit * jnp.sum(unit * grad, axis=1, keepdims=True)) / norm
        for j in range(1, nx):
            copy(fg_ref.at[r], fg_ref.at[r], hsend_sem.at[3], hrecv_sem.at[3], peer(lax.rem(x + j, nx), h, core)).start()

    def hat_5():
        wait_bytes(h2, hrecv_sem.at[3])
        r = pl.ds(mine, half_rows)
        copy(fg_ref.at[r], fg_ref.at[r], hsend_sem.at[4], hrecv_sem.at[4], peer(x, h, 1 - core)).start()

    def hat_6():
        wait_bytes(h1, hrecv_sem.at[4])

    def piece_rows(p):
        return pl.ds((p + 1) * part_rows, part_rows)

    top = nz // 2

    def arrive(q, hc, p):
        b = 2 * q + hc
        block = ubuf[b, piece_rows(p)]
        if p == 0:
            wait_bytes(yrecv.at[b], yrecv_sem.at[b])
            block = block + yrecv[b]
        return block

    def landed(turn, t, hc, p):
        wait_bytes(zrecv.at[turn, t, hc, p], zrecv_sem.at[turn, t, hc, p])
        return zrecv[turn, t, hc, p]

    def ring(t, pieces, same=(True, False)):
        for p in pieces:
            for hc in range(2):
                for turn in range(2):
                    if (hc == turn) not in same or (t == 0 and hc != turn):
                        continue
                    q = 2 * t - 1 + turn if t else 0
                    b = 2 * q + hc
                    block = arrive(q, hc, p)
                    if t > 1 or (t == 1 and hc == turn):
                        block = block + landed(turn, t - 1, hc, p)
                    ubuf[b, piece_rows(p)] = block
                    copy(ubuf.at[b, piece_rows(p)], zrecv.at[turn, t, hc, p],
                         zsend_sem.at[turn, min(t, 1)], zrecv_sem.at[turn, t, hc, p], sides[turn]).start()

    def pass_on(t, turn, hc, p):
        if t == top - 1 and hc != turn:
            return
        src = 2 * t - 1 + turn if t else 0
        dst = min(2 * t + 1 + turn, nz - 1)
        r = piece_rows(p)
        copy(gat.at[src, hc, r], gat.at[dst, hc, r], gzsend_sem.at[turn, min(top - 1 - t, 1)],
             gzrecv_sem.at[dst, hc, p], sides[turn]).start()

    def hand_over(slot, hc):
        copy(gat.at[slot, hc, piece_rows(0)], gat.at[slot, hc, pl.ds(0, part_rows)],
             gysend_sem, gyrecv_sem.at[slot, hc], other).start()

    lax.fori_loop(0, 2, functools.partial(grad_block, made=True), 0)
    ring(0, (1, 2))
    lax.fori_loop(2, 6, grad_block, 0)
    ring(0, (0,))
    ring(1, (1, 2), (False,))
    for t in range(1, top):
        if t == 1:
            ring(t, (1, 2), (True,))
            ring(t, (0,))
        else:
            ring(t, (1, 2, 0) if t < top - 1 else (1, 0, 2))
        if t < top - 1:
            lax.fori_loop(4 * t + 2, 4 * t + (6 if t < top - 2 else 8), grad_block, 0)
        if t == top - 2:
            hat_1()
    own = 2 * nz - 2

    def trade(p):
        for hc in range(2):
            block = arrive(nz - 1, hc, p)
            ubuf[own + hc, piece_rows(p)] = block + landed(0, top - 1, hc, p) + landed(1, top - 1, hc, p)
            copy(ubuf.at[own + hc, piece_rows(p)], brecv.at[hc, p - 1], bsend_sem, brecv_sem.at[hc, p - 1], other).start()

    def traded(p):
        for hc in range(2):
            wait_bytes(brecv.at[hc, p - 1], brecv_sem.at[hc, p - 1])
            gat[0, hc, piece_rows(p)] = ubuf[own + hc, piece_rows(p)] + brecv[hc, p - 1]
            for turn in range(2):
                pass_on(0, turn, hc, p)

    trade(1)
    for hc in range(2):
        gat[0, hc, piece_rows(0)] = arrive(nz - 1, hc, 0) + landed(0, top - 1, hc, 0) + landed(1, top - 1, hc, 0)
        for turn in range(2):
            pass_on(0, turn, hc, 0)
        hand_over(0, hc)
    traded(1)
    trade(2)
    hat_2()
    traded(2)

    wait_bytes(yrecv, ysend_sem)
    for turn in range(2):
        wait_bytes(zrecv.at[turn, 0, turn], zsend_sem.at[turn, 0])
        wait_bytes(zrecv.at[turn, pl.ds(1, top - 1)], zsend_sem.at[turn, 1])
    wait_bytes(brecv, bsend_sem)
    low = pl.ds(pl.multiple_of(y * part_rows, part_rows), part_rows)
    high = pl.ds(pl.multiple_of((1 - y) * part_rows, part_rows), part_rows)
    rest = pl.ds(2 * part_rows, 2 * part_rows)

    def finish(b, _):
        slot = b // 2
        hc = lax.rem(b, 2)
        far = (slot + 1) // 2
        c = span(jnp.where(lax.rem(slot, 2) == 1, nz - far, far), hc)
        wait_bytes(gat.at[slot, hc, pl.ds(0, part_rows)], gyrecv_sem.at[slot, hc])
        places = ((low, pl.ds(part_rows, part_rows)), (high, pl.ds(0, part_rows)), (rest, rest))
        wide = [sp_ref[here, c].astype(F32) for here, _ in places]
        square = sum(jnp.sum(w * w, axis=0, keepdims=True) for w in wide)
        inverse = 1.0 / jnp.sqrt(square + EPS)
        units = [w * inverse for w in wide]
        grads = [gat[slot, hc, there] for _, there in places]
        along = sum(jnp.sum(u * g, axis=0, keepdims=True) for u, g in zip(units, grads))
        for (here, _), u, g in zip(places, units, grads):
            pg_ref[here, c] = (g - u * along) * inverse
        return 0

    hat_3()
    later = {0: hat_4, 1: hat_5, 2: hat_6}
    for t in range(top):
        for p in range(3):
            for hc in range(2):
                for turn in range(2):
                    if t == top - 1 and hc != turn:
                        continue
                    slot = min(2 * t + 1 + turn, nz - 1)
                    wait_bytes(gat.at[slot, hc, piece_rows(p)], gzrecv_sem.at[slot, hc, p])
                    if t < top - 1:
                        pass_on(t + 1, turn, hc, p)
                    if p == 0:
                        hand_over(slot, hc)
        if t == 0:
            lax.fori_loop(0, 2, finish, 0)
        else:
            lax.fori_loop(4 * t - 2, 4 * t + 2, finish, 0)
        if t in later:
            later[t]()
    lax.fori_loop(2 * nz - 2, 2 * nz, finish, 0)

    for turn in range(2):
        wait_bytes(zrecv.at[turn, 0, turn], gzsend_sem.at[turn, 0])
        wait_bytes(zrecv.at[turn, pl.ds(1, top - 1)], gzsend_sem.at[turn, 1])
    wait_bytes(yrecv, gysend_sem)
    wait_bytes(h1, hsend_sem.at[0])
    wait_bytes(h2, hsend_sem.at[1])
    wait_bytes(h3.at[1], hsend_sem.at[2])
    wait_bytes(h2, hsend_sem.at[3])
    wait_bytes(h1, hsend_sem.at[4])
    for rnd in range(ROUNDS):
        for hf in range(2):
            wait_bytes(crecv.at[rnd, hf], csend_sem.at[rnd, hf])
    for slot in range(ROUNDS + 1):
        wait_bytes(rrecv.at[slot], rsend_sem.at[slot])


def fused(n_dp, n_pr, sf, tf, sp, tp):
    rows, dim = sf.shape
    cols = tp.shape[1]
    width = cols // n_dp
    blocks = rows // 128
    nz, nx = n_dp // 2, n_pr // 4
    quarter = dim // 4
    vmem = pl.BlockSpec(memory_space=pltpu.VMEM)
    anywhere = pl.BlockSpec(memory_space=pl.ANY)
    dma = pltpu.SemaphoreType.DMA
    return pl.pallas_call(
        functools.partial(kernel, n_dp, n_pr),
        out_shape=(
            pltpu.VMEM((dim, cols), F32),
            pltpu.VMEM((rows, dim), F32),
        ),
        in_specs=[anywhere] * 4,
        out_specs=[vmem] * 2,
        scratch_shapes=[
            pltpu.VMEM((rows, dim), BF16),
            pltpu.VMEM((rows, dim), BF16),
            pltpu.VMEM((dim, cols), BF16),
            pltpu.VMEM((dim, cols), BF16),
            pltpu.VMEM((2, dim, width), BF16),
            pltpu.VMEM((rows, cols), F32),
            pltpu.VMEM((rows, dim), BF16),
            pltpu.VMEM((rows, dim), BF16),
            pltpu.VMEM((rows, 128), F32),
            pltpu.VMEM((8, cols), F32),
            pltpu.VMEM((rows, 128), F32),
            pltpu.VMEM((rows, 128), F32),
            pltpu.VMEM((2, rows, width), F32),
            pltpu.VMEM((ROUNDS, cols // 128, 128), F32),
            pltpu.VMEM((ROUNDS, 2, n_dp - 1, cols // 256, 128), F32),
            pltpu.VMEM((ROUNDS + 1, blocks, 128), F32),
            pltpu.VMEM((ROUNDS + 1, n_pr - 1, blocks, 128), F32),
            pltpu.VMEM((dim, rows), BF16),
            pltpu.VMEM((dim, cols), BF16),
            pltpu.VMEM((rows, 128), F32),
            pltpu.VMEM((rows, width), BF16),
            pltpu.VMEM((rows, dim), F32),
            pltpu.VMEM((n_dp, dim, width), F32),
            pltpu.VMEM((n_dp, quarter, width), F32),
            pltpu.VMEM((2, nz // 2, 2, 3, quarter, width), F32),
            pltpu.VMEM((2, 2, quarter, width), F32),
            pltpu.VMEM((nz, 2, dim, width), F32),
            pltpu.VMEM((rows // 2, dim), F32),
            pltpu.VMEM((nx - 1, rows // 2 // nx, dim), F32),
            pltpu.VMEM((2, rows // 2 // nx, dim), F32),
            dma((ROUNDS, 2)), dma((ROUNDS, 2)),
            dma((ROUNDS + 1,)), dma((ROUNDS + 1,)),
            dma, dma((n_dp,)), dma((2, 2)), dma((2, nz // 2, 2, 3)), dma, dma((2, 2)),
            dma((2, 2)), dma((nz, 2, 3)), dma, dma((nz, 2)), dma((5,)), dma((5,)), dma((5,)),
        ],
        compiler_params=pltpu.CompilerParams(
            collective_id=0, has_side_effects=True, vmem_limit_bytes=56 * 1024 * 1024
        ),
    )(sf, tf, sp, tp)


def drain(parts, pg_ref, fg_ref, pg_out, fg_out, sem):
    copies = []
    for src, dst in ((pg_ref, pg_out), (fg_ref, fg_out)):
        step = src.shape[0] // parts
        for k in range(parts):
            r = pl.ds(k * step, step)
            copies.append(pltpu.make_async_copy(src.at[r], dst.at[r], sem.at[len(copies)]))
    for copy in copies:
        copy.start()
    for copy in copies:
        copy.wait()


def step(n_dp, n_pr, sf, tf, sp, tp):
    pg, fg = fused(n_dp, n_pr, sf, tf, sp, tp)
    parts = 4
    return pl.pallas_call(
        functools.partial(drain, parts),
        out_shape=(jax.ShapeDtypeStruct(pg.shape, F32), jax.ShapeDtypeStruct(fg.shape, F32)),
        in_specs=[pl.BlockSpec(memory_space=pltpu.VMEM)] * 2,
        out_specs=[pl.BlockSpec(memory_space=pl.ANY)] * 2,
        scratch_shapes=[pltpu.SemaphoreType.DMA((2 * parts,))],
        compiler_params=pltpu.CompilerParams(vmem_limit_bytes=16 * 1024 * 1024),
    )(pltpu.with_memory_space_constraint(pg, pltpu.VMEM), pltpu.with_memory_space_constraint(fg, pltpu.VMEM))


def solution(mesh):
    in_specs = (P("dp", None), P("dp", None), P(None, "proto"), P(None, "proto"))
    out_specs = (P(None, "proto"), P("dp", None))
    return jax.shard_map(
        functools.partial(step, mesh.shape["dp"], mesh.shape["proto"]),
        mesh=mesh, in_specs=in_specs, out_specs=out_specs, check_vma=False,
    )
```

```python
import functools
import math

import jax
import jax.numpy as jnp
from jax import lax
from jax.experimental import pallas as pl
from jax.experimental.pallas import tpu as pltpu
from jax.sharding import PartitionSpec as P

PROTOS = 65536
ROUNDS = 3
EPS = 1e-06
TEACHER_TEMP = 0.07
STUDENT_TEMP = 0.1
LOG2E = 1.4426950408889634
MESH = pl.DeviceIdType.MESH
F32 = jnp.float32
BF16 = jnp.bfloat16


def unit_rows(values):
    wide = values.astype(F32)
    norms = jnp.sqrt(jnp.sum(wide * wide, axis=1, keepdims=True) + EPS)
    return (wide * (1.0 / norms), norms)


def unit_cols(values):
    wide = values.astype(F32)
    norms = jnp.sqrt(jnp.sum(wide * wide, axis=0, keepdims=True) + EPS)
    return (wide * (1.0 / norms), norms)


def wait_bytes(ref, sem):
    pltpu.make_async_copy(ref, ref, sem).wait()


def kernel(
    n_dp, n_pr,
    sf_in, tf_in, sp_in, tp_in,
    pg_ref, fg_ref,
    sf_ref, tf_ref, sp_ref, tp_ref, wts,
    expo, th, sh, part, vb, ub, racc, first,
    csend, crecv, rsend, rrecv,
    st, wsn, pb, gbuf, hat, ubuf, yrecv, zrecv, brecv, gat, h1, h2, h3,
    csend_sem, crecv_sem, rsend_sem, rrecv_sem,
    ysend_sem, yrecv_sem, zsend_sem, zrecv_sem, bsend_sem, brecv_sem,
    gzsend_sem, gzrecv_sem, gysend_sem, gyrecv_sem, hsend_sem, hrecv_sem, in_sem,
):
    rows, dim = sf_ref.shape
    cols = tp_ref.shape[1]
    me = lax.axis_index("dp")
    mp = lax.axis_index("proto")
    width = cols // n_dp
    blocks = rows // 128
    nz = n_dp // 2
    y, z = me // nz, lax.rem(me, nz)
    other = {"dp": (1 - y) * nz + z}
    sides = ({"dp": y * nz + lax.rem(z + 1, nz)}, {"dp": y * nz + lax.rem(z + nz - 1, nz)})
    part_rows = dim // 4
    core, h, x = lax.rem(mp, 2), lax.rem(mp // 2, 2), mp // 4
    nx = n_pr // 4
    factor = PROTOS / math.sqrt(rows * n_dp) / STUDENT_TEMP

    def peer(nx_, nh, ncore):
        return {"proto": (nx_ * 2 + nh) * 2 + ncore}

    loads = [
        pltpu.make_async_copy(src, dst, in_sem.at[k])
        for k, (src, dst) in enumerate((
            (tf_in, tf_ref),
            (tp_in.at[:, pl.ds(0, cols // 2)], tp_ref.at[:, pl.ds(0, cols // 2)]),
            (tp_in.at[:, pl.ds(cols // 2, cols // 2)], tp_ref.at[:, pl.ds(cols // 2, cols // 2)]),
            (sf_in, sf_ref),
            (sp_in, sp_ref),
        ))
    ]
    for load in loads[:3]:
        load.start()
    barrier = pltpu.get_barrier_semaphore()

    def greet_dp(j, _):
        pl.semaphore_signal(barrier, inc=1, device_id={"dp": lax.rem(me + j, n_dp)}, device_id_type=MESH)
        return 0

    def greet_pr(j, _):
        pl.semaphore_signal(barrier, inc=1, device_id={"proto": lax.rem(mp + j, n_pr)}, device_id_type=MESH)
        return 0

    lax.fori_loop(1, n_dp, greet_dp, 0)
    lax.fori_loop(1, n_pr, greet_pr, 0)

    def norm_rows(b, _):
        r = pl.ds(pl.multiple_of(b * 128, 128), 128)
        th[r, :] = unit_rows(tf_ref[r, :])[0].astype(BF16)
        return 0

    def norm_student(b, _):
        r = pl.ds(pl.multiple_of(b * 128, 128), 128)
        unit = unit_rows(sf_ref[r, :])[0]
        sh[r, :] = unit.astype(BF16)
        turned = unit.T.astype(BF16)
        st[pl.ds(pl.multiple_of((1 - y) * part_rows, part_rows), part_rows), r] = turned[:part_rows]
        st[pl.ds(pl.multiple_of(y * part_rows, part_rows), part_rows), r] = turned[part_rows:2 * part_rows]
        st[2 * part_rows:, r] = turned[2 * part_rows:]
        return 0

    loads[0].wait()
    lax.fori_loop(0, blocks, norm_rows, 0)
    loads[1].wait()
    loads[2].wait()
    for load in loads[3:]:
        load.start()
    tiles = width // 128
    cuts = (0, n_dp // 4, 3 * n_dp // 4, n_dp)

    def hops(j, n):
        return min(j, n - j)

    dp_peers = sorted(
        [(a, j) for a in range(2) for j in range(nz) if a or j],
        key=lambda o: -(o[0] + hops(o[1], nz)))
    pr_peers = sorted(
        [(i, b, c) for i in range(nx) for b in range(2) for c in range(2) if i or b or c],
        key=lambda o: -(2 * hops(o[0], nx) + 4 * o[1] + o[2]))

    def send_cols(rnd, hf):
        r = pl.ds(cuts[hf] * tiles, (cuts[hf + 1] - cuts[hf]) * tiles)
        for slot, (a, j) in enumerate(dp_peers):
            pltpu.make_async_remote_copy(
                src_ref=csend.at[rnd, r], dst_ref=crecv[hf].at[rnd, slot],
                send_sem=csend_sem.at[rnd, hf], recv_sem=crecv_sem.at[rnd, hf],
                device_id={"dp": lax.rem(y + a, 2) * nz + lax.rem(z + j, nz)}, device_id_type=MESH,
            ).start()

    def put_cols(rnd, k, sums):
        for t in range(tiles):
            csend[rnd, pl.ds(k * tiles + t, 1), :] = sums[:, t * 128:(t + 1) * 128]

    def teacher_unit(k):
        c = pl.ds(pl.multiple_of(k * width, width), width)
        return unit_cols(tp_ref[:, c])[0].astype(BF16)

    def first_cols(k, _):
        c = pl.ds(pl.multiple_of(k * width, width), width)
        wt = wts[lax.rem(k, 2)]
        wts[lax.rem(k + 1, 2)] = teacher_unit(jnp.minimum(k + 1, n_dp - 1))
        acc = jnp.zeros((8, width), F32)
        for m in range(rows // 256):
            r = pl.ds(m * 256, 256)
            logits = jnp.dot(th[r, :], wt, preferred_element_type=F32)
            e = jnp.exp2(logits * (LOG2E / TEACHER_TEMP))
            expo[r, c] = e
            acc = acc + jnp.sum(e.reshape(32, 8, width), axis=0)
        put_cols(0, k, jnp.sum(acc, axis=0, keepdims=True))
        return 0

    wts[0] = teacher_unit(0)
    lax.fori_loop(0, cuts[1], first_cols, 0, unroll=4)
    pl.semaphore_wait(barrier, n_dp + n_pr - 2)
    send_cols(0, 0)
    for hf in range(1, 3):
        lax.fori_loop(cuts[hf], cuts[hf + 1], first_cols, 0, unroll=4)
        send_cols(0, hf)
    loads[3].wait()
    lax.fori_loop(0, blocks, norm_student, 0)
    loads[4].wait()

    part[...] = jnp.zeros_like(part)

    def student(lo, hi):
        def body(k, _):
            c = pl.ds(pl.multiple_of(k * width, width), width)
            ws = unit_cols(sp_ref[:, c])[0].astype(BF16)
            wsn[:, c] = ws
            for m in range(rows // 256):
                r = pl.ds(m * 256, 256)
                logits = jnp.dot(sh[r, :], ws, preferred_element_type=F32)
                e = jnp.exp2(logits * (LOG2E / STUDENT_TEMP))
                s = e[:, 0:128]
                for t in range(1, width // 128):
                    s = s + e[:, t * 128:(t + 1) * 128]
                part[r, :] += s
            return 0

        lax.fori_loop(lo, hi, body, 0)

    def receive_v(rnd, hf):
        wait_bytes(crecv[hf].at[rnd], crecv_sem.at[rnd, hf])
        count = (cuts[hf + 1] - cuts[hf]) * tiles
        base = cuts[hf] * tiles
        v = 1.0 / (csend[rnd, pl.ds(base, count), :] + jnp.sum(crecv[hf][rnd], axis=0))
        for t in range(count):
            lanes = slice((base + t) * 128, (base + t + 1) * 128)
            vb[:, lanes] = jnp.broadcast_to(v[t:t + 1, :], (8, 128))

    def lane_sums(slot, acc):
        for k in range(blocks):
            turned = acc[k * 128:(k + 1) * 128, :].T
            rsend[slot, k:k + 1, :] = jnp.sum(turned, axis=0, keepdims=True)

    def send_rows(slot):
        for place, (i, b, c) in enumerate(pr_peers):
            pltpu.make_async_remote_copy(
                src_ref=rsend.at[slot], dst_ref=rrecv.at[slot, place],
                send_sem=rsend_sem.at[slot], recv_sem=rrecv_sem.at[slot],
                device_id=peer(lax.rem(x + i, nx), lax.rem(h + b, 2), lax.rem(core + c, 2)), device_id_type=MESH,
            ).start()

    def receive_rows(slot):
        wait_bytes(rrecv.at[slot], rrecv_sem.at[slot])
        return 1.0 / (rsend[slot] + jnp.sum(rrecv[slot], axis=0))

    def widen(u, out):
        for k in range(blocks):
            out[k * 128:(k + 1) * 128, :] = jnp.broadcast_to(u[k:k + 1, :], (128, 128)).T

    def row_pass(rnd, hf):
        def body(k, _):
            r = pl.ds(pl.multiple_of(k * 128, 128), 128)
            acc = racc[r, :].reshape(16, 8, 128) if hf else jnp.zeros((16, 8, 128), F32)
            for t in range(cuts[hf] * tiles, cuts[hf + 1] * tiles):
                e = expo[r, t * 128:(t + 1) * 128].reshape(16, 8, 128)
                acc = acc + e * vb[:, t * 128:(t + 1) * 128][None]
            racc[r, :] = acc.reshape(128, 128)
            return 0

        lax.fori_loop(0, blocks, body, 0)
        if hf == len(cuts) - 2:
            lane_sums(rnd, racc)

    def col_pass(rnd, hf):
        def body(i, _):
            k = cuts[hf] + i
            c = pl.ds(pl.multiple_of(k * width, width), width)

            def inner(b, acc):
                r = pl.ds(pl.multiple_of(b * 128, 128), 128)
                u = ub[r, :].reshape(16, 8, 128)
                e = expo[r, c].reshape(16, 8, width)
                new = [e[:, :, t * 128:(t + 1) * 128] * u for t in range(tiles)]
                return tuple(a + jnp.sum(n, axis=0) for a, n in zip(acc, new))

            acc = lax.fori_loop(0, blocks, inner, (jnp.zeros((8, 128), F32),) * tiles)
            put_cols(rnd, k, jnp.sum(jnp.concatenate(acc, axis=1), axis=0, keepdims=True))
            return 0

        lax.fori_loop(0, cuts[hf + 1] - cuts[hf], body, 0)

    def span(rel, hc):
        chunk = lax.rem(z + rel, nz)
        return pl.ds(pl.multiple_of((chunk * 2 + hc) * width, width), width)

    def place(b):
        q = b // 2
        far = nz // 2 - (q + 1) // 2
        return span(jnp.where(lax.rem(q, 2) == 1, far, nz - far), lax.rem(b, 2))

    def ready(b, _):
        ws = wsn[:, place(b)]
        for m in range(rows // 256):
            r = pl.ds(m * 256, 256)
            logits = jnp.dot(sh[r, :], ws, preferred_element_type=F32)
            e = jnp.exp2(logits * (LOG2E / STUDENT_TEMP)).reshape(32, 8, width)
            ps = pb[r, :].reshape(32, 8, 128)
            first[b, r, :] = jnp.concatenate(
                [e[:, :, t * 128:(t + 1) * 128] * ps for t in range(tiles)], axis=2).reshape(256, width)
        return 0

    share = n_dp // 4
    student(0, share)
    for rnd in range(ROUNDS):
        if rnd == 1:
            student(2 * share, 3 * share)
        receive_v(rnd, 0)
        row_pass(rnd, 0)
        for hf in range(1, 3):
            receive_v(rnd, hf)
            row_pass(rnd, hf)
        send_rows(rnd)
        if rnd == 0:
            student(share, 2 * share)
        if rnd == 1:
            student(3 * share, 4 * share)

            lane_sums(ROUNDS, part)
            send_rows(ROUNDS)
        if rnd == ROUNDS - 1:
            widen(receive_rows(ROUNDS) * factor, pb)
            hat[...] = jnp.zeros_like(hat)
            lax.fori_loop(0, 2, ready, 0)
        u = receive_rows(rnd)
        if rnd < ROUNDS - 1:
            widen(u, ub)
            col_pass(rnd + 1, 0)
            send_cols(rnd + 1, 0)
            for hf in range(1, 3):
                col_pass(rnd + 1, hf)
                send_cols(rnd + 1, hf)
        else:
            widen(u * factor, ub)
    def copy(src, dst, send, recv, to):
        return pltpu.make_async_remote_copy(
            src_ref=src, dst_ref=dst, send_sem=send, recv_sem=recv, device_id=to, device_id_type=MESH)

    def grad_block(b, _, made=False):
        c = place(b)
        ws = wsn[:, c]
        v = vb[:, c]
        for m in range(rows // 256):
            r = pl.ds(m * 256, 256)
            if made:
                e = first[b, r, :].reshape(32, 8, width)
            else:
                logits = jnp.dot(sh[r, :], ws, preferred_element_type=F32)
                e = jnp.exp2(logits * (LOG2E / STUDENT_TEMP)).reshape(32, 8, width)
            q = expo[r, c].reshape(32, 8, width)
            us = ub[r, :].reshape(32, 8, 128)
            ps = pb[r, :].reshape(32, 8, 128)
            g = []
            for t in range(tiles):
                lanes = slice(t * 128, (t + 1) * 128)
                p = e[:, :, lanes] if made else e[:, :, lanes] * ps
                g.append(p - q[:, :, lanes] * us * v[None, :, lanes])
            g = jnp.concatenate(g, axis=2).reshape(256, width).astype(BF16)
            gbuf[r, :] = g
            hat[r, :] += lax.dot_general(g, ws, (((1,), (1,)), ((), ())), preferred_element_type=F32)
        ubuf[b] = jnp.dot(st[...], gbuf[...], preferred_element_type=F32)
        copy(ubuf.at[b, pl.ds(0, part_rows)], yrecv.at[b], ysend_sem, yrecv_sem.at[b], other).start()
        return 0

    half_rows = rows // 2
    x_rows = half_rows // nx

    mine = pl.multiple_of(core * half_rows, half_rows)
    theirs = pl.multiple_of((1 - core) * half_rows, half_rows)

    def x_start(xx):
        return pl.multiple_of(xx * x_rows, x_rows)

    def hat_1():
        copy(hat.at[pl.ds(theirs, half_rows)], h1, hsend_sem.at[0], hrecv_sem.at[0], peer(x, h, 1 - core)).start()

    def hat_2():
        wait_bytes(h1, hrecv_sem.at[0])
        hat[pl.ds(mine, half_rows), :] += h1[...]
        for j in range(1, nx):
            to = lax.rem(x + j, nx)
            copy(hat.at[pl.ds(mine + x_start(to), x_rows)], h2.at[j - 1], hsend_sem.at[1], hrecv_sem.at[1],
                 peer(to, h, core)).start()

    def hat_3():
        wait_bytes(h2, hrecv_sem.at[1])
        h3[0] = hat[pl.ds(mine + x_start(x), x_rows), :] + jnp.sum(h2[...], axis=0)
        copy(h3.at[0], h3.at[1], hsend_sem.at[2], hrecv_sem.at[2], peer(x, 1 - h, core)).start()

    def hat_4():
        wait_bytes(h3.at[1], hrecv_sem.at[2])
        r = pl.ds(mine + x_start(x), x_rows)
        grad = h3[0] + h3[1]
        unit, norm = unit_rows(sf_ref[r, :])
        fg_ref[r, :] = (grad - unit * jnp.sum(unit * grad, axis=1, keepdims=True)) / norm
        for j in range(1, nx):
            copy(fg_ref.at[r], fg_ref.at[r], hsend_sem.at[3], hrecv_sem.at[3], peer(lax.rem(x + j, nx), h, core)).start()

    def hat_5():
        wait_bytes(h2, hrecv_sem.at[3])
        r = pl.ds(mine, half_rows)
        copy(fg_ref.at[r], fg_ref.at[r], hsend_sem.at[4], hrecv_sem.at[4], peer(x, h, 1 - core)).start()

    def hat_6():
        wait_bytes(h1, hrecv_sem.at[4])

    def piece_rows(p):
        return pl.ds((p + 1) * part_rows, part_rows)

    top = nz // 2

    def arrive(q, hc, p):
        b = 2 * q + hc
        block = ubuf[b, piece_rows(p)]
        if p == 0:
            wait_bytes(yrecv.at[b], yrecv_sem.at[b])
            block = block + yrecv[b]
        return block

    def landed(turn, t, hc, p):
        wait_bytes(zrecv.at[turn, t, hc, p], zrecv_sem.at[turn, t, hc, p])
        return zrecv[turn, t, hc, p]

    def ring(t, pieces, same=(True, False)):
        for p in pieces:
            for hc in range(2):
                for turn in range(2):
                    if (hc == turn) not in same or (t == 0 and hc != turn):
                        continue
                    q = 2 * t - 1 + turn if t else 0
                    b = 2 * q + hc
                    block = arrive(q, hc, p)
                    if t > 1 or (t == 1 and hc == turn):
                        block = block + landed(turn, t - 1, hc, p)
                    ubuf[b, piece_rows(p)] = block
                    copy(ubuf.at[b, piece_rows(p)], zrecv.at[turn, t, hc, p],
                         zsend_sem.at[turn, min(t, 1)], zrecv_sem.at[turn, t, hc, p], sides[turn]).start()

    def pass_on(t, turn, hc, p):
        if t == top - 1 and hc != turn:
            return
        src = 2 * t - 1 + turn if t else 0
        dst = min(2 * t + 1 + turn, nz - 1)
        r = piece_rows(p)
        copy(gat.at[src, hc, r], gat.at[dst, hc, r], gzsend_sem.at[turn, min(top - 1 - t, 1)],
             gzrecv_sem.at[dst, hc, p], sides[turn]).start()

    def hand_over(slot, hc):
        copy(gat.at[slot, hc, piece_rows(0)], gat.at[slot, hc, pl.ds(0, part_rows)],
             gysend_sem, gyrecv_sem.at[slot, hc], other).start()

    lax.fori_loop(0, 2, functools.partial(grad_block, made=True), 0)
    ring(0, (1, 2))
    lax.fori_loop(2, 6, grad_block, 0)
    ring(0, (0,))
    ring(1, (1, 2), (False,))
    for t in range(1, top):
        if t == 1:
            ring(t, (1, 2), (True,))
            ring(t, (0,))
        else:
            ring(t, (1, 2, 0) if t < top - 1 else (1, 0, 2))
        if t < top - 1:
            lax.fori_loop(4 * t + 2, 4 * t + (6 if t < top - 2 else 8), grad_block, 0)
        if t == top - 2:
            hat_1()
    own = 2 * nz - 2

    def trade(p):
        for hc in range(2):
            block = arrive(nz - 1, hc, p)
            ubuf[own + hc, piece_rows(p)] = block + landed(0, top - 1, hc, p) + landed(1, top - 1, hc, p)
            copy(ubuf.at[own + hc, piece_rows(p)], brecv.at[hc, p - 1], bsend_sem, brecv_sem.at[hc, p - 1], other).start()

    def traded(p):
        for hc in range(2):
            wait_bytes(brecv.at[hc, p - 1], brecv_sem.at[hc, p - 1])
            gat[0, hc, piece_rows(p)] = ubuf[own + hc, piece_rows(p)] + brecv[hc, p - 1]
            for turn in range(2):
                pass_on(0, turn, hc, p)

    trade(1)
    for hc in range(2):
        gat[0, hc, piece_rows(0)] = arrive(nz - 1, hc, 0) + landed(0, top - 1, hc, 0) + landed(1, top - 1, hc, 0)
        for turn in range(2):
            pass_on(0, turn, hc, 0)
        hand_over(0, hc)
    traded(1)
    trade(2)
    hat_2()
    traded(2)

    wait_bytes(yrecv, ysend_sem)
    for turn in range(2):
        wait_bytes(zrecv.at[turn, 0, turn], zsend_sem.at[turn, 0])
        wait_bytes(zrecv.at[turn, pl.ds(1, top - 1)], zsend_sem.at[turn, 1])
    wait_bytes(brecv, bsend_sem)
    low = pl.ds(pl.multiple_of(y * part_rows, part_rows), part_rows)
    high = pl.ds(pl.multiple_of((1 - y) * part_rows, part_rows), part_rows)
    rest = pl.ds(2 * part_rows, 2 * part_rows)

    def finish(b, _):
        slot = b // 2
        hc = lax.rem(b, 2)
        far = (slot + 1) // 2
        c = span(jnp.where(lax.rem(slot, 2) == 1, nz - far, far), hc)
        wait_bytes(gat.at[slot, hc, pl.ds(0, part_rows)], gyrecv_sem.at[slot, hc])
        places = ((low, pl.ds(part_rows, part_rows)), (high, pl.ds(0, part_rows)), (rest, rest))
        wide = [sp_ref[here, c].astype(F32) for here, _ in places]
        square = sum(jnp.sum(w * w, axis=0, keepdims=True) for w in wide)
        inverse = 1.0 / jnp.sqrt(square + EPS)
        units = [w * inverse for w in wide]
        grads = [gat[slot, hc, there] for _, there in places]
        along = sum(jnp.sum(u * g, axis=0, keepdims=True) for u, g in zip(units, grads))
        for (here, _), u, g in zip(places, units, grads):
            pg_ref[here, c] = (g - u * along) * inverse
        return 0

    hat_3()
    later = {0: hat_4, 1: hat_5, 2: hat_6}
    for t in range(top):
        for p in range(3):
            for hc in range(2):
                for turn in range(2):
                    if t == top - 1 and hc != turn:
                        continue
                    slot = min(2 * t + 1 + turn, nz - 1)
                    wait_bytes(gat.at[slot, hc, piece_rows(p)], gzrecv_sem.at[slot, hc, p])
                    if t < top - 1:
                        pass_on(t + 1, turn, hc, p)
                    if p == 0:
                        hand_over(slot, hc)
        if t == 0:
            lax.fori_loop(0, 2, finish, 0)
        else:
            lax.fori_loop(4 * t - 2, 4 * t + 2, finish, 0)
        if t in later:
            later[t]()
    lax.fori_loop(2 * nz - 2, 2 * nz, finish, 0)

    for turn in range(2):
        wait_bytes(zrecv.at[turn, 0, turn], gzsend_sem.at[turn, 0])
        wait_bytes(zrecv.at[turn, pl.ds(1, top - 1)], gzsend_sem.at[turn, 1])
    wait_bytes(yrecv, gysend_sem)
    wait_bytes(h1, hsend_sem.at[0])
    wait_bytes(h2, hsend_sem.at[1])
    wait_bytes(h3.at[1], hsend_sem.at[2])
    wait_bytes(h2, hsend_sem.at[3])
    wait_bytes(h1, hsend_sem.at[4])
    for rnd in range(ROUNDS):
        for hf in range(len(cuts) - 1):
            wait_bytes(crecv[hf].at[rnd], csend_sem.at[rnd, hf])
    for slot in range(ROUNDS + 1):
        wait_bytes(rrecv.at[slot], rsend_sem.at[slot])


def fused(n_dp, n_pr, sf, tf, sp, tp):
    rows, dim = sf.shape
    cols = tp.shape[1]
    width = cols // n_dp
    blocks = rows // 128
    nz, nx = n_dp // 2, n_pr // 4
    quarter = dim // 4
    vmem = pl.BlockSpec(memory_space=pltpu.VMEM)
    anywhere = pl.BlockSpec(memory_space=pl.ANY)
    dma = pltpu.SemaphoreType.DMA
    return pl.pallas_call(
        functools.partial(kernel, n_dp, n_pr),
        out_shape=(
            pltpu.VMEM((dim, cols), F32),
            pltpu.VMEM((rows, dim), F32),
        ),
        in_specs=[anywhere] * 4,
        out_specs=[vmem] * 2,
        scratch_shapes=[
            pltpu.VMEM((rows, dim), BF16),
            pltpu.VMEM((rows, dim), BF16),
            pltpu.VMEM((dim, cols), BF16),
            pltpu.VMEM((dim, cols), BF16),
            pltpu.VMEM((2, dim, width), BF16),
            pltpu.VMEM((rows, cols), F32),
            pltpu.VMEM((rows, dim), BF16),
            pltpu.VMEM((rows, dim), BF16),
            pltpu.VMEM((rows, 128), F32),
            pltpu.VMEM((8, cols), F32),
            pltpu.VMEM((rows, 128), F32),
            pltpu.VMEM((rows, 128), F32),
            pltpu.VMEM((2, rows, width), F32),
            pltpu.VMEM((ROUNDS, cols // 128, 128), F32),
            [
                pltpu.VMEM((ROUNDS, n_dp - 1, cols // 512, 128), F32),
                pltpu.VMEM((ROUNDS, n_dp - 1, cols // 256, 128), F32),
                pltpu.VMEM((ROUNDS, n_dp - 1, cols // 512, 128), F32),
            ],
            pltpu.VMEM((ROUNDS + 1, blocks, 128), F32),
            pltpu.VMEM((ROUNDS + 1, n_pr - 1, blocks, 128), F32),
            pltpu.VMEM((dim, rows), BF16),
            pltpu.VMEM((dim, cols), BF16),
            pltpu.VMEM((rows, 128), F32),
            pltpu.VMEM((rows, width), BF16),
            pltpu.VMEM((rows, dim), F32),
            pltpu.VMEM((n_dp, dim, width), F32),
            pltpu.VMEM((n_dp, quarter, width), F32),
            pltpu.VMEM((2, nz // 2, 2, 3, quarter, width), F32),
            pltpu.VMEM((2, 2, quarter, width), F32),
            pltpu.VMEM((nz, 2, dim, width), F32),
            pltpu.VMEM((rows // 2, dim), F32),
            pltpu.VMEM((nx - 1, rows // 2 // nx, dim), F32),
            pltpu.VMEM((2, rows // 2 // nx, dim), F32),
            dma((ROUNDS, 3)), dma((ROUNDS, 3)),
            dma((ROUNDS + 1,)), dma((ROUNDS + 1,)),
            dma, dma((n_dp,)), dma((2, 2)), dma((2, nz // 2, 2, 3)), dma, dma((2, 2)),
            dma((2, 2)), dma((nz, 2, 3)), dma, dma((nz, 2)), dma((5,)), dma((5,)), dma((5,)),
        ],
        compiler_params=pltpu.CompilerParams(
            collective_id=0, has_side_effects=True, vmem_limit_bytes=56 * 1024 * 1024
        ),
    )(sf, tf, sp, tp)


def drain(parts, pg_ref, fg_ref, pg_out, fg_out, sem):
    copies = []
    for src, dst in ((pg_ref, pg_out), (fg_ref, fg_out)):
        step = src.shape[0] // parts
        for k in range(parts):
            r = pl.ds(k * step, step)
            copies.append(pltpu.make_async_copy(src.at[r], dst.at[r], sem.at[len(copies)]))
    for copy in copies:
        copy.start()
    for copy in copies:
        copy.wait()


def step(n_dp, n_pr, sf, tf, sp, tp):
    pg, fg = fused(n_dp, n_pr, sf, tf, sp, tp)
    parts = 4
    return pl.pallas_call(
        functools.partial(drain, parts),
        out_shape=(jax.ShapeDtypeStruct(pg.shape, F32), jax.ShapeDtypeStruct(fg.shape, F32)),
        in_specs=[pl.BlockSpec(memory_space=pltpu.VMEM)] * 2,
        out_specs=[pl.BlockSpec(memory_space=pl.ANY)] * 2,
        scratch_shapes=[pltpu.SemaphoreType.DMA((2 * parts,))],
        compiler_params=pltpu.CompilerParams(vmem_limit_bytes=16 * 1024 * 1024),
    )(pltpu.with_memory_space_constraint(pg, pltpu.VMEM), pltpu.with_memory_space_constraint(fg, pltpu.VMEM))


def solution(mesh):
    in_specs = (P("dp", None), P("dp", None), P(None, "proto"), P(None, "proto"))
    out_specs = (P(None, "proto"), P("dp", None))
    return jax.shard_map(
        functools.partial(step, mesh.shape["dp"], mesh.shape["proto"]),
        mesh=mesh, in_specs=in_specs, out_specs=out_specs, check_vma=False,
    )
```
